256 devices in a mesh: replica: 8 (over z_lo, y), node: 32 (over x, z_hi, core).
Axes of the slice: x: 4, y: 4, z: 8 (z_hi: 4, z_lo: 2; z = z_hi * 2 + z_lo), core: 2. Of those that a mesh axis runs over, the one named last changes fastest.
Arguments:
- tokens: bfloat16 [65536, 6144], P(('replica', 'node')), may hold values from -6 to 6
- gain: float32 [6144], replicated, may hold values from 0.1 to 1.9
- w_up: bfloat16 [6144, 12288], P('replica', 'node'), may hold values from -0.078125 to 0.078125
- w_down: bfloat16 [12288, 6144], P('node', 'replica'), may hold values from -0.0546875 to 0.0546875
- cotangent: bfloat16 [65536, 6144], P(('replica', 'node')), may hold values from -2 to 2
- keep_index: int32 [32, 72], P('replica'), may hold values from 0 to 2047, as said below
Outputs:
- input_grad: bfloat16 [65536, 6144], P(('replica', 'node'))
- gain_grad: float32 [6144], replicated
- up_grad: bfloat16 [6144, 12288], P('replica', 'node')
- down_grad: bfloat16 [12288, 6144], P('node', 'replica')
The draws below stay inside these ranges and needn't reach their ends.
Inputs may be any that keep to these rules, and one draw needn't show every extreme that they name: `keep_index`: in each sequence the kept positions are distinct and ascending. Each device's block of 256 tokens within a sequence holds at most 12 kept tokens, and exactly 12 on one of the 8 devices of every sequence.
All inputs are finite; a program needn't handle non-finite values.
Results may differ from the reference program's by a relative error of at most 0.024.
Values may be sent and summed in bfloat16 or wider, within the bound.
A program may use at most 128 MiB of HBM per device.

```python
import jax
import jax.numpy as jnp
from jax import lax

D = 6144
FF = 12288
TOK_DEV = 256
CAP = 12
SEQ = 2048
KEEP = 72
SEQS = 32
TOKENS = 65536
N_REPLICA = 8
N_NODE = 32


def one_sequence(key_seq):
    seq_span = SEQ // TOK_DEV
    key_heavy, key_slots, key_rank = jax.random.split(key_seq, 3)
    heavy = jax.random.randint(key_heavy, (), 0, seq_span)
    slot_perm = jax.random.permutation(key_slots, (seq_span - 1) * CAP)
    marked = (slot_perm < KEEP - CAP).astype(jnp.int32)
    others = jnp.sum(marked.reshape(seq_span - 1, CAP), axis=1)
    device_ids = jnp.arange(seq_span, dtype=jnp.int32)
    shifted = jnp.clip(device_ids - (device_ids > heavy).astype(jnp.int32), 0, seq_span - 2)
    counts = jnp.where(device_ids == heavy, CAP, others[shifted])
    rank_keys = jax.random.split(key_rank, seq_span)
    rank_table = jax.vmap(lambda inner_key: jax.random.permutation(inner_key, TOK_DEV))(rank_keys)
    kept_flag = (rank_table < counts[:, None]).astype(jnp.int32).reshape(-1)
    ordering = jnp.argsort(1 - kept_flag, stable=True)
    return ordering[:KEEP].astype(jnp.int32)


def draw_keep_index(key, part):
    key = jax.random.fold_in(key, 7)
    seq_keys = jax.random.split(key, SEQS)
    return jax.vmap(one_sequence)(seq_keys)


def block_scale(own_key, extent, pieces, low, largest):
    level, own = 1.0, jax.random.fold_in(own_key, 6)
    for dim, blocks in pieces:
        draws = jnp.exp(jax.random.uniform(jax.random.fold_in(own, dim), (blocks,), jnp.float32, low / len(pieces), largest / len(pieces)))
        level = level * jnp.repeat(draws, extent[dim] // blocks).reshape([-1 if axis == dim else 1 for axis in range(len(extent))])
    return level


def scatter_about(stream_key, shape, deviation, limit, shards=(), kind=jnp.bfloat16):
    level = block_scale(stream_key, shape, shards, -0.22, 0.18) if shards else 1.0
    drawn = jax.random.normal(stream_key, shape, jnp.float32) * deviation * level
    return jnp.minimum(jnp.maximum(drawn, -limit), limit).astype(kind)


def setup_inputs(seed: int = 0) -> dict:
    seeds = jax.random.split(jax.random.key(seed), 7)
    return {
        "tokens": scatter_about(seeds[0], (TOKENS, D), 1.0, 6.0, ((0, 256),)),
        "gain": jnp.clip(1.0 + 0.18 * jax.random.normal(seeds[1], (D,), jnp.float32), 0.1, 1.9),
        "w_up": scatter_about(seeds[2], (D, FF), D ** -0.5, 0.078125, ((0, 8), (1, 32))),
        "w_down": scatter_about(seeds[3], (FF, D), FF ** -0.5, 0.0546875, ((0, 32), (1, 8))),
        "cotangent": scatter_about(seeds[4], (TOKENS, D), 0.25, 2.0, ((0, 256),)),
        "keep_index": draw_keep_index(jax.random.fold_in(seeds[6], 71), 0),
    }


epsilon = 1e-05

def gelu_tanh(values):
    return jax.nn.gelu(values, approximate=True)

def reference(tokens, gain, w_up, w_down, cotangent, keep_index):
    group_len = 4 * SEQ
    block_width = FF // N_NODE
    up_total = jnp.zeros((D, FF), jnp.float32)
    down_total = jnp.zeros((FF, D), jnp.float32)
    gain_total = jnp.zeros((D,), jnp.float32)
    grads_out = []
    for group in range(N_REPLICA):
        rows_x = tokens[group * group_len:(group + 1) * group_len]
        rows_dy = cotangent[group * group_len:(group + 1) * group_len]
        seq_offsets = (jnp.arange(4, dtype=jnp.int32) * SEQ)[:, None]
        kept = (keep_index[4 * group:4 * group + 4].astype(jnp.int32) + seq_offsets).reshape(-1)
        kept_x = rows_x[kept].astype(jnp.float32)
        kept_dy = rows_dy[kept]
        mean_val = lax.optimization_barrier(jnp.mean(kept_x, axis=1, keepdims=True))
        centred = kept_x - mean_val
        variance = lax.optimization_barrier(jnp.mean(centred * centred, axis=1, keepdims=True))
        rstd = lax.rsqrt(variance + epsilon)
        nhat = centred * rstd
        normed = (nhat * gain).astype(jnp.bfloat16)
        pre_act = jnp.dot(normed, w_up, preferred_element_type=jnp.float32)
        act_f, back_fn = jax.vjp(gelu_tanh, pre_act)
        act = act_f.astype(jnp.bfloat16)
        d_act = jnp.dot(kept_dy, w_down.T, preferred_element_type=jnp.float32)
        d_pre = back_fn(d_act)[0].astype(jnp.bfloat16)
        rows = d_pre.shape[0]
        d_blocks = d_pre.reshape(rows, N_NODE, block_width).astype(jnp.float32)
        w_blocks = w_up.reshape(D, N_NODE, block_width).astype(jnp.float32)
        partials = jnp.einsum('rbf,dbf->brd', d_blocks, w_blocks)
        d_norm = lax.optimization_barrier(jnp.sum(partials.astype(jnp.bfloat16).astype(jnp.float32), axis=0))
        scaled = d_norm * gain
        inner = scaled - lax.optimization_barrier(jnp.mean(scaled, axis=1, keepdims=True)) - nhat * lax.optimization_barrier(jnp.mean(scaled * nhat, axis=1, keepdims=True))
        d_rows = rstd * inner
        grads_out.append(rows_dy.astype(jnp.float32).at[kept].add(d_rows).astype(jnp.bfloat16))
        gain_total = gain_total + lax.optimization_barrier(jnp.sum(d_norm * nhat, axis=0))
        up_part = jnp.dot(normed.T, d_pre, preferred_element_type=jnp.float32)
        down_part = jnp.dot(act.T, kept_dy, preferred_element_type=jnp.float32)
        up_total = up_total + up_part.astype(jnp.bfloat16).astype(jnp.float32)
        down_total = down_total + down_part.astype(jnp.bfloat16).astype(jnp.float32)
    input_grad = jnp.concatenate(grads_out, axis=0)
    return (input_grad, gain_total, up_total.astype(jnp.bfloat16), down_total.astype(jnp.bfloat16))
```

```python
import functools

import jax
import jax.numpy as jnp
from jax import lax
from jax.experimental import pallas as pl
from jax.experimental.pallas import tpu as pltpu
from jax.sharding import PartitionSpec as P

CAP = 12
TOK = 256
D = 6144
HALF = 3072
QW = 768
FB = 384
SEQ_ROWS = 72
BOTH = 144
EPS = 1e-05
NONE = 255
F32 = jnp.float32
BF16 = jnp.bfloat16
MESH = pl.DeviceIdType.MESH

A_TANH = 0.7978845608028654
B_TANH = 0.044715


def dot(a, b, ca=1, cb=0):
    return lax.dot_general(a, b, (((ca,), (cb,)), ((), ())), preferred_element_type=F32)


def iota(shape, dim):
    return lax.broadcasted_iota(jnp.int32, shape, dim)


def body(
    keep_ref, tok_ref, cot_ref, gain_ref, wup_ref, wdn_ref,
    rows_ref, sel_ref, gsum_ref, upg_ref, dng_ref,
    pk0, pk1, g0, g1, ordered, t_buf, wu, wd, keepf, psend, precv, ad, act_t, dpre_t, dpre_b,
    csend, crecv, cown, xs1, xr1, xs2, xr2, zs, zr, nhat_s, dy_s, rstd_s,
    ys1, yr1, ys2, yr2, ykeep, gx, gz, gy,
    ssem, rsem,
):
    r = lax.axis_index("replica")
    n = lax.axis_index("node")
    zl, y = r // 4, lax.rem(r, 4)
    x, zh, c = n // 8, lax.rem(n // 2, 4), lax.rem(n, 2)

    def dev(x_=None, y_=None, zh_=None, zl_=None, c_=None):
        x_ = x if x_ is None else x_
        y_ = y if y_ is None else y_
        zh_ = zh if zh_ is None else zh_
        zl_ = zl if zl_ is None else zl_
        c_ = c if c_ is None else c_
        return (zl_ * 4 + y_, x_ * 8 + zh_ * 2 + c_)

    def step(v, d):
        return lax.rem(v + (d % 4), 4)

    count = [0]
    started = []

    def send(src, dst, to):
        k = count[0]
        count[0] += 1
        d = pltpu.make_async_remote_copy(
            src_ref=src, dst_ref=dst, send_sem=ssem.at[k], recv_sem=rsem.at[k],
            device_id=to, device_id_type=MESH,
        )
        d.start()
        started.append(d)
        return d

    z_peers = [(a, b, e) for a in range(4) for b in range(2) for e in range(2)][1:]

    def z_peer(a, b, e):
        return dev(zh_=step(zh, a), zl_=lax.rem(zl + b, 2), c_=lax.rem(c + e, 2))

    barrier = pltpu.get_barrier_semaphore()
    peers = [z_peer(*p) for p in z_peers]
    peers += [dev(x_=step(x, d)) for d in (1, 2, 3)]
    peers += [dev(y_=step(y, d)) for d in (1, 2, 3)]
    for p in peers:
        pl.semaphore_signal(barrier, inc=1, device_id=p, device_id_type=MESH)

    n8 = lax.rem(n, 8)
    kv = keep_ref[pl.ds(x, 1), :]
    owner = kv // TOK
    before = jnp.sum((owner < n8).astype(F32), axis=1, keepdims=True)
    mine = jnp.sum((owner == n8).astype(F32), axis=1, keepdims=True)
    slot_col = iota((16, SEQ_ROWS), 0).astype(F32)
    j_row = iota((16, SEQ_ROWS), 1).astype(F32)
    local_pos = (kv - n8 * TOK).astype(F32)
    hit = (j_row == before + slot_col) & (slot_col < mine)
    pos = jnp.sum(jnp.where(hit, local_pos, 0.0), axis=1, keepdims=True)
    live = iota((16, TOK), 0).astype(F32) < mine
    sel = jnp.where((iota((16, TOK), 1).astype(F32) == pos) & live, 1.0, 0.0).astype(BF16)
    sel_ref[...] = sel

    row_i, lane_i = iota((16, 128), 0), iota((16, 128), 1)
    kind = lax.rem(row_i, 8)
    i_in = lane_i - (zh * 2 + c) * 16
    slot = jnp.where(
        kind == 0, i_in,
        jnp.where(kind == 1, i_in - 8, jnp.where(kind < 6, 8 + i_in - 4 * (kind - 2), i_in)),
    )
    is_b = (kind >= 2) & (kind < 6)
    ok = (slot >= jnp.where(is_b, 8, 0)) & (slot < jnp.where(kind < 2, 8, CAP))
    slot_f = slot.astype(F32)
    target = jnp.where(ok & (slot_f < mine), before + slot_f, float(NONE))
    here = (i_in >= 0) & (i_in < 16) & (row_i // 8 == zl)
    meta = jnp.where(here, target, 0.0).astype(BF16)

    xr = dot(sel, tok_ref[...])
    dyr = dot(sel, cot_ref[...])
    mean = jnp.mean(xr, axis=1, keepdims=True)
    cen = xr - mean
    rstd = lax.rsqrt(jnp.mean(cen * cen, axis=1, keepdims=True) + EPS)
    nhat = cen * rstd
    nhat_s[...] = nhat
    dy_s[...] = dyr
    rstd_s[...] = jnp.broadcast_to(rstd, (16, 128))
    normed = nhat * gain_ref[...]

    def pack(rows, col):
        blk = rows[:, col:col + 1536]
        main = jnp.concatenate([blk[0:8, 0:768], blk[0:8, 768:1536]], axis=0)
        t = [blk[8:16, 384 * b:384 * (b + 1)] for b in range(4)]
        extra = jnp.concatenate(
            [t[0] + pltpu.roll(t[1], 4, 0), t[2] + pltpu.roll(t[3], 4, 0)], axis=0
        )
        return main.astype(BF16), extra.astype(BF16)

    for a, rows in enumerate((normed, dyr)):
        for h in range(2):
            m, e = pack(rows, h * HALF)
            pk0[a, h, :, 0:768] = m
            pk0[a, h, :, 768:1152] = e
            pk0[a, h, :, 1152:1280] = meta
            m, e = pack(rows, h * HALF + 1536)
            pk1[a, h, :, 0:768] = m
            pk1[a, h, :, 768:1152] = e
    wu[pl.ds(y, 1)] = wup_ref[...][None]
    wd[pl.ds(y, 1)] = wdn_ref[...][None]

    pl.semaphore_wait(barrier, len(peers))

    pks, gs = (pk0, pk1), (g0, g1)
    first = []
    for k in range(2):
        group = []
        for b, e in ((0, 1), (1, 0), (1, 1)):
            zl2, c2 = lax.rem(zl + b, 2), lax.rem(c + e, 2)
            group.append(
                send(pks[k].at[c2, zl2], gs[k].at[zl, zh, c], dev(zl_=zl2, c_=c2))
            )
        first.append(group)

    wu_r = send(wup_ref, wu.at[y], dev(y_=step(y, 1)))
    wd_l = send(wdn_ref, wd.at[y], dev(y_=step(y, -1)))
    wu_l = send(wup_ref, wu.at[y], dev(y_=step(y, -1)))
    wd_r = send(wdn_ref, wd.at[y], dev(y_=step(y, 1)))

    for k in range(2):
        gs[k][pl.ds(zl, 1), pl.ds(zh, 1), pl.ds(c, 1)] = pks[k][pl.ds(c, 1), pl.ds(zl, 1)][None]

    up_z, dn_z = dev(zh_=step(zh, 1)), dev(zh_=step(zh, -1))
    ring = []
    for k in range(2):
        for d in first[k]:
            d.wait_recv()
        ring.append(
            (send(gs[k].at[:, zh], gs[k].at[:, zh], up_z),
             send(gs[k].at[:, zh], gs[k].at[:, zh], dn_z))
        )
    ring2 = []
    for k in range(2):
        ring[k][0].wait_recv()
        f0 = send(gs[k].at[:, step(zh, -1), 0], gs[k].at[:, step(zh, -1), 0], up_z)
        ring[k][1].wait_recv()
        f1 = send(gs[k].at[:, step(zh, 1), 1], gs[k].at[:, step(zh, 1), 1], dn_z)
        ring2.append((f0, f1))

    xp, xm, sib = dev(x_=step(x, 1)), dev(x_=step(x, -1)), dev(c_=1 - c)
    row_f = iota((BOTH, 128), 0).astype(F32)

    def one_hot(meta_sum, kk):
        return jnp.concatenate(
            [
                jnp.where(row_f == meta_sum[kk:kk + 1, :], 1.0, 0.0),
                jnp.where(row_f == meta_sum[8 + kk:9 + kk, :] + SEQ_ROWS, 1.0, 0.0),
            ],
            axis=1,
        )

    hops = []
    for k in range(2):
        for d in ring2[k]:
            d.wait_recv()
        if k == 0:
            ms = jnp.zeros((16, 128), F32)
            for a in range(2):
                for b in range(4):
                    for e in range(2):
                        ms = ms + g0[a, b, e, :, 1152:1280].astype(F32)
            oh = [one_hot(ms, kk).astype(BF16) for kk in range(6)]
            oh_slot = one_hot(ms, 6)
        ga = gs[k][:, :, :, :, 0:768].reshape(256, 768)
        gb = gs[k][:, :, :, :, 768:1152].reshape(256, 384)
        for b in range(4):
            cols = slice((b % 2) * 384, (b % 2) * 384 + 384)
            v = dot(oh[b // 2], ga[:, cols]) + dot(oh[2 + b], gb)
            ordered[2 * k + b // 2, :, cols] = v.astype(BF16)
        src, dst = ordered.at[pl.ds(2 * k, 2)], t_buf.at[c, x, pl.ds(2 * k, 2)]
        hops.append((send(src, dst, xp), send(src, dst, xm), send(src, dst, sib)))
        t_buf[pl.ds(c, 1), pl.ds(x, 1), 2 * k:2 * k + 2] = ordered[2 * k:2 * k + 2][None, None]

    wu_r.wait_recv()
    wu_f = send(wu.at[step(y, -1)], wu.at[step(y, -1)], dev(y_=step(y, 1)))
    wd_l.wait_recv()
    wd_f = send(wd.at[step(y, 1)], wd.at[step(y, 1)], dev(y_=step(y, -1)))

    def piece_of(s, k):
        return t_buf.at[c, s, pl.ds(2 * k, 2)]

    s_m, s_p, s_2 = step(x, -1), step(x, 1), step(x, 2)
    hops[0][0].wait_recv()
    p = piece_of(s_m, 0)
    fx0 = send(p, p, xp)
    sib_m0 = send(p, p, sib)
    hops[0][1].wait_recv()
    p = piece_of(s_p, 0)
    sib_p0 = send(p, p, sib)
    hops[1][1].wait_recv()
    p = piece_of(s_p, 1)
    fx1 = send(p, p, xm)
    sib_p1 = send(p, p, sib)
    hops[1][0].wait_recv()
    p = piece_of(s_m, 1)
    sib_m1 = send(p, p, sib)

    wu_l.wait_recv()
    wd_r.wait_recv()
    wu_f.wait_recv()
    wd_f.wait_recv()

    zp = dev(zl_=1 - zl)

    def forward_part(s):
        pre = jnp.zeros((BOTH, FB), F32)
        dac = jnp.zeros((BOTH, FB), F32)
        for q in range(4):
            pre = pre + dot(t_buf[0, s, q], wu[q])
            dac = dac + dot(t_buf[1, s, q], wd[q], 1, 1)
        lo = jnp.concatenate([pre[:SEQ_ROWS], dac[:SEQ_ROWS]], axis=0)
        hi = jnp.concatenate([pre[SEQ_ROWS:], dac[SEQ_ROWS:]], axis=0)
        is0 = zl == 0
        keepf[s] = jnp.where(is0, lo, hi)
        psend[s] = jnp.where(is0, hi, lo).astype(BF16)
        return send(psend.at[s], precv.at[s], zp)

    def middle(s):
        full = keepf[s] + precv[s].astype(F32)
        v, da = full[:SEQ_ROWS], full[SEQ_ROWS:]
        v2 = v * v
        t = jnp.tanh(A_TANH * (v + B_TANH * v * v2))
        act = 0.5 * v * (1.0 + t)
        slope = 0.5 * (1.0 + t) + 0.5 * v * (1.0 - t * t) * (A_TANH * (1.0 + 3.0 * B_TANH * v2))
        both = jnp.concatenate([act, da * slope], axis=0).astype(BF16)
        ad[zl, s] = both
        return send(ad.at[zl, s], ad.at[zl, s], zp)

    parts = {}
    hops[0][2].wait_recv()
    hops[1][2].wait_recv()
    parts[0] = forward_part(x)
    sib_m0.wait_recv()
    sib_m1.wait_recv()
    parts[1] = forward_part(s_m)
    sib_p0.wait_recv()
    sib_p1.wait_recv()
    parts[2] = forward_part(s_p)
    fx0.wait_recv()
    p = piece_of(s_2, 0)
    sib_20 = send(p, p, sib)
    fx1.wait_recv()
    p = piece_of(s_2, 1)
    sib_21 = send(p, p, sib)
    mids = []
    for i, s in ((0, x), (1, s_m), (2, s_p)):
        parts[i].wait_recv()
        mids.append(middle(s))
    sib_20.wait_recv()
    sib_21.wait_recv()
    parts[3] = forward_part(s_2)
    parts[3].wait_recv()
    mids.append(middle(s_2))

    for m in mids:
        m.wait_recv()
    a_all, d_all = [], []
    for s in range(4):
        u, w = ad[0, s].astype(F32), ad[1, s].astype(F32)
        a_all += [u[:SEQ_ROWS], w[:SEQ_ROWS]]
        d_s = jnp.concatenate([u[SEQ_ROWS:], w[SEQ_ROWS:]], axis=0)
        d_all.append(d_s)
        dpre_b[s] = d_s.astype(BF16)
    act_t[...] = jnp.concatenate(a_all, axis=0).T.astype(BF16)
    dpre_t[...] = jnp.concatenate(d_all, axis=0).T.astype(BF16)

    gx[pl.ds(x, 1)] = jnp.zeros((1, 8, QW), F32)

    def norm_part(s):
        for j in range(2):
            q_own, q_oth = 2 * c + j, 2 * (1 - c) + j
            for q, mine_ in ((q_oth, False), (q_own, True)):
                v = dot(dpre_b[s], wu[q], 1, 1)
                if mine_:
                    cown[s, j] = v
                else:
                    csend[s, j] = v.astype(BF16)
                g = jnp.sum(v * t_buf[0, s, q].astype(F32), axis=0, keepdims=True)
                gx[pl.ds(x, 1), pl.ds(q, 1)] += g[None]
        return send(csend.at[s], crecv.at[s], sib)

    cores = {}
    for i, s in ((2, s_2), (1, s_p), (-1, s_m), (0, x)):
        cores[i] = norm_part(s)
    gain1 = []
    for d in (1, 2, 3):
        gain1.append(send(gx.at[x], gx.at[x], dev(x_=step(x, d))))

    def up_part(q):
        return dot(dpre_t[...], t_buf[0, :, q].reshape(4 * BOTH, QW))

    def down_part(q):
        return dot(act_t[...], t_buf[1, :, q].reshape(4 * BOTH, QW))

    yp, ym = dev(y_=step(y, 1)), dev(y_=step(y, -1))
    q_p, q_m, q_2 = step(y, 1), step(y, -1), step(y, 2)
    ys1[0] = up_part(q_2).astype(BF16)
    y1u = send(ys1.at[0], yr1.at[0], yp)
    ys1[1] = down_part(q_2).astype(BF16)
    y1d = send(ys1.at[1], yr1.at[1], ym)

    def summed(s, j):
        return cown[s, j] + crecv[s, j].astype(F32)

    cores[2].wait_recv()
    xs1[0] = summed(s_2, 0).astype(BF16)
    x1p = send(xs1.at[0], xr1.at[0], xp)
    xs1[1] = summed(s_2, 1).astype(BF16)
    x1m = send(xs1.at[1], xr1.at[1], xm)

    ys2[0, 1] = down_part(q_p).astype(BF16)
    y2pd = send(ys2.at[0, 1], yr2.at[0, 1], yp)
    ys2[1, 0] = up_part(q_m).astype(BF16)
    y2mu = send(ys2.at[1, 0], yr2.at[1, 0], ym)

    cores[1].wait_recv()
    xs2[0, 1] = summed(s_p, 1).astype(BF16)
    x2p1 = send(xs2.at[0, 1], xr2.at[0, 1], xp)
    cores[-1].wait_recv()
    xs2[1, 0] = summed(s_m, 0).astype(BF16)
    x2m0 = send(xs2.at[1, 0], xr2.at[1, 0], xm)

    ykeep[0] = up_part(q_p)
    ykeep[1] = down_part(q_m)

    x1p.wait_recv()
    xs2[0, 0] = (summed(s_p, 0) + xr1[0].astype(F32)).astype(BF16)
    x2p0 = send(xs2.at[0, 0], xr2.at[0, 0], xp)
    x1m.wait_recv()
    xs2[1, 1] = (summed(s_m, 1) + xr1[1].astype(F32)).astype(BF16)
    x2m1 = send(xs2.at[1, 1], xr2.at[1, 1], xm)

    for d in gain1:
        d.wait_recv()
    slot_me = zh * 2 + c
    gz[pl.ds(zl, 1), pl.ds(slot_me, 1)] = (gx[0] + gx[1] + gx[2] + gx[3])[None, None]
    gain2 = [send(gz.at[zl, slot_me], gz.at[zl, slot_me], z_peer(*p_)) for p_ in z_peers]

    y1u.wait_recv()
    ys2[0, 0] = (ykeep[0] + yr1[0].astype(F32)).astype(BF16)
    y2pu = send(ys2.at[0, 0], yr2.at[0, 0], yp)
    y1d.wait_recv()
    ys2[1, 1] = (ykeep[1] + yr1[1].astype(F32)).astype(BF16)
    y2md = send(ys2.at[1, 1], yr2.at[1, 1], ym)

    ykeep[0] = up_part(y)
    ykeep[1] = down_part(y)

    cores[0].wait_recv()
    for d in (x2p0, x2p1, x2m0, x2m1):
        d.wait_recv()
    oh_s = oh_slot.T.astype(BF16)
    for j in range(2):
        total = summed(x, j) + xr2[0, j].astype(F32) + xr2[1, j].astype(F32)
        v = dot(oh_s, total.astype(BF16)).astype(BF16)
        zs[:, :, :, :, 768 * j:768 * (j + 1)] = v.reshape(2, 4, 2, 16, 768)
    owners = []
    for a, b, e in z_peers:
        zh2, zl2, c2 = step(zh, a), lax.rem(zl + b, 2), lax.rem(c + e, 2)
        owners.append(send(zs.at[zl2, zh2, c2], zr.at[zl, c, zh], z_peer(a, b, e)))
    zr[pl.ds(zl, 1), pl.ds(c, 1), pl.ds(zh, 1)] = zs[pl.ds(zl, 1), pl.ds(zh, 1), pl.ds(c, 1)].reshape(1, 1, 1, 16, 1536)

    for d in gain2:
        d.wait_recv()
    for h in range(2):
        g = gz[h, 0]
        for i in range(1, 8):
            g = g + gz[h, i]
        gy[pl.ds(y, 1), h] = g[None]
    gain3 = [send(gy.at[y], gy.at[y], dev(y_=step(y, d))) for d in (1, 2, 3)]

    for d in owners:
        d.wait_recv()
    cols = []
    for a in range(2):
        for e in range(2):
            t = zr[a, e, 0].astype(F32)
            for b in range(1, 4):
                t = t + zr[a, e, b].astype(F32)
            cols.append(t)
    d_norm = jnp.concatenate(cols, axis=1)
    h = d_norm * gain_ref[...]
    nh = nhat_s[...]
    inner = h - jnp.mean(h, axis=1, keepdims=True) - nh * jnp.mean(h * nh, axis=1, keepdims=True)
    rows_ref[...] = (dy_s[...] + rstd_s[:, 0:1] * inner).astype(BF16)

    for d in gain3:
        d.wait_recv()
    gsum_ref[...] = gy[0] + gy[1] + gy[2] + gy[3]

    for d in (y2pd, y2mu, y2pu, y2md):
        d.wait_recv()
    upg_ref[...] = (ykeep[0] + yr2[0, 0].astype(F32) + yr2[1, 0].astype(F32)).astype(BF16)
    dng_ref[...] = (ykeep[1] + yr2[0, 1].astype(F32) + yr2[1, 1].astype(F32)).astype(BF16)

    for d in started:
        d.wait_send()


N_COPIES = 96


def kernel_call(keep, tokens, cotangent, gain, w_up, w_down):
    vmem = pl.BlockSpec(memory_space=pltpu.VMEM)

    def v(shape, dt=BF16):
        return pltpu.VMEM(shape, dt)

    scratch = [
        v((2, 2, 16, 1280)), v((2, 2, 16, 1152)),
        v((2, 4, 2, 16, 1280)), v((2, 4, 2, 16, 1152)),
        v((4, BOTH, QW)), v((2, 4, 4, BOTH, QW)),
        v((4, QW, FB)), v((4, FB, QW)),
        v((4, BOTH, FB), F32), v((4, BOTH, FB)), v((4, BOTH, FB)),
        v((2, 4, BOTH, FB)),
        v((FB, 4 * BOTH)), v((FB, 4 * BOTH)), v((4, BOTH, FB)),
        v((4, 2, BOTH, QW)), v((4, 2, BOTH, QW)), v((4, 2, BOTH, QW), F32),
        v((2, BOTH, QW)), v((2, BOTH, QW)), v((2, 2, BOTH, QW)), v((2, 2, BOTH, QW)),
        v((2, 4, 2, 16, 1536)), v((2, 2, 4, 16, 1536)),
        v((16, D), F32), v((16, D), F32), v((16, 128), F32),
        v((2, FB, QW)), v((2, FB, QW)), v((2, 2, FB, QW)), v((2, 2, FB, QW)),
        v((2, FB, QW), F32),
        v((4, 8, QW), F32), v((2, 8, 8, QW), F32), v((4, 2, 8, QW), F32),
        pltpu.SemaphoreType.DMA((N_COPIES,)), pltpu.SemaphoreType.DMA((N_COPIES,)),
    ]
    return pl.pallas_call(
        body,
        out_shape=(
            jax.ShapeDtypeStruct((16, D), BF16),
            jax.ShapeDtypeStruct((16, TOK), BF16),
            jax.ShapeDtypeStruct((2, 8, QW), F32),
            jax.ShapeDtypeStruct((FB, QW), BF16),
            jax.ShapeDtypeStruct((FB, QW), BF16),
        ),
        in_specs=[vmem] * 6,
        out_specs=(vmem,) * 5,
        scratch_shapes=scratch,
        compiler_params=pltpu.CompilerParams(
            collective_id=0, has_side_effects=True, vmem_limit_bytes=60 * 2**20
        ),
    )(keep, tokens, cotangent, gain, w_up, w_down)


def local(tokens, gain, w_up, w_down, cotangent, keep_index):
    rows, sel, gsum, up_t, down = kernel_call(
        keep_index, tokens, cotangent, gain.reshape(1, D), w_up, w_down
    )
    placed = dot(sel, rows, 0, 0).astype(BF16)
    kept = jnp.sum(sel.astype(F32), axis=0)[:, None] > 0.5
    input_grad = jnp.where(kept, placed, cotangent)
    gain_grad = gsum[:, :4].reshape(D) / gain
    return (input_grad, gain_grad, up_t.T, down)


def solution(mesh):
    in_specs = (
        P(("replica", "node"), None),
        P(),
        P("replica", "node"),
        P("node", "replica"),
        P(("replica", "node"), None),
        P("replica", None),
    )
    out_specs = (P(("replica", "node"), None), P(), P("replica", "node"), P("node", "replica"))
    return jax.shard_map(local, mesh=mesh, in_specs=in_specs, out_specs=out_specs, check_vma=False)
```

```python
import functools

import jax
import jax.numpy as jnp
from jax import lax
from jax.experimental import pallas as pl
from jax.experimental.pallas import tpu as pltpu
from jax.sharding import PartitionSpec as P

CAP = 12
TOK = 256
D = 6144
HALF = 3072
QW = 768
CW = 512
CHUNKS = 6
WW = 512
FB = 384
SEQ_ROWS = 72
BOTH = 144
EPS = 1e-05
NONE = 255
F32 = jnp.float32
BF16 = jnp.bfloat16
MESH = pl.DeviceIdType.MESH

A_TANH = 0.7978845608028654
B_TANH = 0.044715


def dot(a, b, ca=1, cb=0):
    return lax.dot_general(a, b, (((ca,), (cb,)), ((), ())), preferred_element_type=F32)


def iota(shape, dim):
    return lax.broadcasted_iota(jnp.int32, shape, dim)


def body(
    keep_ref, gain_ref, tok_hbm, cot_hbm, wup_ref, wdn_ref,
    rows_ref, sel_ref, gout_ref, upg_ref, dng_ref,
    tok_ref, cot_ref, pk0, pkn, g0, gn, ordered, t_buf, wu, wd,
    keepf, psend, precv, act_t, dpre_t, act_b, dpre_b,
    csend, crecv, cown, xs1, xr1, xs2, xr2, zs, zr, nhat_s, dy_s, rstd_s,
    ys1, yr1, ys2, yr2, ykeep, gx, gz, gy,
    ssem, rsem, lsem,
):
    r = lax.axis_index("replica")
    n = lax.axis_index("node")
    zl, y = r // 4, lax.rem(r, 4)
    x, zh, c = n // 8, lax.rem(n // 2, 4), lax.rem(n, 2)

    def dev(x_=None, y_=None, zh_=None, zl_=None, c_=None):
        x_ = x if x_ is None else x_
        y_ = y if y_ is None else y_
        zh_ = zh if zh_ is None else zh_
        zl_ = zl if zl_ is None else zl_
        c_ = c if c_ is None else c_
        return (zl_ * 4 + y_, x_ * 8 + zh_ * 2 + c_)

    def step(v, d):
        return lax.rem(v + (d % 4), 4)

    count = [0]
    started = []

    def send(src, dst, to):
        k = count[0]
        count[0] += 1
        d = pltpu.make_async_remote_copy(
            src_ref=src, dst_ref=dst, send_sem=ssem.at[k], recv_sem=rsem.at[k],
            device_id=to, device_id_type=MESH,
        )
        d.start()
        started.append(d)
        return d

    def fetch(src, dst, k):
        d = pltpu.make_async_copy(src, dst, lsem.at[k])
        d.start()
        return d

    def col_of(ref, first, width):
        return ref.at[:, pl.ds(pl.multiple_of(first, 128), width)]

    z_peers = [(a, b, e) for a in range(4) for b in range(2) for e in range(2)][1:]

    def z_peer(a, b, e):
        return dev(zh_=step(zh, a), zl_=lax.rem(zl + b, 2), c_=lax.rem(c + e, 2))

    barrier = pltpu.get_barrier_semaphore()
    peers = [z_peer(*p) for p in z_peers]
    peers += [dev(x_=step(x, d)) for d in (1, 2, 3)]
    peers += [dev(y_=step(y, d)) for d in (1, 2, 3)]
    for p in peers:
        pl.semaphore_signal(barrier, inc=1, device_id=p, device_id_type=MESH)
    tok_in = fetch(tok_hbm, tok_ref, 0)
    cot_in = fetch(cot_hbm, cot_ref, 1)
    wu_own = wu.at[pl.ds(pl.multiple_of(y * QW, QW), QW)]
    wd_own = col_of(wd, y * QW, QW)
    wu_in = fetch(wup_ref, wu_own, 2)
    wd_in = fetch(wdn_ref, wd_own, 3)

    n8 = lax.rem(n, 8)
    kv = keep_ref[pl.ds(x, 1), :]
    owner = kv // TOK
    before = jnp.sum((owner < n8).astype(F32), axis=1, keepdims=True)
    mine = jnp.sum((owner == n8).astype(F32), axis=1, keepdims=True)
    slot_col = iota((16, SEQ_ROWS), 0).astype(F32)
    j_row = iota((16, SEQ_ROWS), 1).astype(F32)
    local_pos = (kv - n8 * TOK).astype(F32)
    hit = (j_row == before + slot_col) & (slot_col < mine)
    pos = jnp.sum(jnp.where(hit, local_pos, 0.0), axis=1, keepdims=True)
    live = iota((16, TOK), 0).astype(F32) < mine
    sel = jnp.where((iota((16, TOK), 1).astype(F32) == pos) & live, 1.0, 0.0).astype(BF16)
    sel_ref[...] = sel.astype(F32).T.astype(BF16)

    row_i, lane_i = iota((16, 128), 0), iota((16, 128), 1)
    kind = lax.rem(row_i, 8)
    i_in = lane_i - (zh * 2 + c) * 16
    slot = jnp.where(
        kind == 0, i_in,
        jnp.where(kind == 1, i_in - 8, jnp.where(kind < 6, 8 + i_in - 4 * (kind - 2), i_in)),
    )
    is_b = (kind >= 2) & (kind < 6)
    ok = (slot >= jnp.where(is_b, 8, 0)) & (slot < jnp.where(kind < 2, 8, CAP))
    slot_f = slot.astype(F32)
    target = jnp.where(ok & (slot_f < mine), before + slot_f, float(NONE))
    here = (i_in >= 0) & (i_in < 16) & (row_i // 8 == zl)
    meta = jnp.where(here, target, 0.0).astype(BF16)

    pks = [pk0] + [pkn.at[k] for k in range(CHUNKS - 1)]
    gs = [g0] + [gn.at[k] for k in range(CHUNKS - 1)]

    def pack(rows, a):
        for h in range(2):
            for k in range(CHUNKS):
                col = h * HALF + k * CW
                blk = rows[:, col:col + CW]
                main = jnp.concatenate([blk[0:8, 0:256], blk[0:8, 256:512]], axis=0)
                t = [blk[8:16, 128 * b:128 * (b + 1)] for b in range(4)]
                extra = jnp.concatenate(
                    [t[0] + pltpu.roll(t[1], 4, 0), t[2] + pltpu.roll(t[3], 4, 0)], axis=0
                )
                pks[k][a, h, :, 0:256] = main.astype(BF16)
                pks[k][a, h, :, 256:384] = extra.astype(BF16)
            pk0[a, h, :, 384:512] = meta

    tok_in.wait()
    xr = dot(sel, tok_ref[...])
    mean = jnp.mean(xr, axis=1, keepdims=True)
    cen = xr - mean
    rstd = lax.rsqrt(jnp.mean(cen * cen, axis=1, keepdims=True) + EPS)
    nhat = cen * rstd
    nhat_s[...] = nhat
    rstd_s[...] = jnp.broadcast_to(rstd, (16, 128))
    pack(nhat * gain_ref[...], 0)
    cot_in.wait()
    dyr = dot(sel, cot_ref[...])
    dy_s[...] = dyr
    pack(dyr, 1)

    pl.semaphore_wait(barrier, len(peers))

    first = []
    for k in range(CHUNKS):
        group = []
        for b, e in ((0, 1), (1, 0), (1, 1)):
            zl2, c2 = lax.rem(zl + b, 2), lax.rem(c + e, 2)
            group.append(
                send(pks[k].at[c2, zl2], gs[k].at[zl, zh, c], dev(zl_=zl2, c_=c2))
            )
        first.append(group)

    wu_in.wait()
    wd_in.wait()
    wu_r = send(wu_own, wu_own, dev(y_=step(y, 1)))
    wd_l = send(wd_own, wd_own, dev(y_=step(y, -1)))
    wu_l = send(wu_own, wu_own, dev(y_=step(y, -1)))
    wd_r = send(wd_own, wd_own, dev(y_=step(y, 1)))

    for k in range(CHUNKS):
        gs[k][pl.ds(zl, 1), pl.ds(zh, 1), pl.ds(c, 1)] = pks[k][pl.ds(c, 1), pl.ds(zl, 1)][None]

    up_z, dn_z = dev(zh_=step(zh, 1)), dev(zh_=step(zh, -1))
    xp, xm, sib = dev(x_=step(x, 1)), dev(x_=step(x, -1)), dev(c_=1 - c)
    s_m, s_p, s_2 = step(x, -1), step(x, 1), step(x, 2)
    row_f = iota((BOTH, 128), 0).astype(F32)
    ring, ring2, hops = {}, {}, {}
    oh = []

    def z_own(k):
        for d in first[k]:
            d.wait_recv()
        ring[k] = (
            send(gs[k].at[:, zh], gs[k].at[:, zh], up_z),
            send(gs[k].at[:, zh], gs[k].at[:, zh], dn_z),
        )

    def z_next(k):
        ring[k][0].wait_recv()
        f0 = send(gs[k].at[:, step(zh, -1), 0], gs[k].at[:, step(zh, -1), 0], up_z)
        ring[k][1].wait_recv()
        f1 = send(gs[k].at[:, step(zh, 1), 1], gs[k].at[:, step(zh, 1), 1], dn_z)
        ring2[k] = (f0, f1)

    def one_hot(meta_sum, kk):
        return jnp.concatenate(
            [
                jnp.where(row_f == meta_sum[kk:kk + 1, :], 1.0, 0.0),
                jnp.where(row_f == meta_sum[8 + kk:9 + kk, :] + SEQ_ROWS, 1.0, 0.0),
            ],
            axis=1,
        )

    def chunk_of(a, s, k):
        return t_buf.at[a, s, :, pl.ds(k * CW, CW)]

    def order(k):
        for d in ring2[k]:
            d.wait_recv()
        if k == 0:
            ms = jnp.zeros((16, 128), F32)
            for a in range(2):
                for b in range(4):
                    for e in range(2):
                        ms = ms + g0[a, b, e, :, 384:512].astype(F32)
            oh.extend(one_hot(ms, kk).astype(BF16) for kk in range(6))
            oh.append(one_hot(ms, 6))
        ga = gs[k][:, :, :, :, 0:256].reshape(256, 256)
        gb = gs[k][:, :, :, :, 256:384].reshape(256, 128)
        for a in range(2):
            v = dot(oh[a], ga) + jnp.concatenate(
                [dot(oh[2 + 2 * a], gb), dot(oh[3 + 2 * a], gb)], axis=1
            )
            ordered[k, :, 256 * a:256 * (a + 1)] = v.astype(BF16)
        dst = chunk_of(c, x, k)
        hops[k] = (send(ordered.at[k], dst, xp), send(ordered.at[k], dst, xm))
        t_buf[pl.ds(c, 1), pl.ds(x, 1), :, CW * k:CW * (k + 1)] = ordered[k][None, None]
        if k % 2:
            to_sib(0, x, k // 2)

    sibs, fx = {}, {}

    def to_sib(i, s, pair):
        p = t_buf.at[c, s, :, pl.ds(2 * CW * pair, 2 * CW)]
        sibs[i, pair] = send(p, p, sib)

    def pass_on(k):
        hops[k][0].wait_recv()
        hops[k][1].wait_recv()
        p = chunk_of(c, s_p if k % 2 else s_m, k)
        fx[k] = send(p, p, xm if k % 2 else xp)
        if k % 2:
            to_sib(-1, s_m, k // 2)
            to_sib(1, s_p, k // 2)

    z_own(0)
    z_own(1)
    z_next(0)
    z_own(2)
    z_next(1)
    order(0)
    z_own(3)
    z_next(2)
    order(1)
    z_own(4)
    z_next(3)
    order(2)
    z_own(5)
    z_next(4)
    pass_on(0)
    order(3)
    z_next(5)
    pass_on(1)
    order(4)
    pass_on(2)
    order(5)

    def wu_at(y_):
        return wu.at[pl.ds(pl.multiple_of(y_ * QW, QW), QW)]

    wu_r.wait_recv()
    p = wu_at(step(y, -1))
    wu_f = send(p, p, dev(y_=step(y, 1)))
    wd_l.wait_recv()
    p = col_of(wd, step(y, 1) * QW, QW)
    wd_f = send(p, p, dev(y_=step(y, -1)))

    for k in range(3, CHUNKS):
        pass_on(k)

    for d in (wu_l, wd_r, wu_f, wd_f):
        d.wait_recv()

    zp = dev(zl_=1 - zl)

    def forward_part(i, s):
        pre = dot(t_buf[0, s], wu[...])
        dac = dot(t_buf[1, s], wd[...], 1, 1)
        keepf[i, 0] = pre
        keepf[i, 1] = dac
        psend[i, 0] = pre.astype(BF16)
        psend[i, 1] = dac.astype(BF16)
        parts[i] = send(psend.at[i], precv.at[i], zp)

    def middle(i, s):
        parts[i].wait_recv()
        v = keepf[i, 0] + precv[i, 0].astype(F32)
        da = keepf[i, 1] + precv[i, 1].astype(F32)
        v2 = v * v
        t = jnp.tanh(A_TANH * (v + B_TANH * v * v2))
        act = 0.5 * v * (1.0 + t)
        slope = 0.5 * (1.0 + t) + 0.5 * v * (1.0 - t * t) * (A_TANH * (1.0 + 3.0 * B_TANH * v2))
        act_b[s] = act.astype(BF16)
        dpre_b[s] = (da * slope).astype(BF16)

    parts = {}

    def from_sib(i):
        for k in range(3):
            sibs[i, k].wait_recv()

    def far_pair(k):
        fx[2 * k].wait_recv()
        fx[2 * k + 1].wait_recv()
        to_sib(2, s_2, k)

    from_sib(0)
    forward_part(0, x)
    far_pair(0)
    from_sib(-1)
    forward_part(1, s_m)
    far_pair(1)
    from_sib(1)
    forward_part(2, s_p)
    middle(0, x)
    far_pair(2)
    middle(1, s_m)
    from_sib(2)
    forward_part(3, s_2)
    middle(2, s_p)
    middle(3, s_2)

    dpre_t[...] = dpre_b[...].reshape(4 * BOTH, FB).astype(F32).T.astype(BF16)
    act_t[...] = act_b[...].reshape(4 * BOTH, FB).astype(F32).T.astype(BF16)

    def rows_of(a, q):
        v = t_buf[a, :, :, pl.ds(pl.multiple_of(q * QW, 128), QW)]
        return v.reshape(4 * BOTH, QW)

    def up_part(q):
        return dot(dpre_t[...], rows_of(0, q))

    def down_part(q):
        return dot(act_t[...], rows_of(1, q))

    yp, ym = dev(y_=step(y, 1)), dev(y_=step(y, -1))
    q_p, q_m, q_2 = step(y, 1), step(y, -1), step(y, 2)
    ys1[0] = up_part(q_2).astype(BF16)
    y1u = send(ys1.at[0], yr1.at[0], yp)
    ys1[1] = down_part(q_2).astype(BF16)
    y1d = send(ys1.at[1], yr1.at[1], ym)

    gx[pl.ds(x, 1)] = jnp.zeros((1, 8, WW), F32)
    cores, x1, x2, own = {}, {}, {}, {}

    def norm_wave(w):
        for cc, mine_ in ((1 - c, False), (c, True)):
            first_col = cc * (3 * WW) + w * WW
            wt = wu[pl.ds(pl.multiple_of(first_col, WW), WW), :]
            g = jnp.zeros((1, WW), F32)
            for s in range(4):
                v = dot(dpre_b[s], wt, 1, 1)
                if mine_:
                    cown[w, s] = v
                else:
                    csend[w, s] = v.astype(BF16)
                rows = t_buf[0, s, :, pl.ds(pl.multiple_of(first_col, WW), WW)]
                g = g + jnp.sum(v * rows.astype(F32), axis=0, keepdims=True)
            gx[pl.ds(x, 1), pl.ds(cc * 3 + w, 1)] = g[None]
            if not mine_:
                cores[w] = send(csend.at[w], crecv.at[w], sib)

    def summed(w, s, lo, hi):
        return cown[w, s, :, lo:hi] + crecv[w, s, :, lo:hi].astype(F32)

    def x_first(w):
        cores[w].wait_recv()
        xs1[w, 0] = summed(w, s_2, 0, 256).astype(BF16)
        a = send(xs1.at[w, 0], xr1.at[w, 0], xp)
        xs1[w, 1] = summed(w, s_2, 256, 512).astype(BF16)
        x1[w] = (a, send(xs1.at[w, 1], xr1.at[w, 1], xm))

    def x_second(w):
        xs2[w, 0, :, 256:512] = summed(w, s_p, 256, 512).astype(BF16)
        xs2[w, 1, :, 0:256] = summed(w, s_m, 0, 256).astype(BF16)
        x1[w][0].wait_recv()
        xs2[w, 0, :, 0:256] = (summed(w, s_p, 0, 256) + xr1[w, 0].astype(F32)).astype(BF16)
        a = send(xs2.at[w, 0], xr2.at[w, 0], xp)
        x1[w][1].wait_recv()
        xs2[w, 1, :, 256:512] = (summed(w, s_m, 256, 512) + xr1[w, 1].astype(F32)).astype(BF16)
        x2[w] = (a, send(xs2.at[w, 1], xr2.at[w, 1], xm))

    owners = {}

    def to_owners(w):
        for d in x2[w]:
            d.wait_recv()
        total = summed(w, x, 0, WW) + xr2[w, 0].astype(F32) + xr2[w, 1].astype(F32)
        total = total.astype(BF16)
        v = dot(own[0], total[:, 0:256]) + dot(own[1], total[:, 256:512])
        zs[w, :, :, :, :, 0:256] = v.astype(BF16).reshape(2, 4, 2, 16, 256)
        v = dot(own[2], total[:, 0:128])
        for b in range(1, 4):
            v = v + dot(own[2 + b], total[:, 128 * b:128 * (b + 1)])
        zs[w, :, :, :, :, 256:384] = v.astype(BF16).reshape(2, 4, 2, 16, 128)
        owners[w] = []
        for a, b, e in z_peers:
            zh2, zl2, c2 = step(zh, a), lax.rem(zl + b, 2), lax.rem(c + e, 2)
            owners[w].append(send(zs.at[w, zl2, zh2, c2], zr.at[w, zl, c, zh], z_peer(a, b, e)))
        zr[w, pl.ds(zl, 1), pl.ds(c, 1), pl.ds(zh, 1)] = zs[
            w, pl.ds(zl, 1), pl.ds(zh, 1), pl.ds(c, 1)
        ].reshape(1, 1, 1, 16, 384)

    for kk in range(6):
        own[kk] = oh[kk].astype(F32).T.astype(BF16)

    norm_wave(0)
    norm_wave(1)
    x_first(0)
    norm_wave(2)
    gain1 = [send(gx.at[x], gx.at[x], dev(x_=step(x, d))) for d in (1, 2, 3)]

    ys2[0, 1] = down_part(q_p).astype(BF16)
    y2pd = send(ys2.at[0, 1], yr2.at[0, 1], yp)
    x_first(1)
    ys2[1, 0] = up_part(q_m).astype(BF16)
    y2mu = send(ys2.at[1, 0], yr2.at[1, 0], ym)
    x_second(0)
    x_first(2)
    ykeep[0] = up_part(q_p)
    x_second(1)
    ykeep[1] = down_part(q_m)

    y1u.wait_recv()
    ys2[0, 0] = (ykeep[0] + yr1[0].astype(F32)).astype(BF16)
    y2pu = send(ys2.at[0, 0], yr2.at[0, 0], yp)
    y1d.wait_recv()
    ys2[1, 1] = (ykeep[1] + yr1[1].astype(F32)).astype(BF16)
    y2md = send(ys2.at[1, 1], yr2.at[1, 1], ym)

    to_owners(0)
    x_second(2)
    ykeep[0] = up_part(y)
    ykeep[1] = down_part(y)
    to_owners(1)

    for d in gain1:
        d.wait_recv()
    slot_me = zh * 2 + c
    gz[pl.ds(zl, 1), pl.ds(slot_me, 1)] = (gx[0] + gx[1] + gx[2] + gx[3])[None, None]
    gain2 = [send(gz.at[zl, slot_me], gz.at[zl, slot_me], z_peer(*p_)) for p_ in z_peers]
    to_owners(2)

    for d in gain2:
        d.wait_recv()
    for h in range(2):
        g = gz[h, 0]
        for i in range(1, 8):
            g = g + gz[h, i]
        gy[pl.ds(y, 1), h] = g[None]
    gain3 = [send(gy.at[y], gy.at[y], dev(y_=step(y, d))) for d in (1, 2, 3)]

    cols = []
    for w in range(3):
        for d in owners[w]:
            d.wait_recv()
    zero4 = iota((8, 128), 0) < 4
    for a in range(2):
        for e in range(2):
            for w in range(3):
                t = zr[w, a, e, 0].astype(F32)
                for b in range(1, 4):
                    t = t + zr[w, a, e, b].astype(F32)
                top = jnp.concatenate([t[0:8, 0:256], t[8:16, 0:256]], axis=1)
                e0, e1 = t[0:8, 256:384], t[8:16, 256:384]
                low = [e0, pltpu.roll(e0, 4, 0), e1, pltpu.roll(e1, 4, 0)]
                low = jnp.concatenate([jnp.where(zero4, v, 0.0) for v in low], axis=1)
                cols.append(jnp.concatenate([top, low], axis=0))
    d_norm = jnp.concatenate(cols, axis=1)
    h = d_norm * gain_ref[...]
    nh = nhat_s[...]
    inner = h - jnp.mean(h, axis=1, keepdims=True) - nh * jnp.mean(h * nh, axis=1, keepdims=True)
    rows_ref[...] = (dy_s[...] + rstd_s[:, 0:1] * inner).astype(BF16)

    for d in gain3:
        d.wait_recv()
    for h in range(2):
        g = gy[0, h] + gy[1, h] + gy[2, h] + gy[3, h]
        for i in range(6):
            at = slice(h * HALF + i * WW, h * HALF + (i + 1) * WW)
            gout_ref[:, at] = g[i:i + 1, :] / gain_ref[:, at]

    for d in (y2pd, y2mu, y2pu, y2md):
        d.wait_recv()
    dng_ref[...] = (ykeep[1] + yr2[0, 1].astype(F32) + yr2[1, 1].astype(F32)).astype(BF16)
    upg_ref[...] = (ykeep[0] + yr2[0, 0].astype(F32) + yr2[1, 0].astype(F32)).T.astype(BF16)

    for d in started:
        d.wait_send()


N_COPIES = 192


def kernel_call(keep, tokens, cotangent, gain, w_up, w_down):
    vmem = pl.BlockSpec(memory_space=pltpu.VMEM)
    hbm = pl.BlockSpec(memory_space=pl.ANY)

    def v(shape, dt=BF16):
        return pltpu.VMEM(shape, dt)

    scratch = [
        v((TOK, D)), v((TOK, D)),
        v((2, 2, 16, 512)), v((CHUNKS - 1, 2, 2, 16, 384)),
        v((2, 4, 2, 16, 512)), v((CHUNKS - 1, 2, 4, 2, 16, 384)),
        v((CHUNKS, BOTH, CW)), v((2, 4, BOTH, HALF)),
        v((HALF, FB)), v((FB, HALF)),
        v((4, 2, BOTH, FB), F32), v((4, 2, BOTH, FB)), v((4, 2, BOTH, FB)),
        v((FB, 4 * BOTH)), v((FB, 4 * BOTH)), v((4, BOTH, FB)), v((4, BOTH, FB)),
        v((3, 4, BOTH, WW)), v((3, 4, BOTH, WW)), v((3, 4, BOTH, WW), F32),
        v((3, 2, BOTH, 256)), v((3, 2, BOTH, 256)), v((3, 2, BOTH, WW)), v((3, 2, BOTH, WW)),
        v((3, 2, 4, 2, 16, 384)), v((3, 2, 2, 4, 16, 384)),
        v((16, D), F32), v((16, D), F32), v((16, 128), F32),
        v((2, FB, QW)), v((2, FB, QW)), v((2, 2, FB, QW)), v((2, 2, FB, QW)),
        v((2, FB, QW), F32),
        v((4, 8, WW), F32), v((2, 8, 8, WW), F32), v((4, 2, 8, WW), F32),
        pltpu.SemaphoreType.DMA((N_COPIES,)), pltpu.SemaphoreType.DMA((N_COPIES,)),
        pltpu.SemaphoreType.DMA((4,)),
    ]
    return pl.pallas_call(
        body,
        out_shape=(
            jax.ShapeDtypeStruct((16, D), BF16),
            jax.ShapeDtypeStruct((TOK, 16), BF16),
            jax.ShapeDtypeStruct((1, D), F32),
            jax.ShapeDtypeStruct((QW, FB), BF16),
            jax.ShapeDtypeStruct((FB, QW), BF16),
        ),
        in_specs=[vmem, vmem, hbm, hbm, hbm, hbm],
        out_specs=(vmem,) * 5,
        scratch_shapes=scratch,
        compiler_params=pltpu.CompilerParams(
            collective_id=0, has_side_effects=True, vmem_limit_bytes=60 * 2**20
        ),
    )(keep, gain, tokens, cotangent, w_up, w_down)


def merge_body(sel_ref, rows_ref, cot_ref, out_ref):
    sel = sel_ref[...]
    placed = dot(sel, rows_ref[...])
    kept = jnp.sum(sel.astype(F32), axis=1, keepdims=True) > 0.5
    out_ref[...] = jnp.where(kept, placed, cot_ref[...].astype(F32)).astype(BF16)


def merge(sel, rows, cotangent):
    h = 64
    return pl.pallas_call(
        merge_body,
        grid=(TOK // h,),
        out_shape=jax.ShapeDtypeStruct((TOK, D), BF16),
        in_specs=[
            pl.BlockSpec((h, 16), lambda i: (i, 0)),
            pl.BlockSpec((16, D), lambda i: (0, 0)),
            pl.BlockSpec((h, D), lambda i: (i, 0)),
        ],
        out_specs=pl.BlockSpec((h, D), lambda i: (i, 0)),
    )(sel, rows, cotangent)


def local(tokens, gain, w_up, w_down, cotangent, keep_index):
    rows, sel, gain_grad, up, down = kernel_call(
        keep_index, tokens, cotangent, gain.reshape(1, D), w_up, w_down
    )
    return (merge(sel, rows, cotangent), gain_grad.reshape(D), up, down)


def solution(mesh):
    in_specs = (
        P(("replica", "node"), None),
        P(),
        P("replica", "node"),
        P("node", "replica"),
        P(("replica", "node"), None),
        P("replica", None),
    )
    out_specs = (P(("replica", "node"), None), P(), P("replica", "node"), P("node", "replica"))
    return jax.shard_map(local, mesh=mesh, in_specs=in_specs, out_specs=out_specs, check_vma=False)
```

```python
import functools

import jax
import jax.numpy as jnp
from jax import lax
from jax.experimental import pallas as pl
from jax.experimental.pallas import tpu as pltpu
from jax.sharding import PartitionSpec as P

CAP = 12
TOK = 256
D = 6144
HALF = 3072
QW = 768
CW = 512
CHUNKS = 6
WW = 512
FB = 384
SEQ_ROWS = 72
BOTH = 144
EPS = 1e-05
NONE = 255
F32 = jnp.float32
BF16 = jnp.bfloat16
MESH = pl.DeviceIdType.MESH

A_TANH = 0.7978845608028654
B_TANH = 0.044715


def dot(a, b, ca=1, cb=0):
    return lax.dot_general(a, b, (((ca,), (cb,)), ((), ())), preferred_element_type=F32)


def iota(shape, dim):
    return lax.broadcasted_iota(jnp.int32, shape, dim)


def body(
    keep_ref, gain_ref, tok_hbm, cot_hbm, wup_ref, wdn_ref,
    rows_ref, sel_ref, gout_ref, upg_ref, dng_ref,
    tok_ref, cot_ref, pk0, pkn, g0, gn, ordered, t_buf, wu, wd,
    keepf, psend, precv, act_t, dpre_t, act_b, dpre_b,
    csend, crecv, cown, xs1, xr1, xs2, xr2, zs, zr, nhat_s, dy_s, rstd_s,
    ys1, yr1, ys2, yr2, ykeep, gx, gz, gy,
    ssem, rsem, lsem,
):
    r = lax.axis_index("replica")
    n = lax.axis_index("node")
    zl, y = r // 4, lax.rem(r, 4)
    x, zh, c = n // 8, lax.rem(n // 2, 4), lax.rem(n, 2)

    def dev(x_=None, y_=None, zh_=None, zl_=None, c_=None):
        x_ = x if x_ is None else x_
        y_ = y if y_ is None else y_
        zh_ = zh if zh_ is None else zh_
        zl_ = zl if zl_ is None else zl_
        c_ = c if c_ is None else c_
        return (zl_ * 4 + y_, x_ * 8 + zh_ * 2 + c_)

    def step(v, d):
        return lax.rem(v + (d % 4), 4)

    count = [0]
    started = []

    def send(src, dst, to):
        k = count[0]
        count[0] += 1
        d = pltpu.make_async_remote_copy(
            src_ref=src, dst_ref=dst, send_sem=ssem.at[k], recv_sem=rsem.at[k],
            device_id=to, device_id_type=MESH,
        )
        d.start()
        started.append(d)
        return d

    def fetch(src, dst, k):
        d = pltpu.make_async_copy(src, dst, lsem.at[k])
        d.start()
        return d

    def col_of(ref, first, width):
        return ref.at[:, pl.ds(pl.multiple_of(first, 128), width)]

    z_peers = [(a, b, e) for a in range(4) for b in range(2) for e in range(2)][1:]

    def z_peer(a, b, e):
        return dev(zh_=step(zh, a), zl_=lax.rem(zl + b, 2), c_=lax.rem(c + e, 2))

    barrier = pltpu.get_barrier_semaphore()
    peers = [z_peer(*p) for p in z_peers]
    peers += [dev(x_=step(x, d)) for d in (1, 2, 3)]
    peers += [dev(y_=step(y, d)) for d in (1, 2, 3)]
    for p in peers:
        pl.semaphore_signal(barrier, inc=1, device_id=p, device_id_type=MESH)
    tok_in = fetch(tok_hbm, tok_ref, 0)
    cot_in = fetch(cot_hbm, cot_ref, 1)
    wu_own = wu.at[pl.ds(pl.multiple_of(y * QW, QW), QW)]
    wd_own = col_of(wd, y * QW, QW)
    wu_in = fetch(wup_ref, wu_own, 2)
    wd_in = fetch(wdn_ref, wd_own, 3)

    n8 = lax.rem(n, 8)
    kv = keep_ref[pl.ds(x, 1), :]
    owner = kv // TOK
    before = jnp.sum((owner < n8).astype(F32), axis=1, keepdims=True)
    mine = jnp.sum((owner == n8).astype(F32), axis=1, keepdims=True)
    slot_col = iota((16, SEQ_ROWS), 0).astype(F32)
    j_row = iota((16, SEQ_ROWS), 1).astype(F32)
    local_pos = (kv - n8 * TOK).astype(F32)
    hit = (j_row == before + slot_col) & (slot_col < mine)
    pos = jnp.sum(jnp.where(hit, local_pos, 0.0), axis=1, keepdims=True)
    live = iota((16, TOK), 0).astype(F32) < mine
    sel = jnp.where((iota((16, TOK), 1).astype(F32) == pos) & live, 1.0, 0.0).astype(BF16)
    sel_ref[...] = sel.astype(F32).T.astype(BF16)

    row_i, lane_i = iota((16, 128), 0), iota((16, 128), 1)
    kind = lax.rem(row_i, 8)
    i_in = lane_i - (zh * 2 + c) * 16
    slot = jnp.where(
        kind == 0, i_in,
        jnp.where(kind == 1, i_in - 8, jnp.where(kind < 6, 8 + i_in - 4 * (kind - 2), i_in)),
    )
    is_b = (kind >= 2) & (kind < 6)
    ok = (slot >= jnp.where(is_b, 8, 0)) & (slot < jnp.where(kind < 2, 8, CAP))
    slot_f = slot.astype(F32)
    target = jnp.where(ok & (slot_f < mine), before + slot_f, float(NONE))
    here = (i_in >= 0) & (i_in < 16) & (row_i // 8 == zl)
    meta = jnp.where(here, target, 0.0).astype(BF16)

    pks = [pk0] + [pkn.at[k] for k in range(CHUNKS - 1)]
    gs = [g0] + [gn.at[k] for k in range(CHUNKS - 1)]

    def pack(rows, a):
        for h in range(2):
            for k in range(CHUNKS):
                col = h * HALF + k * CW
                blk = rows[:, col:col + CW]
                main = jnp.concatenate([blk[0:8, 0:256], blk[0:8, 256:512]], axis=0)
                t = [blk[8:16, 128 * b:128 * (b + 1)] for b in range(4)]
                extra = jnp.concatenate(
                    [t[0] + pltpu.roll(t[1], 4, 0), t[2] + pltpu.roll(t[3], 4, 0)], axis=0
                )
                pks[k][a, h, :, 0:256] = main.astype(BF16)
                pks[k][a, h, :, 256:384] = extra.astype(BF16)
            pk0[a, h, :, 384:512] = meta

    tok_in.wait()
    xr = dot(sel, tok_ref[...])
    mean = jnp.mean(xr, axis=1, keepdims=True)
    cen = xr - mean
    rstd = lax.rsqrt(jnp.mean(cen * cen, axis=1, keepdims=True) + EPS)
    nhat = cen * rstd
    nhat_s[...] = nhat
    rstd_s[...] = jnp.broadcast_to(rstd, (16, 128))
    pack(nhat * gain_ref[...], 0)
    pl.semaphore_wait(barrier, len(peers))

    wu_in.wait()
    wd_in.wait()
    wu_r = send(wu_own, wu_own, dev(y_=step(y, 1)))
    wd_l = send(wd_own, wd_own, dev(y_=step(y, -1)))
    wu_l = send(wu_own, wu_own, dev(y_=step(y, -1)))
    wd_r = send(wd_own, wd_own, dev(y_=step(y, 1)))

    cot_in.wait()
    dyr = dot(sel, cot_ref[...])
    dy_s[...] = dyr
    pack(dyr, 1)


    first = []
    for k in range(CHUNKS):
        group = []
        for b, e in ((0, 1), (1, 0), (1, 1)):
            zl2, c2 = lax.rem(zl + b, 2), lax.rem(c + e, 2)
            group.append(
                send(pks[k].at[c2, zl2], gs[k].at[zl, zh, c], dev(zl_=zl2, c_=c2))
            )
        first.append(group)

    for k in range(CHUNKS):
        gs[k][pl.ds(zl, 1), pl.ds(zh, 1), pl.ds(c, 1)] = pks[k][pl.ds(c, 1), pl.ds(zl, 1)][None]

    up_z, dn_z = dev(zh_=step(zh, 1)), dev(zh_=step(zh, -1))
    xp, xm, sib = dev(x_=step(x, 1)), dev(x_=step(x, -1)), dev(c_=1 - c)
    s_m, s_p, s_2 = step(x, -1), step(x, 1), step(x, 2)
    row_f = iota((BOTH, 128), 0).astype(F32)
    ring, ring2, hops = {}, {}, {}
    oh = []

    def z_own(k):
        for d in first[k]:
            d.wait_recv()
        ring[k] = (
            send(gs[k].at[:, zh], gs[k].at[:, zh], up_z),
            send(gs[k].at[:, zh], gs[k].at[:, zh], dn_z),
        )

    def z_next(k):
        ring[k][0].wait_recv()
        f0 = send(gs[k].at[:, step(zh, -1), 0], gs[k].at[:, step(zh, -1), 0], up_z)
        ring[k][1].wait_recv()
        f1 = send(gs[k].at[:, step(zh, 1), 1], gs[k].at[:, step(zh, 1), 1], dn_z)
        ring2[k] = (f0, f1)

    def one_hot(meta_sum, kk):
        return jnp.concatenate(
            [
                jnp.where(row_f == meta_sum[kk:kk + 1, :], 1.0, 0.0),
                jnp.where(row_f == meta_sum[8 + kk:9 + kk, :] + SEQ_ROWS, 1.0, 0.0),
            ],
            axis=1,
        )

    def chunk_of(a, s, k):
        return t_buf.at[a, s, :, pl.ds(k * CW, CW)]

    def order(k):
        for d in ring2[k]:
            d.wait_recv()
        if k == 0:
            ms = jnp.zeros((16, 128), F32)
            for a in range(2):
                for b in range(4):
                    for e in range(2):
                        ms = ms + g0[a, b, e, :, 384:512].astype(F32)
            oh.extend(one_hot(ms, kk).astype(BF16) for kk in range(6))
            oh.append(one_hot(ms, 6))
        ga = gs[k][:, :, :, :, 0:256].reshape(256, 256)
        gb = gs[k][:, :, :, :, 256:384].reshape(256, 128)
        for a in range(2):
            v = dot(oh[a], ga) + jnp.concatenate(
                [dot(oh[2 + 2 * a], gb), dot(oh[3 + 2 * a], gb)], axis=1
            )
            ordered[k, :, 256 * a:256 * (a + 1)] = v.astype(BF16)
        dst = chunk_of(c, x, k)
        hops[k] = (send(ordered.at[k], dst, xp), send(ordered.at[k], dst, xm))
        t_buf[pl.ds(c, 1), pl.ds(x, 1), :, CW * k:CW * (k + 1)] = ordered[k][None, None]
        if k % 2:
            to_sib(0, x, k // 2)

    sibs, fx = {}, {}

    def to_sib(i, s, pair):
        p = t_buf.at[c, s, :, pl.ds(2 * CW * pair, 2 * CW)]
        sibs[i, pair] = send(p, p, sib)

    def pass_on(k):
        hops[k][0].wait_recv()
        hops[k][1].wait_recv()
        p = chunk_of(c, s_p if k % 2 else s_m, k)
        fx[k] = send(p, p, xm if k % 2 else xp)
        if k % 2:
            to_sib(-1, s_m, k // 2)
            to_sib(1, s_p, k // 2)

    zp = dev(zl_=1 - zl)

    def forward_part(i, s):
        if i < 3:
            pre = dot(t_buf[0, s], wu[...])
            dac = dot(t_buf[1, s], wd[...], 1, 1)
        else:
            pre = jnp.zeros((BOTH, FB), F32)
            dac = jnp.zeros((BOTH, FB), F32)
            for k in range(3):
                sibs[2, k].wait_recv()
                at = slice(2 * CW * k, 2 * CW * (k + 1))
                pre = pre + dot(t_buf[0, s, :, at], wu[at])
                dac = dac + dot(t_buf[1, s, :, at], wd[:, at], 1, 1)
        keepf[i, 0] = pre
        keepf[i, 1] = dac
        psend[i, 0] = pre.astype(BF16)
        psend[i, 1] = dac.astype(BF16)
        parts[i] = send(psend.at[i], precv.at[i], zp)

    def middle(i, s):
        parts[i].wait_recv()
        v = keepf[i, 0] + precv[i, 0].astype(F32)
        da = keepf[i, 1] + precv[i, 1].astype(F32)
        v2 = v * v
        t = jnp.tanh(A_TANH * (v + B_TANH * v * v2))
        act = 0.5 * v * (1.0 + t)
        slope = 0.5 * (1.0 + t) + 0.5 * v * (1.0 - t * t) * (A_TANH * (1.0 + 3.0 * B_TANH * v2))
        act_b[s] = act.astype(BF16)
        dpre_b[s] = (da * slope).astype(BF16)

    parts = {}

    def from_sib(i):
        for k in range(3):
            sibs[i, k].wait_recv()

    def far_pair(k):
        fx[2 * k].wait_recv()
        fx[2 * k + 1].wait_recv()
        to_sib(2, s_2, k)

    z_own(0)
    z_own(1)
    z_next(0)
    z_own(2)
    z_next(1)
    order(0)
    z_own(3)
    z_next(2)
    order(1)
    z_own(4)
    z_next(3)
    order(2)
    z_own(5)
    z_next(4)
    pass_on(0)
    order(3)

    def wu_at(y_):
        return wu.at[pl.ds(pl.multiple_of(y_ * QW, QW), QW)]

    wu_r.wait_recv()
    p = wu_at(step(y, -1))
    wu_f = send(p, p, dev(y_=step(y, 1)))
    wd_l.wait_recv()
    p = col_of(wd, step(y, 1) * QW, QW)
    wd_f = send(p, p, dev(y_=step(y, -1)))

    z_next(5)
    pass_on(1)
    order(4)
    pass_on(2)
    order(5)
    pass_on(3)
    for d in (wu_l, wd_r, wu_f, wd_f):
        d.wait_recv()
    from_sib(0)
    forward_part(0, x)
    pass_on(4)
    pass_on(5)
    far_pair(0)
    from_sib(-1)
    forward_part(1, s_m)
    far_pair(1)
    from_sib(1)
    forward_part(2, s_p)
    middle(0, x)
    far_pair(2)
    middle(1, s_m)
    forward_part(3, s_2)
    middle(2, s_p)
    middle(3, s_2)

    dpre_t[...] = dpre_b[...].reshape(4 * BOTH, FB).astype(F32).T.astype(BF16)
    act_t[...] = act_b[...].reshape(4 * BOTH, FB).astype(F32).T.astype(BF16)

    def rows_of(a, q):
        v = t_buf[a, :, :, pl.ds(pl.multiple_of(q * QW, 128), QW)]
        return v.reshape(4 * BOTH, QW)

    def up_part(q):
        return dot(dpre_t[...], rows_of(0, q))

    def down_part(q):
        return dot(act_t[...], rows_of(1, q))

    yp, ym = dev(y_=step(y, 1)), dev(y_=step(y, -1))
    q_p, q_m, q_2 = step(y, 1), step(y, -1), step(y, 2)
    ys1[0] = up_part(q_2).astype(BF16)
    y1u = send(ys1.at[0], yr1.at[0], yp)
    ys1[1] = down_part(q_2).astype(BF16)
    y1d = send(ys1.at[1], yr1.at[1], ym)

    gx[pl.ds(x, 1)] = jnp.zeros((1, 8, WW), F32)
    cores, x1, x2, own = {}, {}, {}, {}

    def norm_wave(w):
        for cc, mine_ in ((1 - c, False), (c, True)):
            first_col = cc * (3 * WW) + w * WW
            wt = wu[pl.ds(pl.multiple_of(first_col, WW), WW), :]
            g = jnp.zeros((1, WW), F32)
            for s in range(4):
                v = dot(dpre_b[s], wt, 1, 1)
                if mine_:
                    cown[w, s] = v
                else:
                    csend[w, s] = v.astype(BF16)
                rows = t_buf[0, s, :, pl.ds(pl.multiple_of(first_col, WW), WW)]
                g = g + jnp.sum(v * rows.astype(F32), axis=0, keepdims=True)
            gx[pl.ds(x, 1), pl.ds(cc * 3 + w, 1)] = g[None]
            if not mine_:
                cores[w] = send(csend.at[w], crecv.at[w], sib)

    def summed(w, s, lo, hi):
        return cown[w, s, :, lo:hi] + crecv[w, s, :, lo:hi].astype(F32)

    def x_first(w):
        cores[w].wait_recv()
        xs1[w, 0] = summed(w, s_2, 0, 256).astype(BF16)
        a = send(xs1.at[w, 0], xr1.at[w, 0], xp)
        xs1[w, 1] = summed(w, s_2, 256, 512).astype(BF16)
        x1[w] = (a, send(xs1.at[w, 1], xr1.at[w, 1], xm))

    def x_second(w):
        xs2[w, 0, :, 256:512] = summed(w, s_p, 256, 512).astype(BF16)
        xs2[w, 1, :, 0:256] = summed(w, s_m, 0, 256).astype(BF16)
        x1[w][0].wait_recv()
        xs2[w, 0, :, 0:256] = (summed(w, s_p, 0, 256) + xr1[w, 0].astype(F32)).astype(BF16)
        a = send(xs2.at[w, 0], xr2.at[w, 0], xp)
        x1[w][1].wait_recv()
        xs2[w, 1, :, 256:512] = (summed(w, s_m, 256, 512) + xr1[w, 1].astype(F32)).astype(BF16)
        x2[w] = (a, send(xs2.at[w, 1], xr2.at[w, 1], xm))

    owners = {}

    def to_owners(w):
        for d in x2[w]:
            d.wait_recv()
        total = summed(w, x, 0, WW) + xr2[w, 0].astype(F32) + xr2[w, 1].astype(F32)
        total = total.astype(BF16)
        v = dot(own[0], total[:, 0:256]) + dot(own[1], total[:, 256:512])
        zs[w, :, :, :, :, 0:256] = v.astype(BF16).reshape(2, 4, 2, 16, 256)
        v = dot(own[2], total[:, 0:128])
        for b in range(1, 4):
            v = v + dot(own[2 + b], total[:, 128 * b:128 * (b + 1)])
        zs[w, :, :, :, :, 256:384] = v.astype(BF16).reshape(2, 4, 2, 16, 128)
        owners[w] = []
        for a, b, e in z_peers:
            zh2, zl2, c2 = step(zh, a), lax.rem(zl + b, 2), lax.rem(c + e, 2)
            owners[w].append(send(zs.at[w, zl2, zh2, c2], zr.at[w, zl, c, zh], z_peer(a, b, e)))
        zr[w, pl.ds(zl, 1), pl.ds(c, 1), pl.ds(zh, 1)] = zs[
            w, pl.ds(zl, 1), pl.ds(zh, 1), pl.ds(c, 1)
        ].reshape(1, 1, 1, 16, 384)

    for kk in range(6):
        own[kk] = oh[kk].astype(F32).T.astype(BF16)

    norm_wave(0)
    norm_wave(1)
    x_first(0)
    norm_wave(2)
    gain1 = [send(gx.at[x], gx.at[x], dev(x_=step(x, d))) for d in (1, 2, 3)]

    ys2[0, 1] = down_part(q_p).astype(BF16)
    y2pd = send(ys2.at[0, 1], yr2.at[0, 1], yp)
    x_first(1)
    ys2[1, 0] = up_part(q_m).astype(BF16)
    y2mu = send(ys2.at[1, 0], yr2.at[1, 0], ym)
    x_second(0)
    x_first(2)
    ykeep[0] = up_part(q_p)
    x_second(1)
    ykeep[1] = down_part(q_m)

    y1u.wait_recv()
    ys2[0, 0] = (ykeep[0] + yr1[0].astype(F32)).astype(BF16)
    y2pu = send(ys2.at[0, 0], yr2.at[0, 0], yp)
    y1d.wait_recv()
    ys2[1, 1] = (ykeep[1] + yr1[1].astype(F32)).astype(BF16)
    y2md = send(ys2.at[1, 1], yr2.at[1, 1], ym)

    to_owners(0)
    x_second(2)
    ykeep[0] = up_part(y)
    ykeep[1] = down_part(y)
    to_owners(1)

    for d in gain1:
        d.wait_recv()
    slot_me = zh * 2 + c
    gz[pl.ds(zl, 1), pl.ds(slot_me, 1)] = (gx[0] + gx[1] + gx[2] + gx[3])[None, None]
    gain2 = [send(gz.at[zl, slot_me], gz.at[zl, slot_me], z_peer(*p_)) for p_ in z_peers]
    to_owners(2)

    for d in gain2:
        d.wait_recv()
    for h in range(2):
        g = gz[h, 0]
        for i in range(1, 8):
            g = g + gz[h, i]
        gy[pl.ds(y, 1), h] = g[None]
    gain3 = [send(gy.at[y], gy.at[y], dev(y_=step(y, d))) for d in (1, 2, 3)]

    cols = []
    for w in range(3):
        for d in owners[w]:
            d.wait_recv()
    zero4 = iota((8, 128), 0) < 4
    for a in range(2):
        for e in range(2):
            for w in range(3):
                t = zr[w, a, e, 0].astype(F32)
                for b in range(1, 4):
                    t = t + zr[w, a, e, b].astype(F32)
                top = jnp.concatenate([t[0:8, 0:256], t[8:16, 0:256]], axis=1)
                e0, e1 = t[0:8, 256:384], t[8:16, 256:384]
                low = [e0, pltpu.roll(e0, 4, 0), e1, pltpu.roll(e1, 4, 0)]
                low = jnp.concatenate([jnp.where(zero4, v, 0.0) for v in low], axis=1)
                cols.append(jnp.concatenate([top, low], axis=0))
    d_norm = jnp.concatenate(cols, axis=1)
    h = d_norm * gain_ref[...]
    nh = nhat_s[...]
    inner = h - jnp.mean(h, axis=1, keepdims=True) - nh * jnp.mean(h * nh, axis=1, keepdims=True)
    rows_ref[...] = (dy_s[...] + rstd_s[:, 0:1] * inner).astype(BF16)

    for d in gain3:
        d.wait_recv()
    for h in range(2):
        g = gy[0, h] + gy[1, h] + gy[2, h] + gy[3, h]
        for i in range(6):
            at = slice(h * HALF + i * WW, h * HALF + (i + 1) * WW)
            gout_ref[:, at] = g[i:i + 1, :] / gain_ref[:, at]

    for d in (y2pd, y2mu, y2pu, y2md):
        d.wait_recv()
    dng_ref[...] = (ykeep[1] + yr2[0, 1].astype(F32) + yr2[1, 1].astype(F32)).astype(BF16)
    upg_ref[...] = (ykeep[0] + yr2[0, 0].astype(F32) + yr2[1, 0].astype(F32)).T.astype(BF16)

    for d in started:
        d.wait_send()


N_COPIES = 192


def kernel_call(keep, tokens, cotangent, gain, w_up, w_down):
    vmem = pl.BlockSpec(memory_space=pltpu.VMEM)
    hbm = pl.BlockSpec(memory_space=pl.ANY)

    def v(shape, dt=BF16):
        return pltpu.VMEM(shape, dt)

    scratch = [
        v((TOK, D)), v((TOK, D)),
        v((2, 2, 16, 512)), v((CHUNKS - 1, 2, 2, 16, 384)),
        v((2, 4, 2, 16, 512)), v((CHUNKS - 1, 2, 4, 2, 16, 384)),
        v((CHUNKS, BOTH, CW)), v((2, 4, BOTH, HALF)),
        v((HALF, FB)), v((FB, HALF)),
        v((4, 2, BOTH, FB), F32), v((4, 2, BOTH, FB)), v((4, 2, BOTH, FB)),
        v((FB, 4 * BOTH)), v((FB, 4 * BOTH)), v((4, BOTH, FB)), v((4, BOTH, FB)),
        v((3, 4, BOTH, WW)), v((3, 4, BOTH, WW)), v((3, 4, BOTH, WW), F32),
        v((3, 2, BOTH, 256)), v((3, 2, BOTH, 256)), v((3, 2, BOTH, WW)), v((3, 2, BOTH, WW)),
        v((3, 2, 4, 2, 16, 384)), v((3, 2, 2, 4, 16, 384)),
        v((16, D), F32), v((16, D), F32), v((16, 128), F32),
        v((2, FB, QW)), v((2, FB, QW)), v((2, 2, FB, QW)), v((2, 2, FB, QW)),
        v((2, FB, QW), F32),
        v((4, 8, WW), F32), v((2, 8, 8, WW), F32), v((4, 2, 8, WW), F32),
        pltpu.SemaphoreType.DMA((N_COPIES,)), pltpu.SemaphoreType.DMA((N_COPIES,)),
        pltpu.SemaphoreType.DMA((4,)),
    ]
    return pl.pallas_call(
        body,
        out_shape=(
            jax.ShapeDtypeStruct((16, D), BF16),
            jax.ShapeDtypeStruct((TOK, 16), BF16),
            jax.ShapeDtypeStruct((1, D), F32),
            jax.ShapeDtypeStruct((QW, FB), BF16),
            jax.ShapeDtypeStruct((FB, QW), BF16),
        ),
        in_specs=[vmem, vmem, hbm, hbm, hbm, hbm],
        out_specs=(vmem,) * 5,
        scratch_shapes=scratch,
        compiler_params=pltpu.CompilerParams(
            collective_id=0, has_side_effects=True, vmem_limit_bytes=60 * 2**20
        ),
    )(keep, gain, tokens, cotangent, w_up, w_down)


def merge_body(sel_ref, rows_ref, cot_ref, up_ref, down_ref, gain_ref, out_ref, up_out, down_out, gain_out):
    sel = sel_ref[...]
    placed = dot(sel, rows_ref[...])
    kept = jnp.sum(sel.astype(F32), axis=1, keepdims=True) > 0.5
    out_ref[...] = jnp.where(kept, placed, cot_ref[...].astype(F32)).astype(BF16)
    up_out[...] = up_ref[...]
    down_out[...] = down_ref[...]
    gain_out[...] = gain_ref[...]


def merge(sel, rows, cotangent, up, down, gain):
    steps = 8
    h = TOK // steps

    def block(*shape):
        return pl.BlockSpec(shape, lambda i: (i, 0))

    results = [block(h, D), block(QW // steps, FB), block(FB // steps, QW), pl.BlockSpec((1, D), lambda i: (0, 0))]
    return pl.pallas_call(
        merge_body,
        grid=(steps,),
        out_shape=(
            jax.ShapeDtypeStruct((TOK, D), BF16),
            jax.ShapeDtypeStruct((QW, FB), BF16),
            jax.ShapeDtypeStruct((FB, QW), BF16),
            jax.ShapeDtypeStruct((1, D), F32),
        ),
        in_specs=[block(h, 16), pl.BlockSpec((16, D), lambda i: (0, 0))] + results,
        out_specs=results,
    )(sel, rows, cotangent, up, down, gain)


def local(tokens, gain, w_up, w_down, cotangent, keep_index):
    rows, sel, gain_grad, up, down = kernel_call(
        keep_index, tokens, cotangent, gain.reshape(1, D), w_up, w_down
    )
    input_grad, up, down, gain_grad = merge(sel, rows, cotangent, up, down, gain_grad)
    return (input_grad, gain_grad.reshape(D), up, down)


def solution(mesh):
    in_specs = (
        P(("replica", "node"), None),
        P(),
        P("replica", "node"),
        P("node", "replica"),
        P(("replica", "node"), None),
        P("replica", None),
    )
    out_specs = (P(("replica", "node"), None), P(), P("replica", "node"), P("node", "replica"))
    return jax.shard_map(local, mesh=mesh, in_specs=in_specs, out_specs=out_specs, check_vma=False)
```

```python
import functools

import jax
import jax.numpy as jnp
from jax import lax
from jax.experimental import pallas as pl
from jax.experimental.pallas import tpu as pltpu
from jax.sharding import PartitionSpec as P

CAP = 12
TOK = 256
D = 6144
HALF = 3072
QW = 768
CW = 512
CHUNKS = 6
WW = 512
FB = 384
SEQ_ROWS = 72
BOTH = 144
EPS = 1e-05
NONE = 255
F32 = jnp.float32
BF16 = jnp.bfloat16
MESH = pl.DeviceIdType.MESH

A_TANH = 0.7978845608028654
B_TANH = 0.044715


def dot(a, b, ca=1, cb=0):
    return lax.dot_general(a, b, (((ca,), (cb,)), ((), ())), preferred_element_type=F32)


def iota(shape, dim):
    return lax.broadcasted_iota(jnp.int32, shape, dim)


def body(
    keep_ref, gain_ref, tok_hbm, cot_hbm, wup_ref, wdn_ref,
    rows_ref, sel_ref, gout_ref, upg_ref, dng_ref,
    tok_ref, cot_ref, pk0, pkn, g0, gn, ordered, t_buf, wu, wd,
    keepf, psend, precv, act_t, dpre_t, act_b, dpre_b,
    csend, crecv, cown, xs1, xr1, xs2, xr2, zs, zr, nhat_s, dy_s, rstd_s,
    ys1, yr1, ys2, yr2, ykeep, gx, gz, gy,
    ssem, rsem, lsem,
):
    r = lax.axis_index("replica")
    n = lax.axis_index("node")
    zl, y = r // 4, lax.rem(r, 4)
    x, zh, c = n // 8, lax.rem(n // 2, 4), lax.rem(n, 2)

    def dev(x_=None, y_=None, zh_=None, zl_=None, c_=None):
        x_ = x if x_ is None else x_
        y_ = y if y_ is None else y_
        zh_ = zh if zh_ is None else zh_
        zl_ = zl if zl_ is None else zl_
        c_ = c if c_ is None else c_
        return (zl_ * 4 + y_, x_ * 8 + zh_ * 2 + c_)

    def step(v, d):
        return lax.rem(v + (d % 4), 4)

    count = [0]
    started = []

    def send(src, dst, to):
        k = count[0]
        count[0] += 1
        d = pltpu.make_async_remote_copy(
            src_ref=src, dst_ref=dst, send_sem=ssem.at[k], recv_sem=rsem.at[k],
            device_id=to, device_id_type=MESH,
        )
        d.start()
        started.append(d)
        return d

    def fetch(src, dst, k):
        d = pltpu.make_async_copy(src, dst, lsem.at[k])
        d.start()
        return d

    def col_of(ref, first, width):
        return ref.at[:, pl.ds(pl.multiple_of(first, 128), width)]

    z_peers = [(a, b, e) for a in range(4) for b in range(2) for e in range(2)][1:]

    def z_peer(a, b, e):
        return dev(zh_=step(zh, a), zl_=lax.rem(zl + b, 2), c_=lax.rem(c + e, 2))

    barrier = pltpu.get_barrier_semaphore()
    peers = [z_peer(*p) for p in z_peers]
    peers += [dev(x_=step(x, d)) for d in (1, 2, 3)]
    peers += [dev(y_=step(y, d)) for d in (1, 2, 3)]
    for p in peers:
        pl.semaphore_signal(barrier, inc=1, device_id=p, device_id_type=MESH)
    tok_in, cot_in = [], []
    for ref, to, ins, k in ((tok_hbm, tok_ref, tok_in, 2), (cot_hbm, cot_ref, cot_in, 6)):
        for i in range(4):
            at = pl.ds(64 * i, 64)
            ins.append(fetch(ref.at[at], to.at[at], k + i))
    wu_own = wu.at[pl.ds(pl.multiple_of(y * QW, QW), QW)]
    wd_own = col_of(wd, y * QW, QW)
    wu_in = fetch(wup_ref, wu_own, 0)
    wd_in = fetch(wdn_ref, wd_own, 1)

    n8 = lax.rem(n, 8)
    kv = keep_ref[pl.ds(x, 1), :]
    owner = kv // TOK
    before = jnp.sum((owner < n8).astype(F32), axis=1, keepdims=True)
    mine = jnp.sum((owner == n8).astype(F32), axis=1, keepdims=True)
    slot_col = iota((16, SEQ_ROWS), 0).astype(F32)
    j_row = iota((16, SEQ_ROWS), 1).astype(F32)
    local_pos = (kv - n8 * TOK).astype(F32)
    hit = (j_row == before + slot_col) & (slot_col < mine)
    pos = jnp.sum(jnp.where(hit, local_pos, 0.0), axis=1, keepdims=True)
    live = iota((16, TOK), 0).astype(F32) < mine
    sel = jnp.where((iota((16, TOK), 1).astype(F32) == pos) & live, 1.0, 0.0).astype(BF16)
    sel_ref[...] = sel.astype(F32).T.astype(BF16)

    row_i, lane_i = iota((16, 128), 0), iota((16, 128), 1)
    kind = lax.rem(row_i, 8)
    i_in = lane_i - (zh * 2 + c) * 16
    slot = jnp.where(
        kind == 0, i_in,
        jnp.where(kind == 1, i_in - 8, jnp.where(kind < 6, 8 + i_in - 4 * (kind - 2), i_in)),
    )
    is_b = (kind >= 2) & (kind < 6)
    ok = (slot >= jnp.where(is_b, 8, 0)) & (slot < jnp.where(kind < 2, 8, CAP))
    slot_f = slot.astype(F32)
    target = jnp.where(ok & (slot_f < mine), before + slot_f, float(NONE))
    here = (i_in >= 0) & (i_in < 16) & (row_i // 8 == zl)
    meta = jnp.where(here, target, 0.0).astype(BF16)

    pks = [pk0] + [pkn.at[k] for k in range(CHUNKS - 1)]
    gs = [g0] + [gn.at[k] for k in range(CHUNKS - 1)]

    def pack(rows, a):
        for h in range(2):
            for k in range(CHUNKS):
                col = h * HALF + k * CW
                blk = rows[:, col:col + CW]
                main = jnp.concatenate([blk[0:8, 0:256], blk[0:8, 256:512]], axis=0)
                t = [blk[8:16, 128 * b:128 * (b + 1)] for b in range(4)]
                extra = jnp.concatenate(
                    [t[0] + pltpu.roll(t[1], 4, 0), t[2] + pltpu.roll(t[3], 4, 0)], axis=0
                )
                pks[k][a, h, :, 0:256] = main.astype(BF16)
                pks[k][a, h, :, 256:384] = extra.astype(BF16)
            pk0[a, h, :, 384:512] = meta

    for d in tok_in:
        d.wait()
    xr = dot(sel, tok_ref[...])
    mean = jnp.mean(xr, axis=1, keepdims=True)
    cen = xr - mean
    rstd = lax.rsqrt(jnp.mean(cen * cen, axis=1, keepdims=True) + EPS)
    nhat = cen * rstd
    nhat_s[...] = nhat
    rstd_s[...] = jnp.broadcast_to(rstd, (16, 128))
    pack(nhat * gain_ref[...], 0)
    pl.semaphore_wait(barrier, len(peers))

    wu_in.wait()
    wd_in.wait()
    wu_r = send(wu_own, wu_own, dev(y_=step(y, 1)))
    wd_l = send(wd_own, wd_own, dev(y_=step(y, -1)))
    wu_l = send(wu_own, wu_own, dev(y_=step(y, -1)))
    wd_r = send(wd_own, wd_own, dev(y_=step(y, 1)))

    for d in cot_in:
        d.wait()
    dyr = dot(sel, cot_ref[...])
    dy_s[...] = dyr
    pack(dyr, 1)


    first = []
    for k in range(CHUNKS):
        group = []
        for b, e in ((0, 1), (1, 0), (1, 1)):
            zl2, c2 = lax.rem(zl + b, 2), lax.rem(c + e, 2)
            group.append(
                send(pks[k].at[c2, zl2], gs[k].at[zl, zh, c], dev(zl_=zl2, c_=c2))
            )
        first.append(group)

    for k in range(CHUNKS):
        gs[k][pl.ds(zl, 1), pl.ds(zh, 1), pl.ds(c, 1)] = pks[k][pl.ds(c, 1), pl.ds(zl, 1)][None]

    up_z, dn_z = dev(zh_=step(zh, 1)), dev(zh_=step(zh, -1))
    xp, xm, sib = dev(x_=step(x, 1)), dev(x_=step(x, -1)), dev(c_=1 - c)
    s_m, s_p, s_2 = step(x, -1), step(x, 1), step(x, 2)
    row_f = iota((BOTH, 128), 0).astype(F32)
    ring, ring2, hops = {}, {}, {}
    oh = []

    def z_own(k):
        for d in first[k]:
            d.wait_recv()
        ring[k] = (
            send(gs[k].at[:, zh], gs[k].at[:, zh], up_z),
            send(gs[k].at[:, zh], gs[k].at[:, zh], dn_z),
        )

    def z_next(k):
        ring[k][0].wait_recv()
        f0 = send(gs[k].at[:, step(zh, -1), 0], gs[k].at[:, step(zh, -1), 0], up_z)
        ring[k][1].wait_recv()
        f1 = send(gs[k].at[:, step(zh, 1), 1], gs[k].at[:, step(zh, 1), 1], dn_z)
        ring2[k] = (f0, f1)

    def one_hot(meta_sum, kk):
        return jnp.concatenate(
            [
                jnp.where(row_f == meta_sum[kk:kk + 1, :], 1.0, 0.0),
                jnp.where(row_f == meta_sum[8 + kk:9 + kk, :] + SEQ_ROWS, 1.0, 0.0),
            ],
            axis=1,
        )

    def chunk_of(a, s, k):
        return t_buf.at[a, s, :, pl.ds(k * CW, CW)]

    def order(k):
        for d in ring2[k]:
            d.wait_recv()
        if k == 0:
            ms = jnp.zeros((16, 128), F32)
            for a in range(2):
                for b in range(4):
                    for e in range(2):
                        ms = ms + g0[a, b, e, :, 384:512].astype(F32)
            oh.extend(one_hot(ms, kk).astype(BF16) for kk in range(6))
            oh.append(one_hot(ms, 6))
        ga = gs[k][:, :, :, :, 0:256].reshape(256, 256)
        gb = gs[k][:, :, :, :, 256:384].reshape(256, 128)
        for a in range(2):
            v = dot(oh[a], ga) + jnp.concatenate(
                [dot(oh[2 + 2 * a], gb), dot(oh[3 + 2 * a], gb)], axis=1
            )
            ordered[k, :, 256 * a:256 * (a + 1)] = v.astype(BF16)
        dst = chunk_of(c, x, k)
        hops[k] = (send(ordered.at[k], dst, xp), send(ordered.at[k], dst, xm))
        t_buf[pl.ds(c, 1), pl.ds(x, 1), :, CW * k:CW * (k + 1)] = ordered[k][None, None]
        if k % 2:
            to_sib(0, x, k // 2)

    sibs, fx = {}, {}

    def to_sib(i, s, pair):
        p = t_buf.at[c, s, :, pl.ds(2 * CW * pair, 2 * CW)]
        sibs[i, pair] = send(p, p, sib)

    def pass_on(k):
        hops[k][0].wait_recv()
        hops[k][1].wait_recv()
        p = chunk_of(c, s_p if k % 2 else s_m, k)
        fx[k] = send(p, p, xm if k % 2 else xp)
        if k % 2:
            to_sib(-1, s_m, k // 2)
            to_sib(1, s_p, k // 2)

    zp = dev(zl_=1 - zl)

    def forward_part(i, s):
        if i < 3:
            pre = dot(t_buf[0, s], wu[...])
            dac = dot(t_buf[1, s], wd[...], 1, 1)
        else:
            pre = jnp.zeros((BOTH, FB), F32)
            dac = jnp.zeros((BOTH, FB), F32)
            for k in range(3):
                sibs[2, k].wait_recv()
                at = slice(2 * CW * k, 2 * CW * (k + 1))
                pre = pre + dot(t_buf[0, s, :, at], wu[at])
                dac = dac + dot(t_buf[1, s, :, at], wd[:, at], 1, 1)
        keepf[i, 0] = pre
        keepf[i, 1] = dac
        psend[i, 0] = pre.astype(BF16)
        psend[i, 1] = dac.astype(BF16)
        parts[i] = send(psend.at[i], precv.at[i], zp)

    def middle(i, s):
        parts[i].wait_recv()
        v = keepf[i, 0] + precv[i, 0].astype(F32)
        da = keepf[i, 1] + precv[i, 1].astype(F32)
        v2 = v * v
        t = jnp.tanh(A_TANH * (v + B_TANH * v * v2))
        act = 0.5 * v * (1.0 + t)
        slope = 0.5 * (1.0 + t) + 0.5 * v * (1.0 - t * t) * (A_TANH * (1.0 + 3.0 * B_TANH * v2))
        act_b[s] = act.astype(BF16)
        dpre_b[s] = (da * slope).astype(BF16)

    parts = {}

    def from_sib(i):
        for k in range(3):
            sibs[i, k].wait_recv()

    def far_pair(k):
        fx[2 * k].wait_recv()
        fx[2 * k + 1].wait_recv()
        to_sib(2, s_2, k)

    z_own(0)
    z_own(1)
    z_next(0)
    z_own(2)
    z_next(1)
    order(0)
    z_own(3)
    z_next(2)
    order(1)
    z_own(4)
    z_next(3)
    order(2)
    z_own(5)
    z_next(4)
    order(3)

    def wu_at(y_):
        return wu.at[pl.ds(pl.multiple_of(y_ * QW, QW), QW)]

    wu_r.wait_recv()
    p = wu_at(step(y, -1))
    wu_f = send(p, p, dev(y_=step(y, 1)))
    wd_l.wait_recv()
    p = col_of(wd, step(y, 1) * QW, QW)
    wd_f = send(p, p, dev(y_=step(y, -1)))

    z_next(5)
    order(4)
    order(5)
    for k in range(CHUNKS):
        pass_on(k)
    for d in (wu_l, wd_r, wu_f, wd_f):
        d.wait_recv()
    from_sib(0)
    forward_part(0, x)
    from_sib(-1)
    forward_part(1, s_m)
    from_sib(1)
    forward_part(2, s_p)
    far_pair(0)
    middle(0, x)
    far_pair(1)
    middle(1, s_m)
    far_pair(2)
    forward_part(3, s_2)
    middle(2, s_p)
    middle(3, s_2)

    dpre_t[...] = dpre_b[...].reshape(4 * BOTH, FB).astype(F32).T.astype(BF16)

    def rows_of(a, q):
        v = t_buf[a, :, :, pl.ds(pl.multiple_of(q * QW, 128), QW)]
        return v.reshape(4 * BOTH, QW)

    def up_part(q):
        return dot(dpre_t[...], rows_of(0, q))

    def down_part(q):
        return dot(act_t[...], rows_of(1, q))

    yp, ym = dev(y_=step(y, 1)), dev(y_=step(y, -1))
    q_p, q_m, q_2 = step(y, 1), step(y, -1), step(y, 2)
    ys1[0] = up_part(q_2).astype(BF16)
    y1u = send(ys1.at[0], yr1.at[0], yp)
    act_t[...] = act_b[...].reshape(4 * BOTH, FB).astype(F32).T.astype(BF16)
    ys1[1] = down_part(q_2).astype(BF16)
    y1d = send(ys1.at[1], yr1.at[1], ym)

    gx[pl.ds(x, 1)] = jnp.zeros((1, 8, WW), F32)
    cores, x1, x2, own = {}, {}, {}, {}

    def norm_wave(w):
        for cc, mine_ in ((1 - c, False), (c, True)):
            first_col = cc * (3 * WW) + w * WW
            wt = wu[pl.ds(pl.multiple_of(first_col, WW), WW), :]
            g = jnp.zeros((1, WW), F32)
            for s in range(4):
                v = dot(dpre_b[s], wt, 1, 1)
                if mine_:
                    cown[w, s] = v
                else:
                    csend[w, s] = v.astype(BF16)
                rows = t_buf[0, s, :, pl.ds(pl.multiple_of(first_col, WW), WW)]
                g = g + jnp.sum(v * rows.astype(F32), axis=0, keepdims=True)
            gx[pl.ds(x, 1), pl.ds(cc * 3 + w, 1)] = g[None]
            if not mine_:
                cores[w] = send(csend.at[w], crecv.at[w], sib)

    def summed(w, s, lo, hi):
        return cown[w, s, :, lo:hi] + crecv[w, s, :, lo:hi].astype(F32)

    def x_first(w):
        cores[w].wait_recv()
        xs1[w, 0] = summed(w, s_2, 0, 256).astype(BF16)
        a = send(xs1.at[w, 0], xr1.at[w, 0], xp)
        xs1[w, 1] = summed(w, s_2, 256, 512).astype(BF16)
        x1[w] = (a, send(xs1.at[w, 1], xr1.at[w, 1], xm))

    def x_second(w):
        xs2[w, 0, :, 256:512] = summed(w, s_p, 256, 512).astype(BF16)
        xs2[w, 1, :, 0:256] = summed(w, s_m, 0, 256).astype(BF16)
        x1[w][0].wait_recv()
        xs2[w, 0, :, 0:256] = (summed(w, s_p, 0, 256) + xr1[w, 0].astype(F32)).astype(BF16)
        a = send(xs2.at[w, 0], xr2.at[w, 0], xp)
        x1[w][1].wait_recv()
        xs2[w, 1, :, 256:512] = (summed(w, s_m, 256, 512) + xr1[w, 1].astype(F32)).astype(BF16)
        x2[w] = (a, send(xs2.at[w, 1], xr2.at[w, 1], xm))

    owners = {}

    def to_owners(w):
        for d in x2[w]:
            d.wait_recv()
        total = summed(w, x, 0, WW) + xr2[w, 0].astype(F32) + xr2[w, 1].astype(F32)
        total = total.astype(BF16)
        v = dot(own[0], total[:, 0:256]) + dot(own[1], total[:, 256:512])
        zs[w, :, :, :, :, 0:256] = v.astype(BF16).reshape(2, 4, 2, 16, 256)
        v = dot(own[2], total[:, 0:128])
        for b in range(1, 4):
            v = v + dot(own[2 + b], total[:, 128 * b:128 * (b + 1)])
        zs[w, :, :, :, :, 256:384] = v.astype(BF16).reshape(2, 4, 2, 16, 128)
        owners[w] = []
        for a, b, e in z_peers:
            zh2, zl2, c2 = step(zh, a), lax.rem(zl + b, 2), lax.rem(c + e, 2)
            owners[w].append(send(zs.at[w, zl2, zh2, c2], zr.at[w, zl, c, zh], z_peer(a, b, e)))
        zr[w, pl.ds(zl, 1), pl.ds(c, 1), pl.ds(zh, 1)] = zs[
            w, pl.ds(zl, 1), pl.ds(zh, 1), pl.ds(c, 1)
        ].reshape(1, 1, 1, 16, 384)

    for kk in range(6):
        own[kk] = oh[kk].astype(F32).T.astype(BF16)

    norm_wave(0)
    norm_wave(1)
    x_first(0)
    norm_wave(2)
    gain1 = [send(gx.at[x], gx.at[x], dev(x_=step(x, d))) for d in (1, 2, 3)]

    ys2[0, 1] = down_part(q_p).astype(BF16)
    y2pd = send(ys2.at[0, 1], yr2.at[0, 1], yp)
    x_first(1)
    ys2[1, 0] = up_part(q_m).astype(BF16)
    y2mu = send(ys2.at[1, 0], yr2.at[1, 0], ym)
    x_second(0)
    x_first(2)
    ykeep[0] = up_part(q_p)
    x_second(1)
    ykeep[1] = down_part(q_m)

    y1u.wait_recv()
    ys2[0, 0] = (ykeep[0] + yr1[0].astype(F32)).astype(BF16)
    y2pu = send(ys2.at[0, 0], yr2.at[0, 0], yp)
    y1d.wait_recv()
    ys2[1, 1] = (ykeep[1] + yr1[1].astype(F32)).astype(BF16)
    y2md = send(ys2.at[1, 1], yr2.at[1, 1], ym)

    to_owners(0)
    x_second(2)
    ykeep[0] = up_part(y)
    ykeep[1] = down_part(y)
    to_owners(1)

    for d in gain1:
        d.wait_recv()
    slot_me = zh * 2 + c
    gz[pl.ds(zl, 1), pl.ds(slot_me, 1)] = (gx[0] + gx[1] + gx[2] + gx[3])[None, None]
    gain2 = [send(gz.at[zl, slot_me], gz.at[zl, slot_me], z_peer(*p_)) for p_ in z_peers]
    to_owners(2)

    for d in gain2:
        d.wait_recv()
    for h in range(2):
        g = gz[h, 0]
        for i in range(1, 8):
            g = g + gz[h, i]
        gy[pl.ds(y, 1), h] = g[None]
    gain3 = [send(gy.at[y], gy.at[y], dev(y_=step(y, d))) for d in (1, 2, 3)]

    cols = []
    for w in range(3):
        for d in owners[w]:
            d.wait_recv()
    zero4 = iota((8, 128), 0) < 4
    for a in range(2):
        for e in range(2):
            for w in range(3):
                t = zr[w, a, e, 0].astype(F32)
                for b in range(1, 4):
                    t = t + zr[w, a, e, b].astype(F32)
                top = jnp.concatenate([t[0:8, 0:256], t[8:16, 0:256]], axis=1)
                e0, e1 = t[0:8, 256:384], t[8:16, 256:384]
                low = [e0, pltpu.roll(e0, 4, 0), e1, pltpu.roll(e1, 4, 0)]
                low = jnp.concatenate([jnp.where(zero4, v, 0.0) for v in low], axis=1)
                cols.append(jnp.concatenate([top, low], axis=0))
    d_norm = jnp.concatenate(cols, axis=1)
    h = d_norm * gain_ref[...]
    nh = nhat_s[...]
    inner = h - jnp.mean(h, axis=1, keepdims=True) - nh * jnp.mean(h * nh, axis=1, keepdims=True)
    rows_ref[...] = (dy_s[...] + rstd_s[:, 0:1] * inner).astype(BF16)

    for d in gain3:
        d.wait_recv()
    for h in range(2):
        g = gy[0, h] + gy[1, h] + gy[2, h] + gy[3, h]
        for i in range(6):
            at = slice(h * HALF + i * WW, h * HALF + (i + 1) * WW)
            gout_ref[:, at] = g[i:i + 1, :] / gain_ref[:, at]

    for d in (y2pd, y2mu, y2pu, y2md):
        d.wait_recv()
    dng_ref[...] = (ykeep[1] + yr2[0, 1].astype(F32) + yr2[1, 1].astype(F32)).astype(BF16)
    upg_ref[...] = (ykeep[0] + yr2[0, 0].astype(F32) + yr2[1, 0].astype(F32)).T.astype(BF16)

    for d in started:
        d.wait_send()


N_COPIES = 192


def kernel_call(keep, tokens, cotangent, gain, w_up, w_down):
    vmem = pl.BlockSpec(memory_space=pltpu.VMEM)
    hbm = pl.BlockSpec(memory_space=pl.ANY)

    def v(shape, dt=BF16):
        return pltpu.VMEM(shape, dt)

    scratch = [
        v((TOK, D)), v((TOK, D)),
        v((2, 2, 16, 512)), v((CHUNKS - 1, 2, 2, 16, 384)),
        v((2, 4, 2, 16, 512)), v((CHUNKS - 1, 2, 4, 2, 16, 384)),
        v((CHUNKS, BOTH, CW)), v((2, 4, BOTH, HALF)),
        v((HALF, FB)), v((FB, HALF)),
        v((4, 2, BOTH, FB), F32), v((4, 2, BOTH, FB)), v((4, 2, BOTH, FB)),
        v((FB, 4 * BOTH)), v((FB, 4 * BOTH)), v((4, BOTH, FB)), v((4, BOTH, FB)),
        v((3, 4, BOTH, WW)), v((3, 4, BOTH, WW)), v((3, 4, BOTH, WW), F32),
        v((3, 2, BOTH, 256)), v((3, 2, BOTH, 256)), v((3, 2, BOTH, WW)), v((3, 2, BOTH, WW)),
        v((3, 2, 4, 2, 16, 384)), v((3, 2, 2, 4, 16, 384)),
        v((16, D), F32), v((16, D), F32), v((16, 128), F32),
        v((2, FB, QW)), v((2, FB, QW)), v((2, 2, FB, QW)), v((2, 2, FB, QW)),
        v((2, FB, QW), F32),
        v((4, 8, WW), F32), v((2, 8, 8, WW), F32), v((4, 2, 8, WW), F32),
        pltpu.SemaphoreType.DMA((N_COPIES,)), pltpu.SemaphoreType.DMA((N_COPIES,)),
        pltpu.SemaphoreType.DMA((10,)),
    ]
    return pl.pallas_call(
        body,
        out_shape=(
            jax.ShapeDtypeStruct((16, D), BF16),
            jax.ShapeDtypeStruct((TOK, 16), BF16),
            jax.ShapeDtypeStruct((1, D), F32),
            jax.ShapeDtypeStruct((QW, FB), BF16),
            jax.ShapeDtypeStruct((FB, QW), BF16),
        ),
        in_specs=[vmem, vmem, hbm, hbm, hbm, hbm],
        out_specs=(vmem,) * 5,
        scratch_shapes=scratch,
        compiler_params=pltpu.CompilerParams(
            collective_id=0, has_side_effects=True, vmem_limit_bytes=60 * 2**20
        ),
    )(keep, gain, tokens, cotangent, w_up, w_down)


STEPS = 8


def merge_body(
    sel_ref, rows_ref, cot_ref, up_ref, down_ref, gain_ref,
    out_ref, up_out, down_out, gain_out, buf, isem, osem, rsem,
):
    h = TOK // STEPS
    ins = []
    for i in range(STEPS):
        at = pl.ds(h * i, h)
        ins.append(pltpu.make_async_copy(cot_ref.at[at], buf.at[at], isem.at[i]))
        ins[-1].start()
    waits = []
    for i, (a, b) in enumerate(((up_ref, up_out), (down_ref, down_out), (gain_ref, gain_out))):
        waits.append(pltpu.make_async_copy(a, b, rsem.at[i]))
        waits[-1].start()
    rows = rows_ref[...]
    for i in range(STEPS):
        at = slice(h * i, h * (i + 1))
        sel = sel_ref[at, :]
        kept = jnp.sum(sel.astype(F32), axis=1, keepdims=True) > 0.5
        placed = dot(sel, rows)
        ins[i].wait()
        buf[at, :] = jnp.where(kept, placed, buf[at, :].astype(F32)).astype(BF16)
        at = pl.ds(h * i, h)
        waits.append(pltpu.make_async_copy(buf.at[at], out_ref.at[at], osem.at[i]))
        waits[-1].start()
    for d in waits:
        d.wait()


def merge(sel, rows, cotangent, up, down, gain):
    vmem = pl.BlockSpec(memory_space=pltpu.VMEM)
    hbm = pl.BlockSpec(memory_space=pl.ANY)
    return pl.pallas_call(
        merge_body,
        out_shape=(
            jax.ShapeDtypeStruct((TOK, D), BF16),
            jax.ShapeDtypeStruct((QW, FB), BF16),
            jax.ShapeDtypeStruct((FB, QW), BF16),
            jax.ShapeDtypeStruct((1, D), F32),
        ),
        in_specs=[vmem, vmem, hbm, hbm, hbm, hbm],
        out_specs=(hbm,) * 4,
        scratch_shapes=[
            pltpu.VMEM((TOK, D), BF16),
            pltpu.SemaphoreType.DMA((STEPS,)),
            pltpu.SemaphoreType.DMA((STEPS,)),
            pltpu.SemaphoreType.DMA((3,)),
        ],
    )(sel, rows, cotangent, up, down, gain)


def local(tokens, gain, w_up, w_down, cotangent, keep_index):
    rows, sel, gain_grad, up, down = kernel_call(
        keep_index, tokens, cotangent, gain.reshape(1, D), w_up, w_down
    )
    input_grad, up, down, gain_grad = merge(sel, rows, cotangent, up, down, gain_grad)
    return (input_grad, gain_grad.reshape(D), up, down)


def solution(mesh):
    in_specs = (
        P(("replica", "node"), None),
        P(),
        P("replica", "node"),
        P("node", "replica"),
        P(("replica", "node"), None),
        P("replica", None),
    )
    out_specs = (P(("replica", "node"), None), P(), P("replica", "node"), P("node", "replica"))
    return jax.shard_map(local, mesh=mesh, in_specs=in_specs, out_specs=out_specs, check_vma=False)
```

```python
import functools

import jax
import jax.numpy as jnp
from jax import lax
from jax.experimental import pallas as pl
from jax.experimental.pallas import tpu as pltpu
from jax.sharding import PartitionSpec as P

CAP = 12
TOK = 256
D = 6144
HALF = 3072
QW = 768
CW = 512
CHUNKS = 6
WW = 512
FB = 384
SEQ_ROWS = 72
BOTH = 144
EPS = 1e-05
NONE = 255
F32 = jnp.float32
BF16 = jnp.bfloat16
MESH = pl.DeviceIdType.MESH

A_TANH = 0.7978845608028654
B_TANH = 0.044715


def dot(a, b, ca=1, cb=0):
    return lax.dot_general(a, b, (((ca,), (cb,)), ((), ())), preferred_element_type=F32)


def iota(shape, dim):
    return lax.broadcasted_iota(jnp.int32, shape, dim)


def body(
    keep_ref, gain_ref, tok_hbm, cot_hbm, wup_ref, wdn_ref,
    rows_ref, sel_ref, kept_ref, gout_ref, upg_ref, dng_ref,
    tok_ref, cot_ref, pk0, pkn, g0, gn, ordered, t_buf, wu, wd,
    keepf, psend, precv, act_t, dpre_t, act_b, dpre_b,
    csend, crecv, cown, xs1, xr1, xs2, xr2, zs, zr, nhat_s, dy_s, rstd_s,
    ys1, yr1, ys2, yr2, ykeep, gx, gz, gy,
    ssem, rsem, lsem,
):
    r = lax.axis_index("replica")
    n = lax.axis_index("node")
    zl, y = r // 4, lax.rem(r, 4)
    x, zh, c = n // 8, lax.rem(n // 2, 4), lax.rem(n, 2)

    def dev(x_=None, y_=None, zh_=None, zl_=None, c_=None):
        x_ = x if x_ is None else x_
        y_ = y if y_ is None else y_
        zh_ = zh if zh_ is None else zh_
        zl_ = zl if zl_ is None else zl_
        c_ = c if c_ is None else c_
        return (zl_ * 4 + y_, x_ * 8 + zh_ * 2 + c_)

    def step(v, d):
        return lax.rem(v + (d % 4), 4)

    count = [0]
    started = []

    def send(src, dst, to):
        k = count[0]
        count[0] += 1
        d = pltpu.make_async_remote_copy(
            src_ref=src, dst_ref=dst, send_sem=ssem.at[k], recv_sem=rsem.at[k],
            device_id=to, device_id_type=MESH,
        )
        d.start()
        started.append(d)
        return d

    def fetch(src, dst, k):
        d = pltpu.make_async_copy(src, dst, lsem.at[k])
        d.start()
        return d

    def col_of(ref, first, width):
        return ref.at[:, pl.ds(pl.multiple_of(first, 128), width)]

    z_peers = [(a, b, e) for a in range(4) for b in range(2) for e in range(2)][1:]

    def z_peer(a, b, e):
        return dev(zh_=step(zh, a), zl_=lax.rem(zl + b, 2), c_=lax.rem(c + e, 2))

    barrier = pltpu.get_barrier_semaphore()
    peers = [z_peer(*p) for p in z_peers]
    peers += [dev(x_=step(x, d)) for d in (1, 2, 3)]
    peers += [dev(y_=step(y, d)) for d in (1, 2, 3)]
    for p in peers:
        pl.semaphore_signal(barrier, inc=1, device_id=p, device_id_type=MESH)
    tok_in, cot_in = [], []
    for ref, to, ins, k in ((tok_hbm, tok_ref, tok_in, 2), (cot_hbm, cot_ref, cot_in, 6)):
        for i in range(4):
            at = pl.ds(64 * i, 64)
            ins.append(fetch(ref.at[at], to.at[at], k + i))
    wu_own = wu.at[pl.ds(pl.multiple_of(y * QW, QW), QW)]
    wd_own = col_of(wd, y * QW, QW)
    wu_in = fetch(wup_ref, wu_own, 0)
    wd_in = fetch(wdn_ref, wd_own, 1)

    n8 = lax.rem(n, 8)
    kv = keep_ref[pl.ds(x, 1), :]
    owner = kv // TOK
    before = jnp.sum((owner < n8).astype(F32), axis=1, keepdims=True)
    mine = jnp.sum((owner == n8).astype(F32), axis=1, keepdims=True)
    slot_col = iota((16, SEQ_ROWS), 0).astype(F32)
    j_row = iota((16, SEQ_ROWS), 1).astype(F32)
    local_pos = (kv - n8 * TOK).astype(F32)
    hit = (j_row == before + slot_col) & (slot_col < mine)
    pos = jnp.sum(jnp.where(hit, local_pos, 0.0), axis=1, keepdims=True)
    live = iota((16, TOK), 0).astype(F32) < mine
    sel = jnp.where((iota((16, TOK), 1).astype(F32) == pos) & live, 1.0, 0.0).astype(BF16)
    sel_t = sel.astype(F32).T
    sel_ref[...] = sel_t.astype(BF16)
    kept_ref[...] = jnp.sum(sel_t, axis=1, keepdims=True)

    row_i, lane_i = iota((16, 128), 0), iota((16, 128), 1)
    kind = lax.rem(row_i, 8)
    i_in = lane_i - (zh * 2 + c) * 16
    slot = jnp.where(
        kind == 0, i_in,
        jnp.where(kind == 1, i_in - 8, jnp.where(kind < 6, 8 + i_in - 4 * (kind - 2), i_in)),
    )
    is_b = (kind >= 2) & (kind < 6)
    ok = (slot >= jnp.where(is_b, 8, 0)) & (slot < jnp.where(kind < 2, 8, CAP))
    slot_f = slot.astype(F32)
    target = jnp.where(ok & (slot_f < mine), before + slot_f, float(NONE))
    here = (i_in >= 0) & (i_in < 16) & (row_i // 8 == zl)
    meta = jnp.where(here, target, 0.0).astype(BF16)

    pks = [pk0] + [pkn.at[k] for k in range(CHUNKS - 1)]
    gs = [g0] + [gn.at[k] for k in range(CHUNKS - 1)]

    def pack(rows, a):
        for h in range(2):
            for k in range(CHUNKS):
                col = h * HALF + k * CW
                blk = rows[:, col:col + CW]
                main = jnp.concatenate([blk[0:8, 0:256], blk[0:8, 256:512]], axis=0)
                t = [blk[8:16, 128 * b:128 * (b + 1)] for b in range(4)]
                extra = jnp.concatenate(
                    [t[0] + pltpu.roll(t[1], 4, 0), t[2] + pltpu.roll(t[3], 4, 0)], axis=0
                )
                pks[k][a, h, :, 0:256] = main.astype(BF16)
                pks[k][a, h, :, 256:384] = extra.astype(BF16)
            pk0[a, h, :, 384:512] = meta

    pl.semaphore_wait(barrier, len(peers))

    y_p, y_m = dev(y_=step(y, 1)), dev(y_=step(y, -1))
    wu_in.wait()
    wu_r, wu_l = send(wu_own, wu_own, y_p), send(wu_own, wu_own, y_m)
    wd_in.wait()

    def pass_w_up():
        wu_r.wait_recv()
        p = wu.at[pl.ds(pl.multiple_of(step(y, -1) * QW, QW), QW // 2)]
        a = send(p, p, y_p)
        wu_l.wait_recv()
        p = wu.at[pl.ds(pl.multiple_of(step(y, 1) * QW + QW // 2, QW // 2), QW // 2)]
        return a, send(p, p, y_m)

    def send_w_down():
        return send(wd_own, wd_own, y_p), send(wd_own, wd_own, y_m)

    def pass_w_down(own):
        own[0].wait_recv()
        p = col_of(wd, step(y, -1) * QW, QW // 2)
        a = send(p, p, y_p)
        own[1].wait_recv()
        p = col_of(wd, step(y, 1) * QW + QW // 2, QW // 2)
        return a, send(p, p, y_m)

    for d in tok_in:
        d.wait()
    xr = dot(sel, tok_ref[...])
    mean = jnp.mean(xr, axis=1, keepdims=True)
    cen = xr - mean
    rstd = lax.rsqrt(jnp.mean(cen * cen, axis=1, keepdims=True) + EPS)
    nhat = cen * rstd
    nhat_s[...] = nhat
    rstd_s[...] = jnp.broadcast_to(rstd, (16, 128))
    pack(nhat * gain_ref[...], 0)
    for d in cot_in:
        d.wait()
    dyr = dot(sel, cot_ref[...])
    dy_s[...] = dyr
    pack(dyr, 1)


    first = []
    for k in range(CHUNKS):
        group = []
        for b, e in ((0, 1), (1, 0), (1, 1)):
            zl2, c2 = lax.rem(zl + b, 2), lax.rem(c + e, 2)
            group.append(
                send(pks[k].at[c2, zl2], gs[k].at[zl, zh, c], dev(zl_=zl2, c_=c2))
            )
        first.append(group)

    for k in range(CHUNKS):
        gs[k][pl.ds(zl, 1), pl.ds(zh, 1), pl.ds(c, 1)] = pks[k][pl.ds(c, 1), pl.ds(zl, 1)][None]

    up_z, dn_z = dev(zh_=step(zh, 1)), dev(zh_=step(zh, -1))
    xp, xm, sib = dev(x_=step(x, 1)), dev(x_=step(x, -1)), dev(c_=1 - c)
    s_m, s_p, s_2 = step(x, -1), step(x, 1), step(x, 2)
    row_f = iota((BOTH, 128), 0).astype(F32)
    ring, ring2, hops = {}, {}, {}
    oh = []

    def z_own(k):
        for d in first[k]:
            d.wait_recv()
        ring[k] = (
            send(gs[k].at[:, zh], gs[k].at[:, zh], up_z),
            send(gs[k].at[:, zh], gs[k].at[:, zh], dn_z),
        )

    def z_next(k):
        ring[k][0].wait_recv()
        f0 = send(gs[k].at[:, step(zh, -1), 0], gs[k].at[:, step(zh, -1), 0], up_z)
        ring[k][1].wait_recv()
        f1 = send(gs[k].at[:, step(zh, 1), 1], gs[k].at[:, step(zh, 1), 1], dn_z)
        ring2[k] = (f0, f1)

    def one_hot(meta_sum, kk):
        return jnp.concatenate(
            [
                jnp.where(row_f == meta_sum[kk:kk + 1, :], 1.0, 0.0),
                jnp.where(row_f == meta_sum[8 + kk:9 + kk, :] + SEQ_ROWS, 1.0, 0.0),
            ],
            axis=1,
        )

    def chunk_of(a, s, k):
        return t_buf.at[a, s, :, pl.ds(k * CW, CW)]

    def order(k):
        for d in ring2[k]:
            d.wait_recv()
        if k == 0:
            ms = jnp.zeros((16, 128), F32)
            for a in range(2):
                for b in range(4):
                    for e in range(2):
                        ms = ms + g0[a, b, e, :, 384:512].astype(F32)
            oh.extend(one_hot(ms, kk).astype(BF16) for kk in range(6))
            oh.append(one_hot(ms, 6))
        ga = gs[k][:, :, :, :, 0:256].reshape(256, 256)
        gb = gs[k][:, :, :, :, 256:384].reshape(256, 128)
        for a in range(2):
            v = dot(oh[a], ga) + jnp.concatenate(
                [dot(oh[2 + 2 * a], gb), dot(oh[3 + 2 * a], gb)], axis=1
            )
            ordered[k, :, 256 * a:256 * (a + 1)] = v.astype(BF16)
        dst = chunk_of(c, x, k)
        hops[k] = (send(ordered.at[k], dst, xp), send(ordered.at[k], dst, xm))
        t_buf[pl.ds(c, 1), pl.ds(x, 1), :, CW * k:CW * (k + 1)] = ordered[k][None, None]
        if k % 2:
            to_sib(0, x, k // 2)

    sibs, fx = {}, {}

    def to_sib(i, s, pair):
        p = t_buf.at[c, s, :, pl.ds(2 * CW * pair, 2 * CW)]
        sibs[i, pair] = send(p, p, sib)

    def pass_on(k):
        hops[k][0].wait_recv()
        hops[k][1].wait_recv()
        p = chunk_of(c, s_p if k % 2 else s_m, k)
        fx[k] = send(p, p, xm if k % 2 else xp)
        if k % 2:
            to_sib(-1, s_m, k // 2)
            to_sib(1, s_p, k // 2)

    zp = dev(zl_=1 - zl)

    def give(i, j, v):
        keepf[i, j] = v
        psend[i, j] = v.astype(BF16)
        parts[i, j] = send(psend.at[i, j], precv.at[i, j], zp)

    def pre_part(i, s):
        give(i, 0, dot(t_buf[0, s], wu[...]))

    def dac_part(i, s):
        give(i, 1, dot(t_buf[1, s], wd[...], 1, 1))

    def far_parts():
        pre = jnp.zeros((BOTH, FB), F32)
        dac = jnp.zeros((BOTH, FB), F32)
        for k in range(3):
            sibs[2, k].wait_recv()
            at = slice(2 * CW * k, 2 * CW * (k + 1))
            pre = pre + dot(t_buf[0, s_2, :, at], wu[at])
            if k == 2:
                give(3, 0, pre)
            dac = dac + dot(t_buf[1, s_2, :, at], wd[:, at], 1, 1)
        give(3, 1, dac)

    def middle(i, s):
        parts[i, 0].wait_recv()
        parts[i, 1].wait_recv()
        v = keepf[i, 0] + precv[i, 0].astype(F32)
        da = keepf[i, 1] + precv[i, 1].astype(F32)
        v2 = v * v
        t = jnp.tanh(A_TANH * (v + B_TANH * v * v2))
        act = 0.5 * v * (1.0 + t)
        slope = 0.5 * (1.0 + t) + 0.5 * v * (1.0 - t * t) * (A_TANH * (1.0 + 3.0 * B_TANH * v2))
        act_b[s] = act.astype(BF16)
        dpre_b[s] = (da * slope).astype(BF16)

    parts = {}

    def from_sib(i):
        for k in range(3):
            sibs[i, k].wait_recv()

    def far_pair(k):
        fx[2 * k].wait_recv()
        fx[2 * k + 1].wait_recv()
        to_sib(2, s_2, k)

    z_own(0)
    z_own(1)
    z_next(0)
    z_own(2)
    z_next(1)
    wu_far = pass_w_up()
    wd_near = send_w_down()
    order(0)
    z_own(3)
    z_next(2)
    order(1)
    z_own(4)
    z_next(3)
    order(2)
    z_own(5)
    z_next(4)
    order(3)

    z_next(5)
    order(4)
    order(5)
    pass_on(0)
    pass_on(1)
    for d in wu_far:
        d.wait_recv()
    from_sib(0)
    pre_part(0, x)
    pass_on(2)
    pass_on(3)
    wd_far = pass_w_down(wd_near)
    pass_on(4)
    pass_on(5)
    from_sib(-1)
    pre_part(1, s_m)
    from_sib(1)
    pre_part(2, s_p)
    for d in wd_far:
        d.wait_recv()
    dac_part(0, x)
    dac_part(1, s_m)
    dac_part(2, s_p)
    far_pair(0)
    far_pair(1)
    middle(0, x)
    far_pair(2)
    middle(1, s_m)
    far_parts()
    middle(2, s_p)
    middle(3, s_2)

    dpre_t[...] = dpre_b[...].reshape(4 * BOTH, FB).astype(F32).T.astype(BF16)

    def rows_of(a, q):
        v = t_buf[a, :, :, pl.ds(pl.multiple_of(q * QW, 128), QW)]
        return v.reshape(4 * BOTH, QW)

    def up_part(q):
        return dot(dpre_t[...], rows_of(0, q))

    def down_part(q):
        return dot(act_t[...], rows_of(1, q))

    yp, ym = y_p, y_m
    q_p, q_m, q_2 = step(y, 1), step(y, -1), step(y, 2)
    ys1[0] = up_part(q_2).astype(BF16)
    y1u = send(ys1.at[0], yr1.at[0], yp)
    act_t[...] = act_b[...].reshape(4 * BOTH, FB).astype(F32).T.astype(BF16)
    ys1[1] = down_part(q_2).astype(BF16)
    y1d = send(ys1.at[1], yr1.at[1], ym)

    gx[pl.ds(x, 1)] = jnp.zeros((1, 8, WW), F32)
    cores, x1, x2, own = {}, {}, {}, {}

    def norm_wave(w):
        for cc, mine_ in ((1 - c, False), (c, True)):
            first_col = cc * (3 * WW) + w * WW
            wt = wu[pl.ds(pl.multiple_of(first_col, WW), WW), :]
            g = jnp.zeros((1, WW), F32)
            for s in range(4):
                v = dot(dpre_b[s], wt, 1, 1)
                if mine_:
                    cown[w, s] = v
                else:
                    csend[w, s] = v.astype(BF16)
                rows = t_buf[0, s, :, pl.ds(pl.multiple_of(first_col, WW), WW)]
                g = g + jnp.sum(v * rows.astype(F32), axis=0, keepdims=True)
            gx[pl.ds(x, 1), pl.ds(cc * 3 + w, 1)] = g[None]
            if not mine_:
                cores[w] = send(csend.at[w], crecv.at[w], sib)

    def summed(w, s, lo, hi):
        return cown[w, s, :, lo:hi] + crecv[w, s, :, lo:hi].astype(F32)

    def x_first(w):
        cores[w].wait_recv()
        xs1[w, 0] = summed(w, s_2, 0, 256).astype(BF16)
        a = send(xs1.at[w, 0], xr1.at[w, 0], xp)
        xs1[w, 1] = summed(w, s_2, 256, 512).astype(BF16)
        x1[w] = (a, send(xs1.at[w, 1], xr1.at[w, 1], xm))

    def x_second(w):
        xs2[w, 0, :, 256:512] = summed(w, s_p, 256, 512).astype(BF16)
        xs2[w, 1, :, 0:256] = summed(w, s_m, 0, 256).astype(BF16)
        x1[w][0].wait_recv()
        xs2[w, 0, :, 0:256] = (summed(w, s_p, 0, 256) + xr1[w, 0].astype(F32)).astype(BF16)
        a = send(xs2.at[w, 0], xr2.at[w, 0], xp)
        x1[w][1].wait_recv()
        xs2[w, 1, :, 256:512] = (summed(w, s_m, 256, 512) + xr1[w, 1].astype(F32)).astype(BF16)
        x2[w] = (a, send(xs2.at[w, 1], xr2.at[w, 1], xm))

    owners = {}

    def to_owners(w):
        for d in x2[w]:
            d.wait_recv()
        total = summed(w, x, 0, WW) + xr2[w, 0].astype(F32) + xr2[w, 1].astype(F32)
        total = total.astype(BF16)
        v = dot(own[0], total[:, 0:256]) + dot(own[1], total[:, 256:512])
        zs[w, :, :, :, :, 0:256] = v.astype(BF16).reshape(2, 4, 2, 16, 256)
        v = dot(own[2], total[:, 0:128])
        for b in range(1, 4):
            v = v + dot(own[2 + b], total[:, 128 * b:128 * (b + 1)])
        zs[w, :, :, :, :, 256:384] = v.astype(BF16).reshape(2, 4, 2, 16, 128)
        owners[w] = []
        for a, b, e in z_peers:
            zh2, zl2, c2 = step(zh, a), lax.rem(zl + b, 2), lax.rem(c + e, 2)
            owners[w].append(send(zs.at[w, zl2, zh2, c2], zr.at[w, zl, c, zh], z_peer(a, b, e)))
        zr[w, pl.ds(zl, 1), pl.ds(c, 1), pl.ds(zh, 1)] = zs[
            w, pl.ds(zl, 1), pl.ds(zh, 1), pl.ds(c, 1)
        ].reshape(1, 1, 1, 16, 384)

    for kk in range(6):
        own[kk] = oh[kk].astype(F32).T.astype(BF16)

    norm_wave(0)
    norm_wave(1)
    x_first(0)
    norm_wave(2)
    gain1 = [send(gx.at[x], gx.at[x], dev(x_=step(x, d))) for d in (1, 2, 3)]

    ys2[0, 1] = down_part(q_p).astype(BF16)
    y2pd = send(ys2.at[0, 1], yr2.at[0, 1], yp)
    x_first(1)
    ys2[1, 0] = up_part(q_m).astype(BF16)
    y2mu = send(ys2.at[1, 0], yr2.at[1, 0], ym)
    x_second(0)
    x_first(2)
    ykeep[0] = up_part(q_p)
    x_second(1)
    ykeep[1] = down_part(q_m)

    y1u.wait_recv()
    ys2[0, 0] = (ykeep[0] + yr1[0].astype(F32)).astype(BF16)
    y2pu = send(ys2.at[0, 0], yr2.at[0, 0], yp)
    y1d.wait_recv()
    ys2[1, 1] = (ykeep[1] + yr1[1].astype(F32)).astype(BF16)
    y2md = send(ys2.at[1, 1], yr2.at[1, 1], ym)

    to_owners(0)
    x_second(2)
    ykeep[0] = up_part(y)
    ykeep[1] = down_part(y)
    to_owners(1)

    for d in gain1:
        d.wait_recv()
    slot_me = zh * 2 + c
    gz[pl.ds(zl, 1), pl.ds(slot_me, 1)] = (gx[0] + gx[1] + gx[2] + gx[3])[None, None]
    gain2 = [send(gz.at[zl, slot_me], gz.at[zl, slot_me], z_peer(*p_)) for p_ in z_peers]
    to_owners(2)

    for d in gain2:
        d.wait_recv()
    for h in range(2):
        g = gz[h, 0]
        for i in range(1, 8):
            g = g + gz[h, i]
        gy[pl.ds(y, 1), h] = g[None]
    gain3 = [send(gy.at[y], gy.at[y], dev(y_=step(y, d))) for d in (1, 2, 3)]

    cols = []
    for w in range(3):
        for d in owners[w]:
            d.wait_recv()
    zero4 = iota((8, 128), 0) < 4
    for a in range(2):
        for e in range(2):
            for w in range(3):
                t = zr[w, a, e, 0].astype(F32)
                for b in range(1, 4):
                    t = t + zr[w, a, e, b].astype(F32)
                top = jnp.concatenate([t[0:8, 0:256], t[8:16, 0:256]], axis=1)
                e0, e1 = t[0:8, 256:384], t[8:16, 256:384]
                low = [e0, pltpu.roll(e0, 4, 0), e1, pltpu.roll(e1, 4, 0)]
                low = jnp.concatenate([jnp.where(zero4, v, 0.0) for v in low], axis=1)
                cols.append(jnp.concatenate([top, low], axis=0))
    d_norm = jnp.concatenate(cols, axis=1)
    h = d_norm * gain_ref[...]
    nh = nhat_s[...]
    inner = h - jnp.mean(h, axis=1, keepdims=True) - nh * jnp.mean(h * nh, axis=1, keepdims=True)
    rows_ref[...] = (dy_s[...] + rstd_s[:, 0:1] * inner).astype(BF16)

    for d in gain3:
        d.wait_recv()
    for h in range(2):
        g = gy[0, h] + gy[1, h] + gy[2, h] + gy[3, h]
        for i in range(6):
            at = slice(h * HALF + i * WW, h * HALF + (i + 1) * WW)
            gout_ref[:, at] = g[i:i + 1, :] / gain_ref[:, at]

    for d in (y2pd, y2mu, y2pu, y2md):
        d.wait_recv()
    dng_ref[...] = (ykeep[1] + yr2[0, 1].astype(F32) + yr2[1, 1].astype(F32)).astype(BF16)
    upg_ref[...] = (ykeep[0] + yr2[0, 0].astype(F32) + yr2[1, 0].astype(F32)).T.astype(BF16)

    for d in started:
        d.wait_send()


N_COPIES = 192


def kernel_call(keep, tokens, cotangent, gain, w_up, w_down):
    vmem = pl.BlockSpec(memory_space=pltpu.VMEM)
    hbm = pl.BlockSpec(memory_space=pl.ANY)

    def v(shape, dt=BF16):
        return pltpu.VMEM(shape, dt)

    scratch = [
        v((TOK, D)), v((TOK, D)),
        v((2, 2, 16, 512)), v((CHUNKS - 1, 2, 2, 16, 384)),
        v((2, 4, 2, 16, 512)), v((CHUNKS - 1, 2, 4, 2, 16, 384)),
        v((CHUNKS, BOTH, CW)), v((2, 4, BOTH, HALF)),
        v((HALF, FB)), v((FB, HALF)),
        v((4, 2, BOTH, FB), F32), v((4, 2, BOTH, FB)), v((4, 2, BOTH, FB)),
        v((FB, 4 * BOTH)), v((FB, 4 * BOTH)), v((4, BOTH, FB)), v((4, BOTH, FB)),
        v((3, 4, BOTH, WW)), v((3, 4, BOTH, WW)), v((3, 4, BOTH, WW), F32),
        v((3, 2, BOTH, 256)), v((3, 2, BOTH, 256)), v((3, 2, BOTH, WW)), v((3, 2, BOTH, WW)),
        v((3, 2, 4, 2, 16, 384)), v((3, 2, 2, 4, 16, 384)),
        v((16, D), F32), v((16, D), F32), v((16, 128), F32),
        v((2, FB, QW)), v((2, FB, QW)), v((2, 2, FB, QW)), v((2, 2, FB, QW)),
        v((2, FB, QW), F32),
        v((4, 8, WW), F32), v((2, 8, 8, WW), F32), v((4, 2, 8, WW), F32),
        pltpu.SemaphoreType.DMA((N_COPIES,)), pltpu.SemaphoreType.DMA((N_COPIES,)),
        pltpu.SemaphoreType.DMA((10,)),
    ]
    return pl.pallas_call(
        body,
        out_shape=(
            jax.ShapeDtypeStruct((16, D), BF16),
            jax.ShapeDtypeStruct((TOK, 16), BF16),
            jax.ShapeDtypeStruct((TOK, 1), F32),
            jax.ShapeDtypeStruct((1, D), F32),
            jax.ShapeDtypeStruct((QW, FB), BF16),
            jax.ShapeDtypeStruct((FB, QW), BF16),
        ),
        in_specs=[vmem, vmem, hbm, hbm, hbm, hbm],
        out_specs=(vmem,) * 6,
        scratch_shapes=scratch,
        compiler_params=pltpu.CompilerParams(
            collective_id=0, has_side_effects=True, vmem_limit_bytes=60 * 2**20
        ),
    )(keep, gain, tokens, cotangent, w_up, w_down)


def local(tokens, gain, w_up, w_down, cotangent, keep_index):
    rows, sel, kept, gain_grad, up, down = kernel_call(
        keep_index, tokens, cotangent, gain.reshape(1, D), w_up, w_down
    )
    input_grad = jnp.where(kept > 0.5, dot(sel, rows).astype(BF16), cotangent)
    return (input_grad, gain_grad.reshape(D), up, down)


def solution(mesh):
    in_specs = (
        P(("replica", "node"), None),
        P(),
        P("replica", "node"),
        P("node", "replica"),
        P(("replica", "node"), None),
        P("replica", None),
    )
    out_specs = (P(("replica", "node"), None), P(), P("replica", "node"), P("node", "replica"))
    return jax.shard_map(local, mesh=mesh, in_specs=in_specs, out_specs=out_specs, check_vma=False)
```

```python
import functools

import jax
import jax.numpy as jnp
from jax import lax
from jax.experimental import pallas as pl
from jax.experimental.pallas import tpu as pltpu
from jax.sharding import PartitionSpec as P

CAP = 12
TOK = 256
D = 6144
HALF = 3072
QW = 768
CW = 512
CHUNKS = 6
WW = 512
FB = 384
SEQ_ROWS = 72
BOTH = 144
EPS = 1e-05
NONE = 255
F32 = jnp.float32
BF16 = jnp.bfloat16
MESH = pl.DeviceIdType.MESH

A_TANH = 0.7978845608028654
B_TANH = 0.044715


def dot(a, b, ca=1, cb=0):
    return lax.dot_general(a, b, (((ca,), (cb,)), ((), ())), preferred_element_type=F32)


def iota(shape, dim):
    return lax.broadcasted_iota(jnp.int32, shape, dim)


def body(
    keep_ref, gain_ref, tok_hbm, cot_hbm, wup_ref, wdn_ref,
    rows_ref, sel_ref, gout_ref, upg_ref, dng_ref,
    tok_ref, cot_ref, pk0, pkn, g0, gn, ordered, t_buf, wu, wd,
    keepf, psend, precv, act_t, dpre_t, act_b, dpre_b,
    csend, crecv, cown, xs1, xr1, xs2, xr2, zs, zr, nhat_s, rstd_s,
    ys1, yr1, ys2, yr2, ykeep, gx, gz, gy,
    ssem, rsem, lsem,
):
    r = lax.axis_index("replica")
    n = lax.axis_index("node")
    zl, y = r // 4, lax.rem(r, 4)
    x, zh, c = n // 8, lax.rem(n // 2, 4), lax.rem(n, 2)

    def dev(x_=None, y_=None, zh_=None, zl_=None, c_=None):
        x_ = x if x_ is None else x_
        y_ = y if y_ is None else y_
        zh_ = zh if zh_ is None else zh_
        zl_ = zl if zl_ is None else zl_
        c_ = c if c_ is None else c_
        return (zl_ * 4 + y_, x_ * 8 + zh_ * 2 + c_)

    def step(v, d):
        return lax.rem(v + (d % 4), 4)

    count = [0]
    started = []

    def send(src, dst, to):
        k = count[0]
        count[0] += 1
        d = pltpu.make_async_remote_copy(
            src_ref=src, dst_ref=dst, send_sem=ssem.at[k], recv_sem=rsem.at[k],
            device_id=to, device_id_type=MESH,
        )
        d.start()
        started.append(d)
        return d

    def fetch(src, dst, k):
        d = pltpu.make_async_copy(src, dst, lsem.at[k])
        d.start()
        return d

    def col_of(ref, first, width):
        return ref.at[:, pl.ds(pl.multiple_of(first, 128), width)]

    z_peers = [(a, b, e) for a in range(4) for b in range(2) for e in range(2)][1:]

    def z_peer(a, b, e):
        return dev(zh_=step(zh, a), zl_=lax.rem(zl + b, 2), c_=lax.rem(c + e, 2))

    barrier = pltpu.get_barrier_semaphore()
    peers = [z_peer(*p) for p in z_peers]
    peers += [dev(x_=step(x, d)) for d in (1, 2, 3)]
    peers += [dev(y_=step(y, d)) for d in (1, 2, 3)]
    for p in peers:
        pl.semaphore_signal(barrier, inc=1, device_id=p, device_id_type=MESH)
    tok_in, cot_in = [], []
    for ref, to, ins, k in ((tok_hbm, tok_ref, tok_in, 2), (cot_hbm, cot_ref, cot_in, 6)):
        for i in range(4):
            at = pl.ds(64 * i, 64)
            ins.append(fetch(ref.at[at], to.at[at], k + i))
    wu_own = wu.at[pl.ds(pl.multiple_of(y * QW, QW), QW)]
    wd_own = col_of(wd, y * QW, QW)
    wu_in = fetch(wup_ref, wu_own, 0)
    wd_in = fetch(wdn_ref, wd_own, 1)

    n8 = lax.rem(n, 8)
    kv = keep_ref[pl.ds(x, 1), :]
    owner = kv // TOK
    before = jnp.sum((owner < n8).astype(F32), axis=1, keepdims=True)
    mine = jnp.sum((owner == n8).astype(F32), axis=1, keepdims=True)
    slot_col = iota((16, SEQ_ROWS), 0).astype(F32)
    j_row = iota((16, SEQ_ROWS), 1).astype(F32)
    local_pos = (kv - n8 * TOK).astype(F32)
    hit = (j_row == before + slot_col) & (slot_col < mine)
    pos = jnp.sum(jnp.where(hit, local_pos, 0.0), axis=1, keepdims=True)
    live = iota((16, TOK), 0).astype(F32) < mine
    sel = jnp.where((iota((16, TOK), 1).astype(F32) == pos) & live, 1.0, 0.0).astype(BF16)
    sel_f = sel.astype(F32)
    sel_ref[...] = jnp.concatenate([sel_f, sel_f], axis=0).T.astype(BF16)

    row_i, lane_i = iota((16, 128), 0), iota((16, 128), 1)
    kind = lax.rem(row_i, 8)
    i_in = lane_i - (zh * 2 + c) * 16
    slot = jnp.where(
        kind == 0, i_in,
        jnp.where(kind == 1, i_in - 8, jnp.where(kind < 6, 8 + i_in - 4 * (kind - 2), i_in)),
    )
    is_b = (kind >= 2) & (kind < 6)
    ok = (slot >= jnp.where(is_b, 8, 0)) & (slot < jnp.where(kind < 2, 8, CAP))
    slot_f = slot.astype(F32)
    target = jnp.where(ok & (slot_f < mine), before + slot_f, float(NONE))
    here = (i_in >= 0) & (i_in < 16) & (row_i // 8 == zl)
    meta = jnp.where(here, target, 0.0).astype(BF16)

    pks = [pk0] + [pkn.at[k] for k in range(CHUNKS - 1)]
    gs = [g0] + [gn.at[k] for k in range(CHUNKS - 1)]

    def pack(rows, a):
        for h in range(2):
            for k in range(CHUNKS):
                col = h * HALF + k * CW
                blk = rows[:, col:col + CW]
                main = jnp.concatenate([blk[0:8, 0:256], blk[0:8, 256:512]], axis=0)
                t = [blk[8:16, 128 * b:128 * (b + 1)] for b in range(4)]
                extra = jnp.concatenate(
                    [t[0] + pltpu.roll(t[1], 4, 0), t[2] + pltpu.roll(t[3], 4, 0)], axis=0
                )
                pks[k][a, h, :, 0:256] = main.astype(BF16)
                pks[k][a, h, :, 256:384] = extra.astype(BF16)
            pk0[a, h, :, 384:512] = meta

    pl.semaphore_wait(barrier, len(peers))

    y_p, y_m = dev(y_=step(y, 1)), dev(y_=step(y, -1))
    wu_in.wait()
    wu_r, wu_l = send(wu_own, wu_own, y_p), send(wu_own, wu_own, y_m)
    wd_in.wait()

    def pass_w_up():
        wu_r.wait_recv()
        p = wu.at[pl.ds(pl.multiple_of(step(y, -1) * QW, QW), QW // 2)]
        a = send(p, p, y_p)
        wu_l.wait_recv()
        p = wu.at[pl.ds(pl.multiple_of(step(y, 1) * QW + QW // 2, QW // 2), QW // 2)]
        return a, send(p, p, y_m)

    def send_w_down():
        return send(wd_own, wd_own, y_p), send(wd_own, wd_own, y_m)

    def pass_w_down(own):
        own[0].wait_recv()
        p = col_of(wd, step(y, -1) * QW, QW // 2)
        a = send(p, p, y_p)
        own[1].wait_recv()
        p = col_of(wd, step(y, 1) * QW + QW // 2, QW // 2)
        return a, send(p, p, y_m)

    for d in tok_in:
        d.wait()
    xr = dot(sel, tok_ref[...])
    mean = jnp.mean(xr, axis=1, keepdims=True)
    cen = xr - mean
    rstd = lax.rsqrt(jnp.mean(cen * cen, axis=1, keepdims=True) + EPS)
    nhat = cen * rstd
    nhat_s[...] = nhat
    rstd_s[...] = jnp.broadcast_to(rstd, (16, 128))
    pack(nhat * gain_ref[...], 0)
    for d in cot_in:
        d.wait()
    pack(dot(sel, cot_ref[...]), 1)


    for k in range(CHUNKS):
        gs[k][pl.ds(zl, 1), pl.ds(zh, 1), pl.ds(c, 1)] = pks[k][pl.ds(c, 1), pl.ds(zl, 1)][None]

    up_z, dn_z = dev(zh_=step(zh, 1)), dev(zh_=step(zh, -1))
    xp, xm, sib = dev(x_=step(x, 1)), dev(x_=step(x, -1)), dev(c_=1 - c)
    s_m, s_p, s_2 = step(x, -1), step(x, 1), step(x, 2)
    row_f = iota((BOTH, 128), 0).astype(F32)
    ring, ring2, hops = {}, {}, {}
    oh = []

    def z_own(k):
        for dz in (1, 3, 0):
            ring[k, dz] = []
            for b, e in ((0, 1), (1, 0), (1, 1), (0, 0)):
                if dz or b or e:
                    zl2, c2 = lax.rem(zl + b, 2), lax.rem(c + e, 2)
                    ring[k, dz].append(
                        send(pks[k].at[c2, zl2], gs[k].at[zl, zh, c], z_peer(dz, b, e))
                    )

    def z_next(k):
        for d in ring[k, 1]:
            d.wait_recv()
        f0 = send(gs[k].at[:, step(zh, -1), 0], gs[k].at[:, step(zh, -1), 0], up_z)
        for d in ring[k, 3]:
            d.wait_recv()
        f1 = send(gs[k].at[:, step(zh, 1), 1], gs[k].at[:, step(zh, 1), 1], dn_z)
        ring2[k] = (f0, f1)

    def one_hot(meta_sum, kk):
        return jnp.concatenate(
            [
                jnp.where(row_f == meta_sum[kk:kk + 1, :], 1.0, 0.0),
                jnp.where(row_f == meta_sum[8 + kk:9 + kk, :] + SEQ_ROWS, 1.0, 0.0),
            ],
            axis=1,
        )

    def chunk_of(a, s, k):
        return t_buf.at[a, s, :, pl.ds(k * CW, CW)]

    def order(k):
        for d in ring[k, 0]:
            d.wait_recv()
        for d in ring2[k]:
            d.wait_recv()
        if k == 0:
            ms = jnp.zeros((16, 128), F32)
            for a in range(2):
                for b in range(4):
                    for e in range(2):
                        ms = ms + g0[a, b, e, :, 384:512].astype(F32)
            oh.extend(one_hot(ms, kk).astype(BF16) for kk in range(6))
            oh.append(one_hot(ms, 6))
        ga = gs[k][:, :, :, :, 0:256].reshape(256, 256)
        gb = gs[k][:, :, :, :, 256:384].reshape(256, 128)
        for a in range(2):
            v = dot(oh[a], ga) + jnp.concatenate(
                [dot(oh[2 + 2 * a], gb), dot(oh[3 + 2 * a], gb)], axis=1
            )
            ordered[k, :, 256 * a:256 * (a + 1)] = v.astype(BF16)
        dst = chunk_of(c, x, k)
        hops[k] = (send(ordered.at[k], dst, xp), send(ordered.at[k], dst, xm))
        t_buf[pl.ds(c, 1), pl.ds(x, 1), :, CW * k:CW * (k + 1)] = ordered[k][None, None]
        if k % 2:
            to_sib(0, x, k // 2)

    sibs, fx = {}, {}

    def to_sib(i, s, pair):
        p = t_buf.at[c, s, :, pl.ds(2 * CW * pair, 2 * CW)]
        sibs[i, pair] = send(p, p, sib)

    def pass_on(k):
        hops[k][0].wait_recv()
        hops[k][1].wait_recv()
        p = chunk_of(c, s_p if k % 2 else s_m, k)
        fx[k] = send(p, p, xm if k % 2 else xp)
        if k % 2:
            to_sib(-1, s_m, k // 2)
            to_sib(1, s_p, k // 2)

    zp = dev(zl_=1 - zl)

    def give(i, j, v):
        keepf[i, j] = v
        psend[i, j] = v.astype(BF16)
        parts[i, j] = send(psend.at[i, j], precv.at[i, j], zp)

    def pre_part(i, s):
        give(i, 0, dot(t_buf[0, s], wu[...]))

    def dac_part(i, s):
        give(i, 1, dot(t_buf[1, s], wd[...], 1, 1))

    def far_parts():
        pre = jnp.zeros((BOTH, FB), F32)
        dac = jnp.zeros((BOTH, FB), F32)
        for k in range(3):
            sibs[2, k].wait_recv()
            at = slice(2 * CW * k, 2 * CW * (k + 1))
            pre = pre + dot(t_buf[0, s_2, :, at], wu[at])
            if k == 2:
                give(3, 0, pre)
            dac = dac + dot(t_buf[1, s_2, :, at], wd[:, at], 1, 1)
        give(3, 1, dac)

    def middle(i, s):
        parts[i, 0].wait_recv()
        parts[i, 1].wait_recv()
        v = keepf[i, 0] + precv[i, 0].astype(F32)
        da = keepf[i, 1] + precv[i, 1].astype(F32)
        v2 = v * v
        t = jnp.tanh(A_TANH * (v + B_TANH * v * v2))
        act = 0.5 * v * (1.0 + t)
        slope = 0.5 * (1.0 + t) + 0.5 * v * (1.0 - t * t) * (A_TANH * (1.0 + 3.0 * B_TANH * v2))
        act_b[s] = act.astype(BF16)
        dpre_b[s] = (da * slope).astype(BF16)

    parts = {}

    def from_sib(i):
        for k in range(3):
            sibs[i, k].wait_recv()

    def far_pair(k):
        fx[2 * k].wait_recv()
        fx[2 * k + 1].wait_recv()
        to_sib(2, s_2, k)

    z_own(0)
    z_own(1)
    z_next(0)
    z_own(2)
    z_next(1)
    wu_far = pass_w_up()
    wd_near = send_w_down()
    order(0)
    z_own(3)
    z_next(2)
    order(1)
    z_own(4)
    z_next(3)
    order(2)
    z_own(5)
    z_next(4)
    order(3)

    z_next(5)
    order(4)
    order(5)
    pass_on(0)
    pass_on(1)
    for d in wu_far:
        d.wait_recv()
    from_sib(0)
    pre_part(0, x)
    pass_on(2)
    pass_on(3)
    wd_far = pass_w_down(wd_near)
    pass_on(4)
    pass_on(5)
    from_sib(-1)
    pre_part(1, s_m)
    from_sib(1)
    pre_part(2, s_p)
    for d in wd_far:
        d.wait_recv()
    dac_part(0, x)
    dac_part(1, s_m)
    dac_part(2, s_p)
    far_pair(0)
    far_pair(1)
    middle(0, x)
    far_pair(2)
    middle(1, s_m)
    far_parts()
    middle(2, s_p)
    middle(3, s_2)

    dpre_t[...] = dpre_b[...].reshape(4 * BOTH, FB).astype(F32).T.astype(BF16)

    def rows_of(a, q):
        v = t_buf[a, :, :, pl.ds(pl.multiple_of(q * QW, 128), QW)]
        return v.reshape(4 * BOTH, QW)

    def up_part(q):
        return dot(dpre_t[...], rows_of(0, q))

    def down_part(q):
        return dot(act_t[...], rows_of(1, q))

    yp, ym = y_p, y_m
    q_p, q_m, q_2 = step(y, 1), step(y, -1), step(y, 2)
    ys1[0] = up_part(q_2).astype(BF16)
    y1u = send(ys1.at[0], yr1.at[0], yp)
    act_t[...] = act_b[...].reshape(4 * BOTH, FB).astype(F32).T.astype(BF16)
    ys1[1] = down_part(q_2).astype(BF16)
    y1d = send(ys1.at[1], yr1.at[1], ym)

    gx[pl.ds(x, 1)] = jnp.zeros((1, 8, WW), F32)
    cores, x1, x2, own = {}, {}, {}, {}

    def norm_wave(w):
        for cc, mine_ in ((1 - c, False), (c, True)):
            first_col = cc * (3 * WW) + w * WW
            wt = wu[pl.ds(pl.multiple_of(first_col, WW), WW), :]
            g = jnp.zeros((1, WW), F32)
            for s in range(4):
                v = dot(dpre_b[s], wt, 1, 1)
                if mine_:
                    cown[w, s] = v
                else:
                    csend[w, s] = v.astype(BF16)
                rows = t_buf[0, s, :, pl.ds(pl.multiple_of(first_col, WW), WW)]
                g = g + jnp.sum(v * rows.astype(F32), axis=0, keepdims=True)
            gx[pl.ds(x, 1), pl.ds(cc * 3 + w, 1)] = g[None]
            if not mine_:
                cores[w] = send(csend.at[w], crecv.at[w], sib)

    def summed(w, s, lo, hi):
        return cown[w, s, :, lo:hi] + crecv[w, s, :, lo:hi].astype(F32)

    def x_first(w):
        cores[w].wait_recv()
        xs1[w, 0] = summed(w, s_2, 0, 256).astype(BF16)
        a = send(xs1.at[w, 0], xr1.at[w, 0], xp)
        xs1[w, 1] = summed(w, s_2, 256, 512).astype(BF16)
        x1[w] = (a, send(xs1.at[w, 1], xr1.at[w, 1], xm))

    def x_second(w):
        xs2[w, 0, :, 256:512] = summed(w, s_p, 256, 512).astype(BF16)
        xs2[w, 1, :, 0:256] = summed(w, s_m, 0, 256).astype(BF16)
        x1[w][0].wait_recv()
        xs2[w, 0, :, 0:256] = (summed(w, s_p, 0, 256) + xr1[w, 0].astype(F32)).astype(BF16)
        a = send(xs2.at[w, 0], xr2.at[w, 0], xp)
        x1[w][1].wait_recv()
        xs2[w, 1, :, 256:512] = (summed(w, s_m, 256, 512) + xr1[w, 1].astype(F32)).astype(BF16)
        x2[w] = (a, send(xs2.at[w, 1], xr2.at[w, 1], xm))

    owners = {}

    def to_owners(w):
        for d in x2[w]:
            d.wait_recv()
        total = summed(w, x, 0, WW) + xr2[w, 0].astype(F32) + xr2[w, 1].astype(F32)
        total = total.astype(BF16)
        v = dot(own[0], total[:, 0:256]) + dot(own[1], total[:, 256:512])
        zs[w, :, :, :, :, 0:256] = v.astype(BF16).reshape(2, 4, 2, 16, 256)
        v = dot(own[2], total[:, 0:128])
        for b in range(1, 4):
            v = v + dot(own[2 + b], total[:, 128 * b:128 * (b + 1)])
        zs[w, :, :, :, :, 256:384] = v.astype(BF16).reshape(2, 4, 2, 16, 128)
        owners[w] = []
        for a, b, e in z_peers:
            zh2, zl2, c2 = step(zh, a), lax.rem(zl + b, 2), lax.rem(c + e, 2)
            owners[w].append(send(zs.at[w, zl2, zh2, c2], zr.at[w, zl, c, zh], z_peer(a, b, e)))
        zr[w, pl.ds(zl, 1), pl.ds(c, 1), pl.ds(zh, 1)] = zs[
            w, pl.ds(zl, 1), pl.ds(zh, 1), pl.ds(c, 1)
        ].reshape(1, 1, 1, 16, 384)

    for kk in range(6):
        own[kk] = oh[kk].astype(F32).T.astype(BF16)

    norm_wave(0)
    norm_wave(1)
    x_first(0)
    norm_wave(2)
    gain1 = [send(gx.at[x], gx.at[x], dev(x_=step(x, d))) for d in (1, 2, 3)]

    ys2[0, 1] = down_part(q_p).astype(BF16)
    y2pd = send(ys2.at[0, 1], yr2.at[0, 1], yp)
    x_first(1)
    ys2[1, 0] = up_part(q_m).astype(BF16)
    y2mu = send(ys2.at[1, 0], yr2.at[1, 0], ym)
    x_second(0)
    x_first(2)
    ykeep[0] = up_part(q_p)
    x_second(1)
    ykeep[1] = down_part(q_m)

    y1u.wait_recv()
    ys2[0, 0] = (ykeep[0] + yr1[0].astype(F32)).astype(BF16)
    y2pu = send(ys2.at[0, 0], yr2.at[0, 0], yp)
    y1d.wait_recv()
    ys2[1, 1] = (ykeep[1] + yr1[1].astype(F32)).astype(BF16)
    y2md = send(ys2.at[1, 1], yr2.at[1, 1], ym)

    to_owners(0)
    x_second(2)
    ykeep[0] = up_part(y)
    ykeep[1] = down_part(y)
    to_owners(1)

    for d in gain1:
        d.wait_recv()
    slot_me = zh * 2 + c
    gz[pl.ds(zl, 1), pl.ds(slot_me, 1)] = (gx[0] + gx[1] + gx[2] + gx[3])[None, None]
    gain2 = [send(gz.at[zl, slot_me], gz.at[zl, slot_me], z_peer(*p_)) for p_ in z_peers]
    to_owners(2)

    for d in gain2:
        d.wait_recv()
    for h in range(2):
        g = gz[h, 0]
        for i in range(1, 8):
            g = g + gz[h, i]
        gy[pl.ds(y, 1), h] = g[None]
    gain3 = [send(gy.at[y], gy.at[y], dev(y_=step(y, d))) for d in (1, 2, 3)]

    cols = []
    for w in range(3):
        for d in owners[w]:
            d.wait_recv()
    zero4 = iota((8, 128), 0) < 4
    for a in range(2):
        for e in range(2):
            for w in range(3):
                t = zr[w, a, e, 0].astype(F32)
                for b in range(1, 4):
                    t = t + zr[w, a, e, b].astype(F32)
                top = jnp.concatenate([t[0:8, 0:256], t[8:16, 0:256]], axis=1)
                e0, e1 = t[0:8, 256:384], t[8:16, 256:384]
                low = [e0, pltpu.roll(e0, 4, 0), e1, pltpu.roll(e1, 4, 0)]
                low = jnp.concatenate([jnp.where(zero4, v, 0.0) for v in low], axis=1)
                cols.append(jnp.concatenate([top, low], axis=0))
    d_norm = jnp.concatenate(cols, axis=1)
    h = d_norm * gain_ref[...]
    nh = nhat_s[...]
    inner = h - jnp.mean(h, axis=1, keepdims=True) - nh * jnp.mean(h * nh, axis=1, keepdims=True)
    d_rows = rstd_s[:, 0:1] * inner
    high = d_rows.astype(BF16)
    rows_ref[0:16, :] = high
    rows_ref[16:32, :] = (d_rows - high.astype(F32)).astype(BF16)

    for d in gain3:
        d.wait_recv()
    for h in range(2):
        g = gy[0, h] + gy[1, h] + gy[2, h] + gy[3, h]
        for i in range(6):
            at = slice(h * HALF + i * WW, h * HALF + (i + 1) * WW)
            gout_ref[:, at] = g[i:i + 1, :] / gain_ref[:, at]

    y2mu.wait_recv()
    ykeep[0] += yr2[1, 0].astype(F32)
    y2pd.wait_recv()
    ykeep[1] += yr2[0, 1].astype(F32)
    y2pu.wait_recv()
    upg_ref[...] = (ykeep[0] + yr2[0, 0].astype(F32)).T.astype(BF16)
    y2md.wait_recv()
    dng_ref[...] = (ykeep[1] + yr2[1, 1].astype(F32)).astype(BF16)

    for d in started:
        d.wait_send()


N_COPIES = 256


def kernel_call(keep, tokens, cotangent, gain, w_up, w_down):
    vmem = pl.BlockSpec(memory_space=pltpu.VMEM)
    hbm = pl.BlockSpec(memory_space=pl.ANY)

    def v(shape, dt=BF16):
        return pltpu.VMEM(shape, dt)

    scratch = [
        v((TOK, D)), v((TOK, D)),
        v((2, 2, 16, 512)), v((CHUNKS - 1, 2, 2, 16, 384)),
        v((2, 4, 2, 16, 512)), v((CHUNKS - 1, 2, 4, 2, 16, 384)),
        v((CHUNKS, BOTH, CW)), v((2, 4, BOTH, HALF)),
        v((HALF, FB)), v((FB, HALF)),
        v((4, 2, BOTH, FB), F32), v((4, 2, BOTH, FB)), v((4, 2, BOTH, FB)),
        v((FB, 4 * BOTH)), v((FB, 4 * BOTH)), v((4, BOTH, FB)), v((4, BOTH, FB)),
        v((3, 4, BOTH, WW)), v((3, 4, BOTH, WW)), v((3, 4, BOTH, WW), F32),
        v((3, 2, BOTH, 256)), v((3, 2, BOTH, 256)), v((3, 2, BOTH, WW)), v((3, 2, BOTH, WW)),
        v((3, 2, 4, 2, 16, 384)), v((3, 2, 2, 4, 16, 384)),
        v((16, D), F32), v((16, 128), F32),
        v((2, FB, QW)), v((2, FB, QW)), v((2, 2, FB, QW)), v((2, 2, FB, QW)),
        v((2, FB, QW), F32),
        v((4, 8, WW), F32), v((2, 8, 8, WW), F32), v((4, 2, 8, WW), F32),
        pltpu.SemaphoreType.DMA((N_COPIES,)), pltpu.SemaphoreType.DMA((N_COPIES,)),
        pltpu.SemaphoreType.DMA((10,)),
    ]
    return pl.pallas_call(
        body,
        out_shape=(
            jax.ShapeDtypeStruct((32, D), BF16),
            jax.ShapeDtypeStruct((TOK, 32), BF16),
            jax.ShapeDtypeStruct((1, D), F32),
            jax.ShapeDtypeStruct((QW, FB), BF16),
            jax.ShapeDtypeStruct((FB, QW), BF16),
        ),
        in_specs=[vmem, vmem, hbm, hbm, hbm, hbm],
        out_specs=(vmem,) * 5,
        scratch_shapes=scratch,
        compiler_params=pltpu.CompilerParams(
            collective_id=0, has_side_effects=True, vmem_limit_bytes=60 * 2**20
        ),
    )(keep, gain, tokens, cotangent, w_up, w_down)


def local(tokens, gain, w_up, w_down, cotangent, keep_index):
    rows, sel, gain_grad, up, down = kernel_call(
        keep_index, tokens, cotangent, gain.reshape(1, D), w_up, w_down
    )
    input_grad = (cotangent.astype(F32) + dot(sel, rows)).astype(BF16)
    return (input_grad, gain_grad.reshape(D), up, down)


def solution(mesh):
    in_specs = (
        P(("replica", "node"), None),
        P(),
        P("replica", "node"),
        P("node", "replica"),
        P(("replica", "node"), None),
        P("replica", None),
    )
    out_specs = (P(("replica", "node"), None), P(), P("replica", "node"), P("node", "replica"))
    return jax.shard_map(local, mesh=mesh, in_specs=in_specs, out_specs=out_specs, check_vma=False)
```

```python
import functools

import jax
import jax.numpy as jnp
from jax import lax
from jax.experimental import pallas as pl
from jax.experimental.pallas import tpu as pltpu
from jax.sharding import PartitionSpec as P

CAP = 12
TOK = 256
D = 6144
HALF = 3072
QW = 768
CW = 512
CHUNKS = 6
WW = 512
FB = 384
SEQ_ROWS = 72
BOTH = 144
EPS = 1e-05
NONE = 255
F32 = jnp.float32
BF16 = jnp.bfloat16
MESH = pl.DeviceIdType.MESH

A_TANH = 0.7978845608028654
B_TANH = 0.044715


def dot(a, b, ca=1, cb=0):
    return lax.dot_general(a, b, (((ca,), (cb,)), ((), ())), preferred_element_type=F32)


def iota(shape, dim):
    return lax.broadcasted_iota(jnp.int32, shape, dim)


def body(
    keep_ref, gain_ref, tok_hbm, cot_hbm, wup_ref, wdn_ref,
    rows_ref, sel_ref, gout_ref, upg_ref, dng_ref,
    tok_ref, cot_ref, pk0, pkn, g0, gn, ordered, t_buf, wu, wd,
    keepf, psend, precv, act_t, dpre_t, act_b, dpre_b,
    csend, crecv, cown, xs1, xr1, xs2, xr2, zs, zr, nhat_s, rstd_s,
    ys1, yr1, ys2, yr2, ykeep, gx, gz, gy,
    ssem, rsem, lsem,
):
    r = lax.axis_index("replica")
    n = lax.axis_index("node")
    zl, y = r // 4, lax.rem(r, 4)
    x, zh, c = n // 8, lax.rem(n // 2, 4), lax.rem(n, 2)

    def dev(x_=None, y_=None, zh_=None, zl_=None, c_=None):
        x_ = x if x_ is None else x_
        y_ = y if y_ is None else y_
        zh_ = zh if zh_ is None else zh_
        zl_ = zl if zl_ is None else zl_
        c_ = c if c_ is None else c_
        return (zl_ * 4 + y_, x_ * 8 + zh_ * 2 + c_)

    def step(v, d):
        return lax.rem(v + (d % 4), 4)

    count = [0]
    started = []

    def send(src, dst, to):
        k = count[0]
        count[0] += 1
        d = pltpu.make_async_remote_copy(
            src_ref=src, dst_ref=dst, send_sem=ssem.at[k], recv_sem=rsem.at[k],
            device_id=to, device_id_type=MESH,
        )
        d.start()
        started.append(d)
        return d

    def fetch(src, dst, k):
        d = pltpu.make_async_copy(src, dst, lsem.at[k])
        d.start()
        return d

    def col_of(ref, first, width):
        return ref.at[:, pl.ds(pl.multiple_of(first, 128), width)]

    z_peers = [(a, b, e) for a in range(4) for b in range(2) for e in range(2)][1:]

    def z_peer(a, b, e):
        return dev(zh_=step(zh, a), zl_=lax.rem(zl + b, 2), c_=lax.rem(c + e, 2))

    barrier = pltpu.get_barrier_semaphore()
    peers = [z_peer(*p) for p in z_peers]
    peers += [dev(x_=step(x, d)) for d in (1, 2, 3)]
    peers += [dev(y_=step(y, d)) for d in (1, 2, 3)]
    for p in peers:
        pl.semaphore_signal(barrier, inc=1, device_id=p, device_id_type=MESH)
    tok_in, cot_in = [], []
    for ref, to, ins, k in ((tok_hbm, tok_ref, tok_in, 2), (cot_hbm, cot_ref, cot_in, 6)):
        for i in range(4):
            at = pl.ds(64 * i, 64)
            ins.append(fetch(ref.at[at], to.at[at], k + i))
    wu_own = wu.at[pl.ds(pl.multiple_of(y * QW, QW), QW)]
    wd_own = col_of(wd, y * QW, QW)
    wu_in = fetch(wup_ref, wu_own, 0)
    wd_in = fetch(wdn_ref, wd_own, 1)

    n8 = lax.rem(n, 8)
    kv = keep_ref[pl.ds(x, 1), :]
    owner = kv // TOK
    before = jnp.sum((owner < n8).astype(F32), axis=1, keepdims=True)
    mine = jnp.sum((owner == n8).astype(F32), axis=1, keepdims=True)
    slot_col = iota((16, SEQ_ROWS), 0).astype(F32)
    j_row = iota((16, SEQ_ROWS), 1).astype(F32)
    local_pos = (kv - n8 * TOK).astype(F32)
    hit = (j_row == before + slot_col) & (slot_col < mine)
    pos = jnp.sum(jnp.where(hit, local_pos, 0.0), axis=1, keepdims=True)
    live = iota((16, TOK), 0).astype(F32) < mine
    sel = jnp.where((iota((16, TOK), 1).astype(F32) == pos) & live, 1.0, 0.0).astype(BF16)
    sel_f = sel.astype(F32)
    sel_ref[...] = jnp.concatenate([sel_f, sel_f], axis=0).T.astype(BF16)

    row_i, lane_i = iota((16, 128), 0), iota((16, 128), 1)
    kind = lax.rem(row_i, 8)
    i_in = lane_i - (zh * 2 + c) * 16
    slot = jnp.where(
        kind == 0, i_in,
        jnp.where(kind == 1, i_in - 8, jnp.where(kind < 6, 8 + i_in - 4 * (kind - 2), i_in)),
    )
    is_b = (kind >= 2) & (kind < 6)
    ok = (slot >= jnp.where(is_b, 8, 0)) & (slot < jnp.where(kind < 2, 8, CAP))
    slot_f = slot.astype(F32)
    target = jnp.where(ok & (slot_f < mine), before + slot_f, float(NONE))
    here = (i_in >= 0) & (i_in < 16) & (row_i // 8 == zl)
    meta = jnp.where(here, target, 0.0).astype(BF16)

    pks = [pk0] + [pkn.at[k] for k in range(CHUNKS - 1)]
    gs = [g0] + [gn.at[k] for k in range(CHUNKS - 1)]

    def pack(rows, a):
        for h in range(2):
            for k in range(CHUNKS):
                col = h * HALF + k * CW
                blk = rows[:, col:col + CW]
                main = jnp.concatenate([blk[0:8, 0:256], blk[0:8, 256:512]], axis=0)
                t = [blk[8:16, 128 * b:128 * (b + 1)] for b in range(4)]
                extra = jnp.concatenate(
                    [t[0] + pltpu.roll(t[1], 4, 0), t[2] + pltpu.roll(t[3], 4, 0)], axis=0
                )
                pks[k][a, h, :, 0:256] = main.astype(BF16)
                pks[k][a, h, :, 256:384] = extra.astype(BF16)
            pk0[a, h, :, 384:512] = meta

    pl.semaphore_wait(barrier, len(peers))

    y_p, y_m = dev(y_=step(y, 1)), dev(y_=step(y, -1))
    wu_in.wait()
    wu_r, wu_l = send(wu_own, wu_own, y_p), send(wu_own, wu_own, y_m)
    wd_in.wait()

    def pass_w_up():
        wu_r.wait_recv()
        p = wu.at[pl.ds(pl.multiple_of(step(y, -1) * QW, QW), QW // 2)]
        a = send(p, p, y_p)
        wu_l.wait_recv()
        p = wu.at[pl.ds(pl.multiple_of(step(y, 1) * QW + QW // 2, QW // 2), QW // 2)]
        return a, send(p, p, y_m)

    def send_w_down():
        return send(wd_own, wd_own, y_p), send(wd_own, wd_own, y_m)

    def pass_w_down(own):
        own[0].wait_recv()
        p = col_of(wd, step(y, -1) * QW, QW // 2)
        a = send(p, p, y_p)
        own[1].wait_recv()
        p = col_of(wd, step(y, 1) * QW + QW // 2, QW // 2)
        return a, send(p, p, y_m)

    for d in tok_in:
        d.wait()
    xr = dot(sel, tok_ref[...])
    mean = jnp.mean(xr, axis=1, keepdims=True)
    cen = xr - mean
    rstd = lax.rsqrt(jnp.mean(cen * cen, axis=1, keepdims=True) + EPS)
    nhat = cen * rstd
    nhat_s[...] = nhat
    rstd_s[...] = jnp.broadcast_to(rstd, (16, 128))
    pack(nhat * gain_ref[...], 0)
    for d in cot_in:
        d.wait()
    pack(dot(sel, cot_ref[...]), 1)


    for k in range(CHUNKS):
        gs[k][pl.ds(zl, 1), pl.ds(zh, 1), pl.ds(c, 1)] = pks[k][pl.ds(c, 1), pl.ds(zl, 1)][None]

    up_z, dn_z = dev(zh_=step(zh, 1)), dev(zh_=step(zh, -1))
    xp, xm, sib = dev(x_=step(x, 1)), dev(x_=step(x, -1)), dev(c_=1 - c)
    s_m, s_p, s_2 = step(x, -1), step(x, 1), step(x, 2)
    row_f = iota((BOTH, 128), 0).astype(F32)
    ring, ring2, hops = {}, {}, {}
    oh = []

    def z_own(k):
        for dz in (1, 3, 0):
            ring[k, dz] = []
            for b, e in ((0, 1), (1, 0), (1, 1), (0, 0)):
                if dz or b or e:
                    zl2, c2 = lax.rem(zl + b, 2), lax.rem(c + e, 2)
                    ring[k, dz].append(
                        send(pks[k].at[c2, zl2], gs[k].at[zl, zh, c], z_peer(dz, b, e))
                    )

    def z_next(k):
        for d in ring[k, 1]:
            d.wait_recv()
        f0 = send(gs[k].at[:, step(zh, -1), 0], gs[k].at[:, step(zh, -1), 0], up_z)
        for d in ring[k, 3]:
            d.wait_recv()
        f1 = send(gs[k].at[:, step(zh, 1), 1], gs[k].at[:, step(zh, 1), 1], dn_z)
        ring2[k] = (f0, f1)

    def one_hot(meta_sum, kk):
        return jnp.concatenate(
            [
                jnp.where(row_f == meta_sum[kk:kk + 1, :], 1.0, 0.0),
                jnp.where(row_f == meta_sum[8 + kk:9 + kk, :] + SEQ_ROWS, 1.0, 0.0),
            ],
            axis=1,
        )

    def chunk_of(a, s, k):
        return t_buf.at[a, s, :, pl.ds(k * CW, CW)]

    def order(k):
        for d in ring[k, 0]:
            d.wait_recv()
        for d in ring2[k]:
            d.wait_recv()
        if k == 0:
            ms = jnp.zeros((16, 128), F32)
            for a in range(2):
                for b in range(4):
                    for e in range(2):
                        ms = ms + g0[a, b, e, :, 384:512].astype(F32)
            oh.extend(one_hot(ms, kk).astype(BF16) for kk in range(6))
            oh.append(one_hot(ms, 6))
        ga = gs[k][:, :, :, :, 0:256].reshape(256, 256)
        gb = gs[k][:, :, :, :, 256:384].reshape(256, 128)
        for a in range(2):
            v = dot(oh[a], ga) + jnp.concatenate(
                [dot(oh[2 + 2 * a], gb), dot(oh[3 + 2 * a], gb)], axis=1
            )
            ordered[k, :, 256 * a:256 * (a + 1)] = v.astype(BF16)
        dst = chunk_of(c, x, k)
        hops[k] = (send(ordered.at[k], dst, xp), send(ordered.at[k], dst, xm))
        t_buf[pl.ds(c, 1), pl.ds(x, 1), :, CW * k:CW * (k + 1)] = ordered[k][None, None]
        if k % 2:
            to_sib(0, x, k // 2)

    sibs, fx = {}, {}

    def to_sib(i, s, pair):
        p = t_buf.at[c, s, :, pl.ds(2 * CW * pair, 2 * CW)]
        sibs[i, pair] = send(p, p, sib)

    def pass_on(k):
        hops[k][0].wait_recv()
        hops[k][1].wait_recv()
        p = chunk_of(c, s_p if k % 2 else s_m, k)
        fx[k] = send(p, p, xm if k % 2 else xp)
        if k % 2:
            to_sib(-1, s_m, k // 2)
            to_sib(1, s_p, k // 2)

    zp = dev(zl_=1 - zl)

    def give(i, j, v):
        keepf[i, j] = v
        psend[i, j] = v.astype(BF16)
        parts[i, j] = send(psend.at[i, j], precv.at[i, j], zp)

    def pre_part(i, s):
        give(i, 0, dot(t_buf[0, s], wu[...]))

    def dac_part(i, s):
        give(i, 1, dot(t_buf[1, s], wd[...], 1, 1))

    def far_parts():
        pre = jnp.zeros((BOTH, FB), F32)
        dac = jnp.zeros((BOTH, FB), F32)
        for k in range(3):
            sibs[2, k].wait_recv()
            at = slice(2 * CW * k, 2 * CW * (k + 1))
            pre = pre + dot(t_buf[0, s_2, :, at], wu[at])
            if k == 2:
                give(3, 0, pre)
            dac = dac + dot(t_buf[1, s_2, :, at], wd[:, at], 1, 1)
        give(3, 1, dac)

    def middle(i, s):
        parts[i, 0].wait_recv()
        parts[i, 1].wait_recv()
        v = keepf[i, 0] + precv[i, 0].astype(F32)
        da = keepf[i, 1] + precv[i, 1].astype(F32)
        v2 = v * v
        t = jnp.tanh(A_TANH * (v + B_TANH * v * v2))
        act = 0.5 * v * (1.0 + t)
        slope = 0.5 * (1.0 + t) + 0.5 * v * (1.0 - t * t) * (A_TANH * (1.0 + 3.0 * B_TANH * v2))
        act_b[s] = act.astype(BF16)
        dpre_b[s] = (da * slope).astype(BF16)

    parts = {}

    def from_sib(i):
        for k in range(3):
            sibs[i, k].wait_recv()

    q_p, q_m, q_2 = step(y, 1), step(y, -1), step(y, 2)
    q_cols = pl.ds(pl.multiple_of(q_2 * QW, 128), QW)

    def first_terms(s):
        yield dot(dpre_b[s], t_buf[0, s, :, q_cols], 0, 0)
        yield dot(act_b[s], t_buf[1, s, :, q_cols], 0, 0)

    def far_pair(k):
        fx[2 * k].wait_recv()
        fx[2 * k + 1].wait_recv()
        to_sib(2, s_2, k)

    z_own(0)
    z_own(1)
    z_next(0)
    z_own(2)
    z_next(1)
    wu_far = pass_w_up()
    wd_near = send_w_down()
    order(0)
    z_own(3)
    z_next(2)
    order(1)
    z_own(4)
    z_next(3)
    order(2)
    z_own(5)
    z_next(4)
    order(3)

    z_next(5)
    order(4)
    wd_far = pass_w_down(wd_near)
    order(5)
    pass_on(0)
    pass_on(1)
    for d in wu_far:
        d.wait_recv()
    from_sib(0)
    pre_part(0, x)
    pass_on(2)
    pass_on(3)
    pass_on(4)
    pass_on(5)
    from_sib(-1)
    pre_part(1, s_m)
    from_sib(1)
    pre_part(2, s_p)
    for d in wd_far:
        d.wait_recv()
    dac_part(0, x)
    dac_part(1, s_m)
    dac_part(2, s_p)
    far_pair(0)
    far_pair(1)
    middle(0, x)
    far_pair(2)
    middle(1, s_m)
    far_parts()
    middle(2, s_p)
    for i, s in enumerate((x, s_m, s_p)):
        for j, v in enumerate(first_terms(s)):
            ykeep[j] = v if i == 0 else ykeep[j] + v
    middle(3, s_2)

    def rows_of(a, q):
        v = t_buf[a, :, :, pl.ds(pl.multiple_of(q * QW, 128), QW)]
        return v.reshape(4 * BOTH, QW)

    def up_part(q):
        return dot(dpre_t[...], rows_of(0, q))

    def down_part(q):
        return dot(act_t[...], rows_of(1, q))

    yp, ym = y_p, y_m
    terms = first_terms(s_2)
    ys1[0] = (ykeep[0] + next(terms)).astype(BF16)
    y1u = send(ys1.at[0], yr1.at[0], yp)
    ys1[1] = (ykeep[1] + next(terms)).astype(BF16)
    y1d = send(ys1.at[1], yr1.at[1], ym)

    dpre_t[...] = dpre_b[...].reshape(4 * BOTH, FB).astype(F32).T.astype(BF16)
    act_t[...] = act_b[...].reshape(4 * BOTH, FB).astype(F32).T.astype(BF16)

    gx[pl.ds(x, 1)] = jnp.zeros((1, 8, WW), F32)
    cores, x1, x2, own = {}, {}, {}, {}

    def norm_wave(w):
        for cc, mine_ in ((1 - c, False), (c, True)):
            first_col = cc * (3 * WW) + w * WW
            wt = wu[pl.ds(pl.multiple_of(first_col, WW), WW), :]
            g = jnp.zeros((1, WW), F32)
            for s in range(4):
                v = dot(dpre_b[s], wt, 1, 1)
                if mine_:
                    cown[w, s] = v
                else:
                    csend[w, s] = v.astype(BF16)
                rows = t_buf[0, s, :, pl.ds(pl.multiple_of(first_col, WW), WW)]
                g = g + jnp.sum(v * rows.astype(F32), axis=0, keepdims=True)
            gx[pl.ds(x, 1), pl.ds(cc * 3 + w, 1)] = g[None]
            if not mine_:
                cores[w] = send(csend.at[w], crecv.at[w], sib)

    def summed(w, s, lo, hi):
        return cown[w, s, :, lo:hi] + crecv[w, s, :, lo:hi].astype(F32)

    def x_first(w):
        cores[w].wait_recv()
        xs1[w, 0] = summed(w, s_2, 0, 256).astype(BF16)
        a = send(xs1.at[w, 0], xr1.at[w, 0], xp)
        xs1[w, 1] = summed(w, s_2, 256, 512).astype(BF16)
        x1[w] = (a, send(xs1.at[w, 1], xr1.at[w, 1], xm))

    def x_second(w):
        xs2[w, 0, :, 256:512] = summed(w, s_p, 256, 512).astype(BF16)
        xs2[w, 1, :, 0:256] = summed(w, s_m, 0, 256).astype(BF16)
        x1[w][0].wait_recv()
        xs2[w, 0, :, 0:256] = (summed(w, s_p, 0, 256) + xr1[w, 0].astype(F32)).astype(BF16)
        a = send(xs2.at[w, 0], xr2.at[w, 0], xp)
        x1[w][1].wait_recv()
        xs2[w, 1, :, 256:512] = (summed(w, s_m, 256, 512) + xr1[w, 1].astype(F32)).astype(BF16)
        x2[w] = (a, send(xs2.at[w, 1], xr2.at[w, 1], xm))

    owners = {}

    def to_owners(w):
        for d in x2[w]:
            d.wait_recv()
        total = summed(w, x, 0, WW) + xr2[w, 0].astype(F32) + xr2[w, 1].astype(F32)
        total = total.astype(BF16)
        v = dot(own[0], total[:, 0:256]) + dot(own[1], total[:, 256:512])
        zs[w, :, :, :, :, 0:256] = v.astype(BF16).reshape(2, 4, 2, 16, 256)
        v = dot(own[2], total[:, 0:128])
        for b in range(1, 4):
            v = v + dot(own[2 + b], total[:, 128 * b:128 * (b + 1)])
        zs[w, :, :, :, :, 256:384] = v.astype(BF16).reshape(2, 4, 2, 16, 128)
        owners[w] = []
        for a, b, e in z_peers:
            zh2, zl2, c2 = step(zh, a), lax.rem(zl + b, 2), lax.rem(c + e, 2)
            owners[w].append(send(zs.at[w, zl2, zh2, c2], zr.at[w, zl, c, zh], z_peer(a, b, e)))
        zr[w, pl.ds(zl, 1), pl.ds(c, 1), pl.ds(zh, 1)] = zs[
            w, pl.ds(zl, 1), pl.ds(zh, 1), pl.ds(c, 1)
        ].reshape(1, 1, 1, 16, 384)

    for kk in range(6):
        own[kk] = oh[kk].astype(F32).T.astype(BF16)

    norm_wave(0)
    norm_wave(1)
    x_first(0)
    norm_wave(2)
    gain1 = [send(gx.at[x], gx.at[x], dev(x_=step(x, d))) for d in (1, 2, 3)]

    ys2[0, 1] = down_part(q_p).astype(BF16)
    y2pd = send(ys2.at[0, 1], yr2.at[0, 1], yp)
    x_first(1)
    ys2[1, 0] = up_part(q_m).astype(BF16)
    y2mu = send(ys2.at[1, 0], yr2.at[1, 0], ym)
    x_second(0)
    x_first(2)
    ykeep[0] = up_part(q_p)
    x_second(1)
    ykeep[1] = down_part(q_m)

    y1u.wait_recv()
    ys2[0, 0] = (ykeep[0] + yr1[0].astype(F32)).astype(BF16)
    y2pu = send(ys2.at[0, 0], yr2.at[0, 0], yp)
    y1d.wait_recv()
    ys2[1, 1] = (ykeep[1] + yr1[1].astype(F32)).astype(BF16)
    y2md = send(ys2.at[1, 1], yr2.at[1, 1], ym)

    to_owners(0)
    x_second(2)
    ykeep[0] = up_part(y)
    ykeep[1] = down_part(y)
    to_owners(1)

    for d in gain1:
        d.wait_recv()
    slot_me = zh * 2 + c
    gz[pl.ds(zl, 1), pl.ds(slot_me, 1)] = (gx[0] + gx[1] + gx[2] + gx[3])[None, None]
    gain2 = [send(gz.at[zl, slot_me], gz.at[zl, slot_me], z_peer(*p_)) for p_ in z_peers]
    to_owners(2)

    for d in gain2:
        d.wait_recv()
    for h in range(2):
        g = gz[h, 0]
        for i in range(1, 8):
            g = g + gz[h, i]
        gy[pl.ds(y, 1), h] = g[None]
    gain3 = [send(gy.at[y], gy.at[y], dev(y_=step(y, d))) for d in (1, 2, 3)]

    cols = []
    for w in range(3):
        for d in owners[w]:
            d.wait_recv()
    zero4 = iota((8, 128), 0) < 4
    for a in range(2):
        for e in range(2):
            for w in range(3):
                t = zr[w, a, e, 0].astype(F32)
                for b in range(1, 4):
                    t = t + zr[w, a, e, b].astype(F32)
                top = jnp.concatenate([t[0:8, 0:256], t[8:16, 0:256]], axis=1)
                e0, e1 = t[0:8, 256:384], t[8:16, 256:384]
                low = [e0, pltpu.roll(e0, 4, 0), e1, pltpu.roll(e1, 4, 0)]
                low = jnp.concatenate([jnp.where(zero4, v, 0.0) for v in low], axis=1)
                cols.append(jnp.concatenate([top, low], axis=0))
    d_norm = jnp.concatenate(cols, axis=1)
    h = d_norm * gain_ref[...]
    nh = nhat_s[...]
    inner = h - jnp.mean(h, axis=1, keepdims=True) - nh * jnp.mean(h * nh, axis=1, keepdims=True)
    d_rows = rstd_s[:, 0:1] * inner
    high = d_rows.astype(BF16)
    rows_ref[0:16, :] = high
    rows_ref[16:32, :] = (d_rows - high.astype(F32)).astype(BF16)

    for d in gain3:
        d.wait_recv()
    for h in range(2):
        g = gy[0, h] + gy[1, h] + gy[2, h] + gy[3, h]
        for i in range(6):
            at = slice(h * HALF + i * WW, h * HALF + (i + 1) * WW)
            gout_ref[:, at] = g[i:i + 1, :] / gain_ref[:, at]

    y2mu.wait_recv()
    ykeep[0] += yr2[1, 0].astype(F32)
    y2pd.wait_recv()
    ykeep[1] += yr2[0, 1].astype(F32)
    y2pu.wait_recv()
    upg_ref[...] = (ykeep[0] + yr2[0, 0].astype(F32)).T.astype(BF16)
    y2md.wait_recv()
    dng_ref[...] = (ykeep[1] + yr2[1, 1].astype(F32)).astype(BF16)

    for d in started:
        d.wait_send()


N_COPIES = 256


def kernel_call(keep, tokens, cotangent, gain, w_up, w_down):
    vmem = pl.BlockSpec(memory_space=pltpu.VMEM)
    hbm = pl.BlockSpec(memory_space=pl.ANY)

    def v(shape, dt=BF16):
        return pltpu.VMEM(shape, dt)

    scratch = [
        v((TOK, D)), v((TOK, D)),
        v((2, 2, 16, 512)), v((CHUNKS - 1, 2, 2, 16, 384)),
        v((2, 4, 2, 16, 512)), v((CHUNKS - 1, 2, 4, 2, 16, 384)),
        v((CHUNKS, BOTH, CW)), v((2, 4, BOTH, HALF)),
        v((HALF, FB)), v((FB, HALF)),
        v((4, 2, BOTH, FB), F32), v((4, 2, BOTH, FB)), v((4, 2, BOTH, FB)),
        v((FB, 4 * BOTH)), v((FB, 4 * BOTH)), v((4, BOTH, FB)), v((4, BOTH, FB)),
        v((3, 4, BOTH, WW)), v((3, 4, BOTH, WW)), v((3, 4, BOTH, WW), F32),
        v((3, 2, BOTH, 256)), v((3, 2, BOTH, 256)), v((3, 2, BOTH, WW)), v((3, 2, BOTH, WW)),
        v((3, 2, 4, 2, 16, 384)), v((3, 2, 2, 4, 16, 384)),
        v((16, D), F32), v((16, 128), F32),
        v((2, FB, QW)), v((2, FB, QW)), v((2, 2, FB, QW)), v((2, 2, FB, QW)),
        v((2, FB, QW), F32),
        v((4, 8, WW), F32), v((2, 8, 8, WW), F32), v((4, 2, 8, WW), F32),
        pltpu.SemaphoreType.DMA((N_COPIES,)), pltpu.SemaphoreType.DMA((N_COPIES,)),
        pltpu.SemaphoreType.DMA((10,)),
    ]
    return pl.pallas_call(
        body,
        out_shape=(
            jax.ShapeDtypeStruct((32, D), BF16),
            jax.ShapeDtypeStruct((TOK, 32), BF16),
            jax.ShapeDtypeStruct((1, D), F32),
            jax.ShapeDtypeStruct((QW, FB), BF16),
            jax.ShapeDtypeStruct((FB, QW), BF16),
        ),
        in_specs=[vmem, vmem, hbm, hbm, hbm, hbm],
        out_specs=(vmem,) * 5,
        scratch_shapes=scratch,
        compiler_params=pltpu.CompilerParams(
            collective_id=0, has_side_effects=True, vmem_limit_bytes=60 * 2**20
        ),
    )(keep, gain, tokens, cotangent, w_up, w_down)


def local(tokens, gain, w_up, w_down, cotangent, keep_index):
    rows, sel, gain_grad, up, down = kernel_call(
        keep_index, tokens, cotangent, gain.reshape(1, D), w_up, w_down
    )
    input_grad = (cotangent.astype(F32) + dot(sel, rows)).astype(BF16)
    return (input_grad, gain_grad.reshape(D), up, down)


def solution(mesh):
    in_specs = (
        P(("replica", "node"), None),
        P(),
        P("replica", "node"),
        P("node", "replica"),
        P(("replica", "node"), None),
        P("replica", None),
    )
    out_specs = (P(("replica", "node"), None), P(), P("replica", "node"), P("node", "replica"))
    return jax.shard_map(local, mesh=mesh, in_specs=in_specs, out_specs=out_specs, check_vma=False)
```

```python
import functools

import jax
import jax.numpy as jnp
from jax import lax
from jax.experimental import pallas as pl
from jax.experimental.pallas import tpu as pltpu
from jax.sharding import PartitionSpec as P

CAP = 12
TOK = 256
D = 6144
HALF = 3072
QW = 768
CW = 512
CHUNKS = 6
WW = 512
FB = 384
SEQ_ROWS = 72
BOTH = 144
EPS = 1e-05
NONE = 255
F32 = jnp.float32
BF16 = jnp.bfloat16
MESH = pl.DeviceIdType.MESH

A_TANH = 0.7978845608028654
B_TANH = 0.044715


def dot(a, b, ca=1, cb=0):
    return lax.dot_general(a, b, (((ca,), (cb,)), ((), ())), preferred_element_type=F32)


def iota(shape, dim):
    return lax.broadcasted_iota(jnp.int32, shape, dim)


def body(
    keep_ref, gain_ref, tok_hbm, cot_hbm, wup_ref, wdn_ref,
    rows_ref, sel_ref, gout_ref, upg_ref, dng_ref,
    tok_ref, cot_ref, pk0, pkn, g0, gn, ordered, t_buf, wu, wd,
    keepf, psend, precv, act_t, dpre_t, act_b, dpre_b,
    csend, crecv, cown, xs1, xr1, xs2, xr2, zs, zr, nhat_s, rstd_s,
    ys1, yr1, ys2, yr2, ykeep, gx, gz, gy,
    ssem, rsem, lsem,
):
    r = lax.axis_index("replica")
    n = lax.axis_index("node")
    zl, y = r // 4, lax.rem(r, 4)
    x, zh, c = n // 8, lax.rem(n // 2, 4), lax.rem(n, 2)

    def dev(x_=None, y_=None, zh_=None, zl_=None, c_=None):
        x_ = x if x_ is None else x_
        y_ = y if y_ is None else y_
        zh_ = zh if zh_ is None else zh_
        zl_ = zl if zl_ is None else zl_
        c_ = c if c_ is None else c_
        return (zl_ * 4 + y_, x_ * 8 + zh_ * 2 + c_)

    def step(v, d):
        return lax.rem(v + (d % 4), 4)

    count = [0]
    started = []

    def send(src, dst, to):
        k = count[0]
        count[0] += 1
        d = pltpu.make_async_remote_copy(
            src_ref=src, dst_ref=dst, send_sem=ssem.at[k], recv_sem=rsem.at[k],
            device_id=to, device_id_type=MESH,
        )
        d.start()
        started.append(d)
        return d

    def fetch(src, dst, k):
        d = pltpu.make_async_copy(src, dst, lsem.at[k])
        d.start()
        return d

    def col_of(ref, first, width):
        return ref.at[:, pl.ds(pl.multiple_of(first, 128), width)]

    z_peers = [(a, b, e) for a in range(4) for b in range(2) for e in range(2)][1:]

    def z_peer(a, b, e):
        return dev(zh_=step(zh, a), zl_=lax.rem(zl + b, 2), c_=lax.rem(c + e, 2))

    barrier = pltpu.get_barrier_semaphore()
    peers = [z_peer(*p) for p in z_peers]
    peers += [dev(x_=step(x, d)) for d in (1, 2, 3)]
    peers += [dev(y_=step(y, d)) for d in (1, 2, 3)]
    for p in peers:
        pl.semaphore_signal(barrier, inc=1, device_id=p, device_id_type=MESH)
    tok_in, cot_in = [], []
    for ref, to, ins, k in ((tok_hbm, tok_ref, tok_in, 2), (cot_hbm, cot_ref, cot_in, 6)):
        for i in range(4):
            at = pl.ds(64 * i, 64)
            ins.append(fetch(ref.at[at], to.at[at], k + i))
    wu_own = wu.at[pl.ds(pl.multiple_of(y * QW, QW), QW)]
    wd_own = col_of(wd, y * QW, QW)
    wu_in = fetch(wup_ref, wu_own, 0)
    wd_in = fetch(wdn_ref, wd_own, 1)

    n8 = lax.rem(n, 8)
    kv = keep_ref[pl.ds(x, 1), :]
    owner = kv // TOK
    before = jnp.sum((owner < n8).astype(F32), axis=1, keepdims=True)
    mine = jnp.sum((owner == n8).astype(F32), axis=1, keepdims=True)
    slot_col = iota((16, SEQ_ROWS), 0).astype(F32)
    j_row = iota((16, SEQ_ROWS), 1).astype(F32)
    local_pos = (kv - n8 * TOK).astype(F32)
    hit = (j_row == before + slot_col) & (slot_col < mine)
    pos = jnp.sum(jnp.where(hit, local_pos, 0.0), axis=1, keepdims=True)
    live = iota((16, TOK), 0).astype(F32) < mine
    sel = jnp.where((iota((16, TOK), 1).astype(F32) == pos) & live, 1.0, 0.0).astype(BF16)
    sel_f = sel.astype(F32)
    sel_ref[...] = jnp.concatenate([sel_f, sel_f], axis=0).T.astype(BF16)

    row_i, lane_i = iota((16, 128), 0), iota((16, 128), 1)
    kind = lax.rem(row_i, 8)
    i_in = lane_i - (zh * 2 + c) * 16
    slot = jnp.where(
        kind == 0, i_in,
        jnp.where(kind == 1, i_in - 8, jnp.where(kind < 6, 8 + i_in - 4 * (kind - 2), i_in)),
    )
    is_b = (kind >= 2) & (kind < 6)
    ok = (slot >= jnp.where(is_b, 8, 0)) & (slot < jnp.where(kind < 2, 8, CAP))
    slot_f = slot.astype(F32)
    target = jnp.where(ok & (slot_f < mine), before + slot_f, float(NONE))
    here = (i_in >= 0) & (i_in < 16) & (row_i // 8 == zl)
    meta = jnp.where(here, target, 0.0).astype(BF16)

    pks = [pk0] + [pkn.at[k] for k in range(CHUNKS - 1)]
    gs = [g0] + [gn.at[k] for k in range(CHUNKS - 1)]

    def pack(rows, a):
        for h in range(2):
            for k in range(CHUNKS):
                col = h * HALF + k * CW
                blk = rows[:, col:col + CW]
                main = jnp.concatenate([blk[0:8, 0:256], blk[0:8, 256:512]], axis=0)
                t = [blk[8:16, 128 * b:128 * (b + 1)] for b in range(4)]
                extra = jnp.concatenate(
                    [t[0] + pltpu.roll(t[1], 4, 0), t[2] + pltpu.roll(t[3], 4, 0)], axis=0
                )
                pks[k][a, h, :, 0:256] = main.astype(BF16)
                pks[k][a, h, :, 256:384] = extra.astype(BF16)
            pk0[a, h, :, 384:512] = meta

    pl.semaphore_wait(barrier, len(peers))

    y_p, y_m = dev(y_=step(y, 1)), dev(y_=step(y, -1))
    wu_in.wait()
    wu_r, wu_l = send(wu_own, wu_own, y_p), send(wu_own, wu_own, y_m)
    wd_in.wait()
    wd_near = send(wd_own, wd_own, y_p), send(wd_own, wd_own, y_m)

    def pass_w_up():
        wu_r.wait_recv()
        p = wu.at[pl.ds(pl.multiple_of(step(y, -1) * QW, QW), QW // 2)]
        a = send(p, p, y_p)
        wu_l.wait_recv()
        p = wu.at[pl.ds(pl.multiple_of(step(y, 1) * QW + QW // 2, QW // 2), QW // 2)]
        return a, send(p, p, y_m)

    def pass_w_down(own):
        own[0].wait_recv()
        p = col_of(wd, step(y, -1) * QW, QW // 2)
        a = send(p, p, y_p)
        own[1].wait_recv()
        p = col_of(wd, step(y, 1) * QW + QW // 2, QW // 2)
        return a, send(p, p, y_m)

    for d in tok_in:
        d.wait()
    xr = dot(sel, tok_ref[...])
    mean = jnp.mean(xr, axis=1, keepdims=True)
    cen = xr - mean
    rstd = lax.rsqrt(jnp.mean(cen * cen, axis=1, keepdims=True) + EPS)
    nhat = cen * rstd
    nhat_s[...] = nhat
    rstd_s[...] = jnp.broadcast_to(rstd, (16, 128))
    pack(nhat * gain_ref[...], 0)
    for d in cot_in:
        d.wait()
    pack(dot(sel, cot_ref[...]), 1)


    for k in range(CHUNKS):
        gs[k][pl.ds(zl, 1), pl.ds(zh, 1), pl.ds(c, 1)] = pks[k][pl.ds(c, 1), pl.ds(zl, 1)][None]

    up_z, dn_z = dev(zh_=step(zh, 1)), dev(zh_=step(zh, -1))
    xp, xm, sib = dev(x_=step(x, 1)), dev(x_=step(x, -1)), dev(c_=1 - c)
    s_m, s_p, s_2 = step(x, -1), step(x, 1), step(x, 2)
    row_f = iota((BOTH, 128), 0).astype(F32)
    ring, ring2, hops = {}, {}, {}
    oh = []

    def z_own(k):
        for dz in (1, 3, 0):
            ring[k, dz] = []
            for b, e in ((0, 1), (1, 0), (1, 1), (0, 0)):
                if dz or b or e:
                    zl2, c2 = lax.rem(zl + b, 2), lax.rem(c + e, 2)
                    ring[k, dz].append(
                        send(pks[k].at[c2, zl2], gs[k].at[zl, zh, c], z_peer(dz, b, e))
                    )

    def z_next(k):
        for d in ring[k, 1]:
            d.wait_recv()
        f0 = send(gs[k].at[:, step(zh, -1), 0], gs[k].at[:, step(zh, -1), 0], up_z)
        for d in ring[k, 3]:
            d.wait_recv()
        f1 = send(gs[k].at[:, step(zh, 1), 1], gs[k].at[:, step(zh, 1), 1], dn_z)
        ring2[k] = (f0, f1)

    def one_hot(meta_sum, kk):
        return jnp.concatenate(
            [
                jnp.where(row_f == meta_sum[kk:kk + 1, :], 1.0, 0.0),
                jnp.where(row_f == meta_sum[8 + kk:9 + kk, :] + SEQ_ROWS, 1.0, 0.0),
            ],
            axis=1,
        )

    def chunk_of(a, s, k):
        return t_buf.at[a, s, :, pl.ds(k * CW, CW)]

    def order(k):
        for d in ring[k, 0]:
            d.wait_recv()
        for d in ring2[k]:
            d.wait_recv()
        if k == 0:
            ms = jnp.zeros((16, 128), F32)
            for a in range(2):
                for b in range(4):
                    for e in range(2):
                        ms = ms + g0[a, b, e, :, 384:512].astype(F32)
            oh.extend(one_hot(ms, kk).astype(BF16) for kk in range(6))
            oh.append(one_hot(ms, 6))
        ga = gs[k][:, :, :, :, 0:256].reshape(256, 256)
        gb = gs[k][:, :, :, :, 256:384].reshape(256, 128)
        for a in range(2):
            v = dot(oh[a], ga) + jnp.concatenate(
                [dot(oh[2 + 2 * a], gb), dot(oh[3 + 2 * a], gb)], axis=1
            )
            ordered[k, :, 256 * a:256 * (a + 1)] = v.astype(BF16)
        dst = chunk_of(c, x, k)
        hops[k] = (send(ordered.at[k], dst, xp), send(ordered.at[k], dst, xm))
        t_buf[pl.ds(c, 1), pl.ds(x, 1), :, CW * k:CW * (k + 1)] = ordered[k][None, None]
        if k % 2:
            to_sib(0, x, k // 2)

    sibs, fx = {}, {}

    def to_sib(i, s, pair):
        p = t_buf.at[c, s, :, pl.ds(2 * CW * pair, 2 * CW)]
        sibs[i, pair] = send(p, p, sib)

    def pass_on(k):
        hops[k][0].wait_recv()
        hops[k][1].wait_recv()
        p = chunk_of(c, s_p if k % 2 else s_m, k)
        fx[k] = send(p, p, xm if k % 2 else xp)
        if k % 2:
            to_sib(-1, s_m, k // 2)
            to_sib(1, s_p, k // 2)

    zp = dev(zl_=1 - zl)

    def give(i, j, v):
        keepf[i, j] = v
        psend[i, j] = v.astype(BF16)
        parts[i, j] = send(psend.at[i, j], precv.at[i, j], zp)

    def pre_part(i, s):
        give(i, 0, dot(t_buf[0, s], wu[...]))

    def dac_part(i, s):
        give(i, 1, dot(t_buf[1, s], wd[...], 1, 1))

    def far_parts():
        pre = jnp.zeros((BOTH, FB), F32)
        dac = jnp.zeros((BOTH, FB), F32)
        for k in range(3):
            sibs[2, k].wait_recv()
            at = slice(2 * CW * k, 2 * CW * (k + 1))
            pre = pre + dot(t_buf[0, s_2, :, at], wu[at])
            if k == 2:
                give(3, 0, pre)
            dac = dac + dot(t_buf[1, s_2, :, at], wd[:, at], 1, 1)
        give(3, 1, dac)

    def middle(i, s):
        parts[i, 0].wait_recv()
        parts[i, 1].wait_recv()
        v = keepf[i, 0] + precv[i, 0].astype(F32)
        da = keepf[i, 1] + precv[i, 1].astype(F32)
        v2 = v * v
        t = jnp.tanh(A_TANH * (v + B_TANH * v * v2))
        act = 0.5 * v * (1.0 + t)
        slope = 0.5 * (1.0 + t) + 0.5 * v * (1.0 - t * t) * (A_TANH * (1.0 + 3.0 * B_TANH * v2))
        act_b[s] = act.astype(BF16)
        dpre_b[s] = (da * slope).astype(BF16)

    parts = {}

    def from_sib(i):
        for k in range(3):
            sibs[i, k].wait_recv()

    q_p, q_m, q_2 = step(y, 1), step(y, -1), step(y, 2)
    q_cols = pl.ds(pl.multiple_of(q_2 * QW, 128), QW)

    def first_terms(s):
        yield dot(dpre_b[s], t_buf[0, s, :, q_cols], 0, 0)
        yield dot(act_b[s], t_buf[1, s, :, q_cols], 0, 0)

    def far_pair(k):
        fx[2 * k].wait_recv()
        fx[2 * k + 1].wait_recv()
        to_sib(2, s_2, k)

    z_own(0)
    z_own(1)
    z_next(0)
    z_own(2)
    z_next(1)
    wu_far = pass_w_up()
    order(0)
    z_own(3)
    z_next(2)
    order(1)
    z_own(4)
    z_next(3)
    order(2)
    z_own(5)
    z_next(4)
    order(3)

    z_next(5)
    order(4)
    order(5)
    wd_far = pass_w_down(wd_near)
    pass_on(0)
    pass_on(1)
    for d in wu_far:
        d.wait_recv()
    from_sib(0)
    pre_part(0, x)
    pass_on(2)
    pass_on(3)
    pass_on(4)
    pass_on(5)
    from_sib(-1)
    pre_part(1, s_m)
    from_sib(1)
    pre_part(2, s_p)
    for d in wd_far:
        d.wait_recv()
    dac_part(0, x)
    dac_part(1, s_m)
    dac_part(2, s_p)
    far_pair(0)
    far_pair(1)
    middle(0, x)
    far_pair(2)
    middle(1, s_m)
    far_parts()
    middle(2, s_p)
    for i, s in enumerate((x, s_m, s_p)):
        for j, v in enumerate(first_terms(s)):
            ykeep[j] = v if i == 0 else ykeep[j] + v
    middle(3, s_2)

    def rows_of(a, q):
        v = t_buf[a, :, :, pl.ds(pl.multiple_of(q * QW, 128), QW)]
        return v.reshape(4 * BOTH, QW)

    def up_part(q):
        return dot(dpre_t[...], rows_of(0, q))

    def down_part(q):
        return dot(act_t[...], rows_of(1, q))

    yp, ym = y_p, y_m
    terms = first_terms(s_2)
    ys1[0] = (ykeep[0] + next(terms)).astype(BF16)
    y1u = send(ys1.at[0], yr1.at[0], yp)
    ys1[1] = (ykeep[1] + next(terms)).astype(BF16)
    y1d = send(ys1.at[1], yr1.at[1], ym)

    dpre_t[...] = dpre_b[...].reshape(4 * BOTH, FB).astype(F32).T.astype(BF16)
    act_t[...] = act_b[...].reshape(4 * BOTH, FB).astype(F32).T.astype(BF16)

    gx[pl.ds(x, 1)] = jnp.zeros((1, 8, WW), F32)
    cores, x1, x2, own = {}, {}, {}, {}

    def norm_wave(w):
        for cc, mine_ in ((1 - c, False), (c, True)):
            first_col = cc * (3 * WW) + w * WW
            wt = wu[pl.ds(pl.multiple_of(first_col, WW), WW), :]
            g = jnp.zeros((1, WW), F32)
            for s in range(4):
                v = dot(dpre_b[s], wt, 1, 1)
                if mine_:
                    cown[w, s] = v
                else:
                    csend[w, s] = v.astype(BF16)
                rows = t_buf[0, s, :, pl.ds(pl.multiple_of(first_col, WW), WW)]
                g = g + jnp.sum(v * rows.astype(F32), axis=0, keepdims=True)
            gx[pl.ds(x, 1), pl.ds(cc * 3 + w, 1)] = g[None]
            if not mine_:
                cores[w] = send(csend.at[w], crecv.at[w], sib)

    def summed(w, s, lo, hi):
        return cown[w, s, :, lo:hi] + crecv[w, s, :, lo:hi].astype(F32)

    def x_first(w):
        cores[w].wait_recv()
        xs1[w, 0] = summed(w, s_2, 0, 256).astype(BF16)
        a = send(xs1.at[w, 0], xr1.at[w, 0], xp)
        xs1[w, 1] = summed(w, s_2, 256, 512).astype(BF16)
        x1[w] = (a, send(xs1.at[w, 1], xr1.at[w, 1], xm))

    def x_second(w):
        xs2[w, 0, :, 256:512] = summed(w, s_p, 256, 512).astype(BF16)
        xs2[w, 1, :, 0:256] = summed(w, s_m, 0, 256).astype(BF16)
        x1[w][0].wait_recv()
        xs2[w, 0, :, 0:256] = (summed(w, s_p, 0, 256) + xr1[w, 0].astype(F32)).astype(BF16)
        a = send(xs2.at[w, 0], xr2.at[w, 0], xp)
        x1[w][1].wait_recv()
        xs2[w, 1, :, 256:512] = (summed(w, s_m, 256, 512) + xr1[w, 1].astype(F32)).astype(BF16)
        x2[w] = (a, send(xs2.at[w, 1], xr2.at[w, 1], xm))

    owners = {}

    def to_owners(w):
        for d in x2[w]:
            d.wait_recv()
        total = summed(w, x, 0, WW) + xr2[w, 0].astype(F32) + xr2[w, 1].astype(F32)
        total = total.astype(BF16)
        v = dot(own[0], total[:, 0:256]) + dot(own[1], total[:, 256:512])
        zs[w, :, :, :, :, 0:256] = v.astype(BF16).reshape(2, 4, 2, 16, 256)
        v = dot(own[2], total[:, 0:128])
        for b in range(1, 4):
            v = v + dot(own[2 + b], total[:, 128 * b:128 * (b + 1)])
        zs[w, :, :, :, :, 256:384] = v.astype(BF16).reshape(2, 4, 2, 16, 128)
        owners[w] = []
        for a, b, e in z_peers:
            zh2, zl2, c2 = step(zh, a), lax.rem(zl + b, 2), lax.rem(c + e, 2)
            owners[w].append(send(zs.at[w, zl2, zh2, c2], zr.at[w, zl, c, zh], z_peer(a, b, e)))
        zr[w, pl.ds(zl, 1), pl.ds(c, 1), pl.ds(zh, 1)] = zs[
            w, pl.ds(zl, 1), pl.ds(zh, 1), pl.ds(c, 1)
        ].reshape(1, 1, 1, 16, 384)

    for kk in range(6):
        own[kk] = oh[kk].astype(F32).T.astype(BF16)

    norm_wave(0)
    norm_wave(1)
    x_first(0)
    norm_wave(2)
    gain1 = [send(gx.at[x], gx.at[x], dev(x_=step(x, d))) for d in (1, 2, 3)]

    ys2[0, 1] = down_part(q_p).astype(BF16)
    y2pd = send(ys2.at[0, 1], yr2.at[0, 1], yp)
    x_first(1)
    ys2[1, 0] = up_part(q_m).astype(BF16)
    y2mu = send(ys2.at[1, 0], yr2.at[1, 0], ym)
    x_second(0)
    x_first(2)
    ykeep[0] = up_part(q_p)
    x_second(1)
    ykeep[1] = down_part(q_m)

    y1u.wait_recv()
    ys2[0, 0] = (ykeep[0] + yr1[0].astype(F32)).astype(BF16)
    y2pu = send(ys2.at[0, 0], yr2.at[0, 0], yp)
    y1d.wait_recv()
    ys2[1, 1] = (ykeep[1] + yr1[1].astype(F32)).astype(BF16)
    y2md = send(ys2.at[1, 1], yr2.at[1, 1], ym)

    to_owners(0)
    x_second(2)
    ykeep[0] = up_part(y)
    ykeep[1] = down_part(y)
    to_owners(1)

    for d in gain1:
        d.wait_recv()
    slot_me = zh * 2 + c
    gz[pl.ds(zl, 1), pl.ds(slot_me, 1)] = (gx[0] + gx[1] + gx[2] + gx[3])[None, None]
    gain2 = [send(gz.at[zl, slot_me], gz.at[zl, slot_me], z_peer(*p_)) for p_ in z_peers]
    to_owners(2)

    for d in gain2:
        d.wait_recv()
    for h in range(2):
        g = gz[h, 0]
        for i in range(1, 8):
            g = g + gz[h, i]
        gy[pl.ds(y, 1), h] = g[None]
    gain3 = [send(gy.at[y], gy.at[y], dev(y_=step(y, d))) for d in (1, 2, 3)]

    cols = []
    for w in range(3):
        for d in owners[w]:
            d.wait_recv()
    zero4 = iota((8, 128), 0) < 4
    for a in range(2):
        for e in range(2):
            for w in range(3):
                t = zr[w, a, e, 0].astype(F32)
                for b in range(1, 4):
                    t = t + zr[w, a, e, b].astype(F32)
                top = jnp.concatenate([t[0:8, 0:256], t[8:16, 0:256]], axis=1)
                e0, e1 = t[0:8, 256:384], t[8:16, 256:384]
                low = [e0, pltpu.roll(e0, 4, 0), e1, pltpu.roll(e1, 4, 0)]
                low = jnp.concatenate([jnp.where(zero4, v, 0.0) for v in low], axis=1)
                cols.append(jnp.concatenate([top, low], axis=0))
    d_norm = jnp.concatenate(cols, axis=1)
    h = d_norm * gain_ref[...]
    nh = nhat_s[...]
    inner = h - jnp.mean(h, axis=1, keepdims=True) - nh * jnp.mean(h * nh, axis=1, keepdims=True)
    d_rows = rstd_s[:, 0:1] * inner
    high = d_rows.astype(BF16)
    rows_ref[0:16, :] = high
    rows_ref[16:32, :] = (d_rows - high.astype(F32)).astype(BF16)

    for d in gain3:
        d.wait_recv()
    for h in range(2):
        g = gy[0, h] + gy[1, h] + gy[2, h] + gy[3, h]
        for i in range(6):
            at = slice(h * HALF + i * WW, h * HALF + (i + 1) * WW)
            gout_ref[:, at] = g[i:i + 1, :] / gain_ref[:, at]

    y2mu.wait_recv()
    ykeep[0] += yr2[1, 0].astype(F32)
    y2pd.wait_recv()
    ykeep[1] += yr2[0, 1].astype(F32)
    y2pu.wait_recv()
    upg_ref[...] = (ykeep[0] + yr2[0, 0].astype(F32)).T.astype(BF16)
    y2md.wait_recv()
    dng_ref[...] = (ykeep[1] + yr2[1, 1].astype(F32)).astype(BF16)

    for d in started:
        d.wait_send()


N_COPIES = 256


def kernel_call(keep, tokens, cotangent, gain, w_up, w_down):
    vmem = pl.BlockSpec(memory_space=pltpu.VMEM)
    hbm = pl.BlockSpec(memory_space=pl.ANY)

    def v(shape, dt=BF16):
        return pltpu.VMEM(shape, dt)

    scratch = [
        v((TOK, D)), v((TOK, D)),
        v((2, 2, 16, 512)), v((CHUNKS - 1, 2, 2, 16, 384)),
        v((2, 4, 2, 16, 512)), v((CHUNKS - 1, 2, 4, 2, 16, 384)),
        v((CHUNKS, BOTH, CW)), v((2, 4, BOTH, HALF)),
        v((HALF, FB)), v((FB, HALF)),
        v((4, 2, BOTH, FB), F32), v((4, 2, BOTH, FB)), v((4, 2, BOTH, FB)),
        v((FB, 4 * BOTH)), v((FB, 4 * BOTH)), v((4, BOTH, FB)), v((4, BOTH, FB)),
        v((3, 4, BOTH, WW)), v((3, 4, BOTH, WW)), v((3, 4, BOTH, WW), F32),
        v((3, 2, BOTH, 256)), v((3, 2, BOTH, 256)), v((3, 2, BOTH, WW)), v((3, 2, BOTH, WW)),
        v((3, 2, 4, 2, 16, 384)), v((3, 2, 2, 4, 16, 384)),
        v((16, D), F32), v((16, 128), F32),
        v((2, FB, QW)), v((2, FB, QW)), v((2, 2, FB, QW)), v((2, 2, FB, QW)),
        v((2, FB, QW), F32),
        v((4, 8, WW), F32), v((2, 8, 8, WW), F32), v((4, 2, 8, WW), F32),
        pltpu.SemaphoreType.DMA((N_COPIES,)), pltpu.SemaphoreType.DMA((N_COPIES,)),
        pltpu.SemaphoreType.DMA((10,)),
    ]
    return pl.pallas_call(
        body,
        out_shape=(
            jax.ShapeDtypeStruct((32, D), BF16),
            jax.ShapeDtypeStruct((TOK, 32), BF16),
            jax.ShapeDtypeStruct((1, D), F32),
            jax.ShapeDtypeStruct((QW, FB), BF16),
            jax.ShapeDtypeStruct((FB, QW), BF16),
        ),
        in_specs=[vmem, vmem, hbm, hbm, hbm, hbm],
        out_specs=(vmem,) * 5,
        scratch_shapes=scratch,
        compiler_params=pltpu.CompilerParams(
            collective_id=0, has_side_effects=True, vmem_limit_bytes=60 * 2**20
        ),
    )(keep, gain, tokens, cotangent, w_up, w_down)


def local(tokens, gain, w_up, w_down, cotangent, keep_index):
    rows, sel, gain_grad, up, down = kernel_call(
        keep_index, tokens, cotangent, gain.reshape(1, D), w_up, w_down
    )
    input_grad = (cotangent.astype(F32) + dot(sel, rows)).astype(BF16)
    return (input_grad, gain_grad.reshape(D), up, down)


def solution(mesh):
    in_specs = (
        P(("replica", "node"), None),
        P(),
        P("replica", "node"),
        P("node", "replica"),
        P(("replica", "node"), None),
        P("replica", None),
    )
    out_specs = (P(("replica", "node"), None), P(), P("replica", "node"), P("node", "replica"))
    return jax.shard_map(local, mesh=mesh, in_specs=in_specs, out_specs=out_specs, check_vma=False)
```
